32 devices in a mesh: dp: 4 (over z), row: 2 (over y), col: 4 (over x, core).
Axes of the slice: x: 2, y: 2, z: 4, core: 2. Of those that a mesh axis runs over, the one named last changes fastest.
Arguments:
- grad_blocks: bfloat16 [4, 4096, 1024], P('dp', 'row', 'col'), may hold values from -300 to 300
- ln_grads: bfloat16 [4, 4, 1024], P('dp', None, 'col'), may hold values from -240 to 240, as said below
- master: float32 [4096, 1024], P(('row', 'col')), may hold values from -6 to 6
- first_moment: float32 [4096, 1024], P(('row', 'col')), may hold values from -6 to 6
- second_moment: float32 [4096, 1024], P(('row', 'col')), may hold values from 0.3 to 3
- average: float32 [4096, 1024], P('row', 'col'), may hold values from -6 to 6
- ln_master: float32 [4, 1024], P(None, 'col'), may hold values from -6 to 6
- ln_first: float32 [4, 1024], P(None, 'col'), may hold values from -6 to 6
- ln_second: float32 [4, 1024], P(None, 'col'), may hold values from 0.3 to 3
- ln_average: float32 [4, 1024], P(None, 'col'), may hold values from -6 to 6
Outputs:
- average_new: float32 [4096, 1024], P('row', 'col')
- master_new: float32 [4096, 1024], P(('row', 'col'))
- first_new: float32 [4096, 1024], P(('row', 'col'))
- second_new: float32 [4096, 1024], P(('row', 'col'))
- ln_master_new: float32 [4, 1024], P(None, 'col')
- ln_first_new: float32 [4, 1024], P(None, 'col')
- ln_second_new: float32 [4, 1024], P(None, 'col')
- ln_average_new: float32 [4, 1024], P(None, 'col')
The draws below stay inside these ranges and needn't reach their ends.
Inputs may be any that keep to these rules, and one draw needn't show every extreme that they name: `ln_grads`: partial gradients of each data-parallel group.
All inputs are finite; a program needn't handle non-finite values.
Results may differ from the reference program's by a relative error of at most 0.0003.
Values may be sent and summed in bfloat16 or wider, within the bound.
No kernel may reach another device: no remote copies, remote signals or barrier semaphores. Data moves between devices by JAX's collectives and lax.ppermute only.
A program may use at most 64 MiB of HBM per device.

```python
import math
import jax
import jax.numpy as jnp
from jax import lax

D = 1024
FF = 4096
STEP = 20
N_DP = 4


def draw_grad_blocks(key, part):
    keys = jax.random.split(key, 3)
    noise = jax.random.normal(keys[0], (N_DP, FF, D), jnp.float32)
    noise = jnp.clip(noise, -6.0, 6.0)
    row_level = jax.random.uniform(keys[1], (FF, 1), jnp.float32)
    col_level = jax.random.uniform(keys[2], (1, D), jnp.float32)
    row_trend = jnp.arange(FF, dtype=jnp.float32)[:, None] / FF
    col_trend = jnp.arange(D, dtype=jnp.float32)[None, :] / D
    scale = jnp.exp(jnp.log(10.0) * (row_level + col_level) + jnp.log(3.0) * (row_trend + col_trend) - jnp.log(3.0))
    values = jnp.clip(noise * scale[None, :, :], -300.0, 300.0)
    return values.astype(jnp.bfloat16)


def draw_ln_grads(key, part):
    keys = jax.random.split(key, 1)
    noise = jax.random.normal(keys[0], (N_DP, 4, D), jnp.float32)
    noise = jnp.clip(noise, -3.0, 3.0)
    return (80.0 * noise).astype(jnp.bfloat16)


def block_scale(rng, dims, shards, smallest, largest):
    level, own = 1.0, jax.random.fold_in(rng, 6)
    for position, parts in shards:
        draws = jnp.exp(jax.random.uniform(jax.random.fold_in(own, position), (parts,), jnp.float32, smallest / len(shards), largest / len(shards)))
        level = level * jnp.repeat(draws, dims[position] // parts).reshape([-1 if axis == position else 1 for axis in range(len(dims))])
    return level


def bell_draw(stream_key, dims, width, most, pieces=(), kind=jnp.bfloat16):
    level = block_scale(stream_key, dims, pieces, -0.22, 0.18) if pieces else 1.0
    array = jax.random.normal(stream_key, dims, jnp.float32) * width * level
    return jnp.minimum(jnp.maximum(array, -most), most).astype(kind)


def setup_inputs(seed: int = 0) -> dict:
    key_list = jax.random.split(jax.random.key(seed), 11)
    return {
        "grad_blocks": draw_grad_blocks(jax.random.fold_in(key_list[10], 71), 0),
        "ln_grads": draw_ln_grads(jax.random.fold_in(key_list[10], 71), 0),
        "master": bell_draw(key_list[2], (FF, D), 0.5, 6.0, ((0, 8),), jnp.float32),
        "first_moment": bell_draw(key_list[3], (FF, D), 0.5, 6.0, ((0, 8),), jnp.float32),
        "second_moment": jnp.clip(jnp.exp(math.log(3.0) - 2.3025851 * jax.random.uniform(key_list[4], (FF, D), jnp.float32) ** block_scale(key_list[4], (FF, D), ((0, 8),), -0.2, 0.2)), 0.3, 3.0),
        "average": bell_draw(key_list[5], (FF, D), 0.5, 6.0, ((0, 2), (1, 4)), jnp.float32),
        "ln_master": bell_draw(key_list[6], (4, D), 0.5, 6.0, ((1, 4),), jnp.float32),
        "ln_first": bell_draw(key_list[7], (4, D), 0.5, 6.0, ((1, 4),), jnp.float32),
        "ln_second": jnp.clip(jnp.exp(math.log(3.0) - 2.3025851 * jax.random.uniform(key_list[8], (4, D), jnp.float32) ** block_scale(key_list[8], (4, D), ((1, 4),), -0.2, 0.2)), 0.3, 3.0),
        "ln_average": bell_draw(key_list[9], (4, D), 0.5, 6.0, ((1, 4),), jnp.float32),
    }


beta_one = 0.9
beta_two = 0.95
learn_rate = 0.02
decay_rate = 0.1
epsilon = 1e-08
clip_rms = 1.0
ema_keep = 0.9

def adam_step(gradient, clip_scale, first, second, master, decay_weight):
    clipped = clip_scale * gradient
    first_new = beta_one * first + (1.0 - beta_one) * clipped
    second_new = beta_two * second + (1.0 - beta_two) * clipped * clipped
    direction = first_new / (1.0 - beta_one ** STEP) / (jnp.sqrt(second_new / (1.0 - beta_two ** STEP)) + epsilon)
    master_new = master - learn_rate * (direction + decay_weight * master)
    return (master_new, first_new, second_new)

def clip_factor(norm_total):
    return jnp.minimum(1.0, clip_rms * math.sqrt(FF * D + 4 * D) / jnp.sqrt(norm_total))

def reference(grad_blocks, ln_grads, master, first_moment, second_moment, average, ln_master, ln_first, ln_second, ln_average):
    gradient = lax.optimization_barrier(jnp.sum(grad_blocks.astype(jnp.float32), axis=0))
    ln_gradient = lax.optimization_barrier(jnp.sum(ln_grads.astype(jnp.float32), axis=0))
    norm_total = jnp.sum(gradient * gradient) + jnp.sum(ln_gradient * ln_gradient)
    clip_scale = clip_factor(norm_total)
    master_new, first_new, second_new = adam_step(gradient, clip_scale, first_moment, second_moment, master, decay_rate)
    ln_master_new, ln_first_new, ln_second_new = adam_step(ln_gradient, clip_scale, ln_first, ln_second, ln_master, 0.0)
    average_new = ema_keep * average + (1.0 - ema_keep) * master_new
    ln_average_new = ema_keep * ln_average + (1.0 - ema_keep) * ln_master_new
    return (average_new, master_new, first_new, second_new, ln_master_new, ln_first_new, ln_second_new, ln_average_new)
```

```python
import functools
import math

import jax
import jax.numpy as jnp
from jax import lax
from jax.experimental import pallas as pl
from jax.experimental.pallas import tpu as pltpu
from jax.sharding import PartitionSpec as P

D = 1024
FF = 4096
STEP = 20


beta_one = 0.9
beta_two = 0.95
learn_rate = 0.02
decay_rate = 0.1
epsilon = 1e-08
clip_rms = 1.0
ema_keep = 0.9


def adam_step(gradient, clip_scale, first, second, master, decay_weight):
    clipped = clip_scale * gradient
    first_new = beta_one * first + (1.0 - beta_one) * clipped
    second_new = beta_two * second + (1.0 - beta_two) * clipped * clipped
    direction = (
        first_new
        / (1.0 - beta_one**STEP)
        / (jnp.sqrt(second_new / (1.0 - beta_two**STEP)) + epsilon)
    )
    master_new = master - learn_rate * (direction + decay_weight * master)
    return (master_new, first_new, second_new)


def clip_factor(norm_total):
    return jnp.minimum(1.0, clip_rms * math.sqrt(FF * D + 4 * D) / jnp.sqrt(norm_total))


def fold(squared):
    row = jnp.sum(squared, axis=0, keepdims=True)
    return functools.reduce(
        jnp.add, [row[:, at : at + 128] for at in range(0, row.shape[1], 128)]
    )


def sum_kernel(ln_copies, parts_ref, ln_ref, piece_ref, ln_sum_ref, norm_ref):
    total = jnp.sum(parts_ref[0].astype(jnp.float32), axis=0)
    piece_ref[0] = total

    @pl.when(pl.program_id(0) == 0)
    def _():
        ln_total = jnp.sum(ln_ref[...].astype(jnp.float32), axis=0)
        ln_sum_ref[...] = ln_total
        norm_ref[...] = fold(ln_total * ln_total) * (1.0 / ln_copies)

    norm_ref[...] += fold(total * total)


def update_kernel(
    place_ref,
    norms_ref,
    piece_ref,
    master_ref,
    first_ref,
    second_ref,
    ln_sum_ref,
    ln_master_ref,
    ln_first_ref,
    ln_second_ref,
    ln_average_ref,
    master_new_ref,
    first_new_ref,
    second_new_ref,
    ln_master_new_ref,
    ln_first_new_ref,
    ln_second_new_ref,
    ln_average_new_ref,
):
    clip_scale = clip_factor(jnp.sum(norms_ref[...], keepdims=True).reshape(1, 1))
    columns, _, width = piece_ref.shape[1:]
    for at in range(columns):
        here = slice(at * width, (at + 1) * width)
        master_new, first_new, second_new = adam_step(
            piece_ref[0, at],
            clip_scale,
            first_ref[:, here],
            second_ref[:, here],
            master_ref[:, here],
            decay_rate,
        )
        master_new_ref[:, here] = master_new
        first_new_ref[:, here] = first_new
        second_new_ref[:, here] = second_new

    @pl.when(pl.program_id(0) == 0)
    def _():
        ln_master_new, ln_first_new, ln_second_new = adam_step(
            ln_sum_ref[...],
            clip_scale,
            ln_first_ref[...],
            ln_second_ref[...],
            ln_master_ref[...],
            0.0,
        )
        ln_master_new_ref[...] = ln_master_new
        ln_first_new_ref[...] = ln_first_new
        ln_second_new_ref[...] = ln_second_new
        ln_average_new_ref[...] = (
            ema_keep * ln_average_ref[...] + (1.0 - ema_keep) * ln_master_new
        )


def shards(
    grad_blocks,
    ln_grads,
    master,
    first_moment,
    second_moment,
    average,
    ln_master,
    ln_first,
    ln_second,
    ln_average,
):
    groups, row_count, cols = (lax.axis_size(name) for name in ("dp", "row", "col"))
    _, rows, width = grad_blocks.shape
    flat = rows // cols
    piece_rows = flat // groups
    ln_rows = ln_master.shape[0]
    f32 = functools.partial(jax.ShapeDtypeStruct, dtype=jnp.float32)

    def from_groups(held):
        return [held] + [
            lax.ppermute(held, "dp", [(d, (d + s) % groups) for d in range(groups)])
            for s in range(1, groups)
        ]

    ln_parts = jnp.stack(from_groups(ln_grads[0]))
    outgoing = grad_blocks.reshape(cols * groups, piece_rows, width)
    parts = lax.all_to_all(
        outgoing, ("col", "dp"), split_axis=0, concat_axis=0, tiled=True
    ).reshape(cols, groups, piece_rows, width)

    piece, ln_sum, norm_part = pl.pallas_call(
        functools.partial(sum_kernel, float(row_count * groups)),
        grid=(cols,),
        in_specs=[
            pl.BlockSpec((1, groups, piece_rows, width), lambda c: (c, 0, 0, 0)),
            pl.BlockSpec((groups, ln_rows, width), lambda c: (0, 0, 0)),
        ],
        out_specs=[
            pl.BlockSpec((1, piece_rows, width), lambda c: (c, 0, 0)),
            pl.BlockSpec((ln_rows, width), lambda c: (0, 0)),
            pl.BlockSpec((1, 128), lambda c: (0, 0)),
        ],
        out_shape=[f32((cols, piece_rows, width)), f32((ln_rows, width)), f32((1, 128))],
        name="group_sum",
    )(parts, ln_parts)

    pieces = jnp.stack(from_groups(piece.astype(jnp.float16))).astype(jnp.float32)
    norms = lax.psum(norm_part, ("dp", "row", "col"))
    place = (lax.axis_index("dp") - jnp.arange(groups, dtype=jnp.int32)) % groups

    state = pl.BlockSpec((piece_rows, D), lambda s, place: (place[s], 0))
    ln_state = pl.BlockSpec((ln_rows, width), lambda s, place: (0, 0))
    (
        master_new,
        first_new,
        second_new,
        ln_master_new,
        ln_first_new,
        ln_second_new,
        ln_average_new,
    ) = pl.pallas_call(
        update_kernel,
        grid_spec=pltpu.PrefetchScalarGridSpec(
            num_scalar_prefetch=1,
            grid=(groups,),
            in_specs=[
                pl.BlockSpec((1, 128), lambda s, place: (0, 0)),
                pl.BlockSpec(
                    (1, cols, piece_rows, width), lambda s, place: (s, 0, 0, 0)
                ),
            ]
            + [state] * 3
            + [ln_state] * 5,
            out_specs=[state] * 3 + [ln_state] * 4,
        ),
        out_shape=[f32((flat, D))] * 3 + [f32((ln_rows, width))] * 4,
        compiler_params=pltpu.CompilerParams(vmem_limit_bytes=48 * 2**20),
        name="adam_update",
    )(
        place,
        norms,
        pieces,
        master,
        first_moment,
        second_moment,
        ln_sum,
        ln_master,
        ln_first,
        ln_second,
        ln_average,
    )

    sent = master_new.astype(jnp.float16).reshape(flat, cols, width).transpose(1, 0, 2)
    block = lax.all_to_all(sent, "col", split_axis=0, concat_axis=0, tiled=True)
    average_new = ema_keep * average + (1.0 - ema_keep) * block.reshape(
        rows, width
    ).astype(jnp.float32)
    return (
        average_new,
        master_new,
        first_new,
        second_new,
        ln_master_new,
        ln_first_new,
        ln_second_new,
        ln_average_new,
    )


def solution(mesh):
    placed = (
        P("dp", "row", "col"),
        P("dp", None, "col"),
        P(("row", "col"), None),
        P(("row", "col"), None),
        P(("row", "col"), None),
        P("row", "col"),
        P(None, "col"),
        P(None, "col"),
        P(None, "col"),
        P(None, "col"),
    )
    return jax.shard_map(
        shards,
        mesh=mesh,
        in_specs=placed,
        out_specs=(
            P("row", "col"),
            P(("row", "col"), None),
            P(("row", "col"), None),
            P(("row", "col"), None),
            P(None, "col"),
            P(None, "col"),
            P(None, "col"),
            P(None, "col"),
        ),
        check_vma=False,
    )
```

```python
import functools
import math

import jax
import jax.numpy as jnp
from jax import lax
from jax.experimental import pallas as pl
from jax.experimental.pallas import tpu as pltpu
from jax.sharding import PartitionSpec as P

D = 1024
FF = 4096
STEP = 20


beta_one = 0.9
beta_two = 0.95
learn_rate = 0.02
decay_rate = 0.1
epsilon = 1e-08
clip_rms = 1.0
ema_keep = 0.9


def adam_step(gradient, clip_scale, first, second, master, decay_weight):
    clipped = clip_scale * gradient
    first_new = beta_one * first + (1.0 - beta_one) * clipped
    second_new = beta_two * second + (1.0 - beta_two) * clipped * clipped
    direction = (
        first_new
        * (1.0 / (1.0 - beta_one**STEP))
        / (jnp.sqrt(second_new * (1.0 / (1.0 - beta_two**STEP))) + epsilon)
    )
    master_new = master - learn_rate * (direction + decay_weight * master)
    return (master_new, first_new, second_new)


def clip_factor(norm_total):
    return jnp.minimum(1.0, clip_rms * math.sqrt(FF * D + 4 * D) / jnp.sqrt(norm_total))


def update_kernel(place_ref, norm_ref, piece_ref, states, kept, ln_states, outs, sent_ref, ln_outs):
    del place_ref, kept
    clip_scale = clip_factor(jnp.sum(norm_ref[...], axis=1, keepdims=True))
    master_ref, first_ref, second_ref = states
    results = adam_step(
        piece_ref[0],
        clip_scale,
        first_ref[...],
        second_ref[...],
        master_ref[...],
        decay_rate,
    )
    for out_ref, result in zip(outs, results):
        out_ref[...] = result
    sent_ref[0] = results[0]

    if ln_outs:

        @pl.when(pl.program_id(0) == 0)
        def _():
            ln_gradient, ln_master, ln_first, ln_second, ln_average = (
                ref[...] for ref in ln_states
            )
            results = adam_step(
                ln_gradient, clip_scale, ln_first, ln_second, ln_master, 0.0
            )
            average = ema_keep * ln_average + (1.0 - ema_keep) * results[0]
            for out_ref, result in zip(ln_outs, (*results, average)):
                out_ref[...] = result


def average_kernel(place_ref, average_ref, block_ref, kept, average_new_ref):
    del place_ref, kept
    average_new_ref[...] = (
        ema_keep * average_ref[...] + (1.0 - ema_keep) * block_ref[0]
    )


def update_piece(place, norm, piece, states, kept, ln_states):
    cols, rows, width = piece.shape
    block = pl.BlockSpec((rows, width), lambda k, place: (place[0], place[1 + k]))
    stays = pl.BlockSpec(memory_space=pl.ANY)
    whole = pl.BlockSpec(norm.shape, lambda k, place: (0, 0))
    ln = [pl.BlockSpec(ref.shape, lambda k, place: (0, 0)) for ref in ln_states]
    ln_outs = ln_states[1:]

    def body(place_ref, norm_ref, piece_ref, *refs):
        refs = list(refs)
        take = lambda count: [refs.pop(0) for _ in range(count)]
        update_kernel(
            place_ref,
            norm_ref,
            piece_ref,
            take(len(states)),
            take(len(kept)),
            take(len(ln_states)),
            take(len(states)),
            take(1)[0],
            take(len(ln_outs)),
        )

    out = pl.pallas_call(
        body,
        grid_spec=pltpu.PrefetchScalarGridSpec(
            num_scalar_prefetch=1,
            grid=(cols,),
            in_specs=[
                whole,
                pl.BlockSpec((1, rows, width), lambda k, place: (place[1 + k], 0, 0)),
            ]
            + [block] * len(states)
            + [stays] * len(kept)
            + ln,
            out_specs=[block] * len(states)
            + [pl.BlockSpec((1, rows, width), lambda k, place: (k, 0, 0))]
            + ln[1:],
        ),
        out_shape=[jax.ShapeDtypeStruct(x.shape, x.dtype) for x in states]
        + [jax.ShapeDtypeStruct(piece.shape, jnp.float32)]
        + [jax.ShapeDtypeStruct(x.shape, x.dtype) for x in ln_outs],
        input_output_aliases={3 + len(states) + i: i for i in range(len(kept))},
        compiler_params=pltpu.CompilerParams(vmem_limit_bytes=32 * 2**20),
        name="adam_update",
    )(place, norm, piece, *states, *kept, *ln_states)
    count = len(states)
    return out[:count], out[count], out[count + 1 :]


def average_pieces(place, average, blocks, kept):
    steps, rows, width = blocks.shape
    block = pl.BlockSpec((rows, width), lambda k, place: (place[k], 0))

    def body(place_ref, average_ref, block_ref, *refs):
        average_kernel(place_ref, average_ref, block_ref, refs[:-1], refs[-1])

    return pl.pallas_call(
        body,
        grid_spec=pltpu.PrefetchScalarGridSpec(
            num_scalar_prefetch=1,
            grid=(steps,),
            in_specs=[
                block,
                pl.BlockSpec((1, rows, width), lambda k, place: (k, 0, 0)),
            ]
            + [pl.BlockSpec(memory_space=pl.ANY)] * len(kept),
            out_specs=block,
        ),
        out_shape=jax.ShapeDtypeStruct(average.shape, average.dtype),
        input_output_aliases={3: 0} if kept else {},
        name="average",
    )(place, average, blocks, *kept)


def tree_sum(terms):
    while len(terms) > 1:
        terms = [a + b for a, b in zip(terms[::2], terms[1::2])]
    return terms[0]


def exchange(held, axis):
    size = lax.axis_size(axis)
    return [held] + [
        lax.ppermute(held, axis, [(i, i ^ s) for i in range(size)])
        for s in range(1, size)
    ]


def shards(
    grad_blocks,
    ln_grads,
    master,
    first_moment,
    second_moment,
    average,
    ln_master,
    ln_first,
    ln_second,
    ln_average,
):
    groups, row_count, cols = (lax.axis_size(name) for name in ("dp", "row", "col"))
    group, col = (lax.axis_index(name) for name in ("dp", "col"))
    _, rows, width = grad_blocks.shape
    piece_rows = rows // (cols * groups)
    f32 = jnp.float32

    ln_gradient = tree_sum([x.astype(f32) for x in exchange(ln_grads[0], "dp")])
    parts = lax.all_to_all(
        grad_blocks.reshape(cols * groups, piece_rows, width),
        ("col", "dp"),
        split_axis=0,
        concat_axis=0,
        tiled=True,
    ).reshape(cols, groups, piece_rows, width)
    total = jnp.sum(parts.astype(f32), axis=1)

    norm = jnp.sum(total * total, axis=(0, 1)) + jnp.sum(
        ln_gradient * ln_gradient, axis=0
    ) / float(row_count * groups)
    norm = tree_sum(exchange(norm.reshape(1, width), "dp"))
    pieces = exchange(total.astype(jnp.float16), "dp")
    norm = lax.psum(norm, ("row", "col"))

    columns = [col ^ k for k in range(cols)]
    states = (master, first_moment, second_moment)
    ln_states = (ln_gradient, ln_master, ln_first, ln_second, ln_average)
    kept, ln_new, blocks, places = (), (), [], []
    for s, piece in enumerate(pieces):
        place = jnp.stack([group ^ s] + columns).astype(jnp.int32)
        kept, sent, ln_out = update_piece(
            place, norm, piece.astype(f32), states, kept, () if s else ln_states
        )
        ln_new = ln_new or ln_out
        blocks.append(
            jnp.stack(
                [sent[0]]
                + [
                    lax.ppermute(
                        sent[k].astype(jnp.float16),
                        "col",
                        [(i, i ^ k) for i in range(cols)],
                    ).astype(f32)
                    for k in range(1, cols)
                ]
            )
        )
        places.append(jnp.stack([c * groups + (group ^ s) for c in columns]))

    average_new = ()
    for at in (slice(0, groups - 1), slice(groups - 1, groups)):
        average_new = (
            average_pieces(
                jnp.concatenate(places[at]).astype(jnp.int32),
                average,
                jnp.concatenate(blocks[at]),
                average_new,
            ),
        )
    return (*average_new, *kept, *ln_new)


def solution(mesh):
    placed = (
        P("dp", "row", "col"),
        P("dp", None, "col"),
        P(("row", "col"), None),
        P(("row", "col"), None),
        P(("row", "col"), None),
        P("row", "col"),
        P(None, "col"),
        P(None, "col"),
        P(None, "col"),
        P(None, "col"),
    )
    return jax.shard_map(
        shards,
        mesh=mesh,
        in_specs=placed,
        out_specs=(
            P("row", "col"),
            P(("row", "col"), None),
            P(("row", "col"), None),
            P(("row", "col"), None),
            P(None, "col"),
            P(None, "col"),
            P(None, "col"),
            P(None, "col"),
        ),
        check_vma=False,
    )
```

```python
import functools
import math

import jax
import jax.numpy as jnp
from jax import lax
from jax.experimental import pallas as pl
from jax.experimental.pallas import tpu as pltpu
from jax.sharding import PartitionSpec as P

D = 1024
FF = 4096
STEP = 20


beta_one = 0.9
beta_two = 0.95
learn_rate = 0.02
decay_rate = 0.1
epsilon = 1e-08
clip_rms = 1.0
ema_keep = 0.9


def adam_step(gradient, clip_scale, first, second, master, decay_weight):
    clipped = clip_scale * gradient
    first_new = beta_one * first + (1.0 - beta_one) * clipped
    second_new = beta_two * second + (1.0 - beta_two) * clipped * clipped
    direction = (
        first_new
        * (1.0 / (1.0 - beta_one**STEP))
        / (jnp.sqrt(second_new * (1.0 / (1.0 - beta_two**STEP))) + epsilon)
    )
    master_new = master - learn_rate * (direction + decay_weight * master)
    return (master_new, first_new, second_new)


def clip_factor(norm_total):
    return jnp.minimum(1.0, clip_rms * math.sqrt(FF * D + 4 * D) / jnp.sqrt(norm_total))


def arrange(blocks):
    groups, cols = lax.axis_size("dp"), lax.axis_size("col")

    def body(blocks_ref, *refs):
        outs, sems = refs[:groups], refs[groups]
        group, col = lax.axis_index("dp"), lax.axis_index("col")
        copies = [
            pltpu.make_async_copy(
                blocks_ref.at[(col ^ k) * groups + (group ^ s)],
                outs[s].at[k],
                sems.at[s * cols + k],
            )
            for s in range(groups)
            for k in range(cols)
        ]
        for copy in copies:
            copy.start()
        for copy in copies:
            copy.wait()

    return pl.pallas_call(
        body,
        in_specs=[pl.BlockSpec(memory_space=pl.ANY)],
        out_specs=[pl.BlockSpec(memory_space=pl.ANY)] * groups,
        out_shape=[jax.ShapeDtypeStruct((cols, *blocks.shape[1:]), blocks.dtype)]
        * groups,
        scratch_shapes=[pltpu.SemaphoreType.DMA((groups * cols,))],
        name="arrange",
    )(blocks)


def by_column(states, cols):
    rows, columns = states[0].shape
    width = columns // cols
    count = len(states)

    def body(*refs):
        out_ref, sems = refs[count:]
        copies = [
            pltpu.make_async_copy(
                refs[i].at[:, pl.ds(c * width, width)],
                out_ref.at[c, i],
                sems.at[c * count + i],
            )
            for c in range(cols)
            for i in range(count)
        ]
        for copy in copies:
            copy.start()
        for copy in copies:
            copy.wait()

    return pl.pallas_call(
        body,
        in_specs=[pl.BlockSpec(memory_space=pl.ANY)] * count,
        out_specs=pl.BlockSpec(memory_space=pl.ANY),
        out_shape=jax.ShapeDtypeStruct((cols, count, rows, width), states[0].dtype),
        scratch_shapes=[pltpu.SemaphoreType.DMA((cols * count,))],
        name="by_column",
    )(*states)


def flat_update(place, norm, gradient, states, ln_states):
    groups, cols, rows, width = gradient.shape
    state = pl.BlockSpec((rows, cols * width), lambda s, place: (place[0] ^ s, 0))
    whole = pl.BlockSpec(norm.shape, lambda s, place: (0, 0))
    ln = [pl.BlockSpec(x.shape, lambda s, place: (0, 0)) for x in ln_states]

    def body(place_ref, norm_ref, gradient_ref, *refs):
        refs = list(refs)
        state_refs, ln_refs = refs[:3], refs[3:8]
        out_refs, ln_out_refs = refs[8:11], refs[11:]
        clip_scale = clip_factor(jnp.sum(norm_ref[...], axis=1, keepdims=True))
        for column in range(cols):
            here = slice(column * width, (column + 1) * width)
            master, first, second = (ref[:, here] for ref in state_refs)
            results = adam_step(
                gradient_ref[0, place_ref[1] ^ column],
                clip_scale,
                first,
                second,
                master,
                decay_rate,
            )
            for out_ref, result in zip(out_refs, results):
                out_ref[:, here] = result

        @pl.when(pl.program_id(0) == 0)
        def _():
            ln_gradient, ln_master, ln_first, ln_second, ln_average = (
                ref[...] for ref in ln_refs
            )
            results = adam_step(
                ln_gradient, clip_scale, ln_first, ln_second, ln_master, 0.0
            )
            average = ema_keep * ln_average + (1.0 - ema_keep) * results[0]
            for out_ref, result in zip(ln_out_refs, (*results, average)):
                out_ref[...] = result

    return pl.pallas_call(
        body,
        grid_spec=pltpu.PrefetchScalarGridSpec(
            num_scalar_prefetch=1,
            grid=(groups,),
            in_specs=[
                whole,
                pl.BlockSpec((1, cols, rows, width), lambda s, place: (s, 0, 0, 0)),
            ]
            + [state] * 3
            + ln,
            out_specs=[state] * 3 + ln[1:],
        ),
        out_shape=[
            jax.ShapeDtypeStruct(x.shape, x.dtype) for x in (*states, *ln_states[1:])
        ],
        compiler_params=pltpu.CompilerParams(vmem_limit_bytes=16 * 2**20),
        name="flat_update",
    )(place, norm, gradient, *states, *ln_states)


def block_average(place, norm, gradient, states, average):
    groups, cols, rows, width = gradient.shape
    span = groups * rows

    def body(place_ref, norm_ref, gradient_ref, states_ref, average_ref, out_ref):
        clip_scale = clip_factor(jnp.sum(norm_ref[...], axis=1, keepdims=True))
        for group in range(groups):
            here = slice(group * rows, (group + 1) * rows)
            master, first, second = (states_ref[0, i, here] for i in range(3))
            master_new, _, _ = adam_step(
                gradient_ref[place_ref[0] ^ group, 0],
                clip_scale,
                first,
                second,
                master,
                decay_rate,
            )
            out_ref[here] = (
                ema_keep * average_ref[here] + (1.0 - ema_keep) * master_new
            )

    block = pl.BlockSpec((span, width), lambda c, place: (c, 0))
    return pl.pallas_call(
        body,
        grid_spec=pltpu.PrefetchScalarGridSpec(
            num_scalar_prefetch=1,
            grid=(cols,),
            in_specs=[
                pl.BlockSpec(norm.shape, lambda c, place: (0, 0)),
                pl.BlockSpec(
                    (groups, 1, rows, width),
                    lambda c, place: (0, place[1] ^ c, 0, 0),
                ),
                pl.BlockSpec((1, 3, span, width), lambda c, place: (c, 0, 0, 0)),
                block,
            ],
            out_specs=block,
        ),
        out_shape=jax.ShapeDtypeStruct(average.shape, average.dtype),
        compiler_params=pltpu.CompilerParams(vmem_limit_bytes=16 * 2**20),
        name="block_average",
    )(place, norm, gradient, states, average)


def tree_sum(terms):
    while len(terms) > 1:
        terms = [a + b for a, b in zip(terms[::2], terms[1::2])]
    return terms[0]


def send(held, axis, s):
    if s == 0:
        return held
    size = lax.axis_size(axis)
    return lax.ppermute(held, axis, [(i, i ^ s) for i in range(size)])


def exchange(held, axis):
    return [send(held, axis, s) for s in range(lax.axis_size(axis))]


def shards(
    grad_blocks,
    ln_grads,
    master,
    first_moment,
    second_moment,
    average,
    ln_master,
    ln_first,
    ln_second,
    ln_average,
):
    groups, row_count, cols = (lax.axis_size(name) for name in ("dp", "row", "col"))
    place = jnp.stack([lax.axis_index("dp"), lax.axis_index("col")]).astype(jnp.int32)
    _, rows, width = grad_blocks.shape
    flat = rows // cols
    piece_rows = flat // groups
    f32, f16 = jnp.float32, jnp.float16
    states = (master, first_moment, second_moment)

    parts = arrange(grad_blocks.reshape(cols * groups, piece_rows, width))
    parts = [send(part, "dp", s) for s, part in enumerate(parts)]
    ln_gradient = tree_sum([x.astype(f32) for x in exchange(ln_grads[0], "dp")])

    block_states = lax.all_to_all(
        by_column(states, cols).astype(f16),
        "col",
        split_axis=0,
        concat_axis=0,
        tiled=True,
    )

    total = tree_sum([part.astype(f32) for part in parts])
    norm = jnp.sum(total * total, axis=(0, 1)) + jnp.sum(
        ln_gradient * ln_gradient, axis=0
    ) / float(row_count * groups)
    norm = tree_sum(exchange(norm.reshape(1, width), "dp"))
    pieces = exchange(total.astype(f16), "dp")
    norm = lax.psum(norm, ("row", "col"))

    flat_pieces = [[send(piece[k], "col", k) for k in range(cols)] for piece in pieces]
    average_new = block_average(
        place, norm, jnp.stack(pieces).astype(f32), block_states.astype(f32), average
    )
    updated = flat_update(
        place,
        norm,
        jnp.stack([jnp.stack(piece) for piece in flat_pieces]).astype(f32),
        states,
        (ln_gradient, ln_master, ln_first, ln_second, ln_average),
    )
    return (average_new, *updated)


def solution(mesh):
    placed = (
        P("dp", "row", "col"),
        P("dp", None, "col"),
        P(("row", "col"), None),
        P(("row", "col"), None),
        P(("row", "col"), None),
        P("row", "col"),
        P(None, "col"),
        P(None, "col"),
        P(None, "col"),
        P(None, "col"),
    )
    return jax.shard_map(
        shards,
        mesh=mesh,
        in_specs=placed,
        out_specs=(
            P("row", "col"),
            P(("row", "col"), None),
            P(("row", "col"), None),
            P(("row", "col"), None),
            P(None, "col"),
            P(None, "col"),
            P(None, "col"),
            P(None, "col"),
        ),
        check_vma=False,
    )
```

```python
import functools
import math

import jax
import jax.numpy as jnp
from jax import lax
from jax.experimental import pallas as pl
from jax.experimental.pallas import tpu as pltpu
from jax.sharding import PartitionSpec as P

D = 1024
FF = 4096
STEP = 20


beta_one = 0.9
beta_two = 0.95
learn_rate = 0.02
decay_rate = 0.1
epsilon = 1e-08
clip_rms = 1.0
ema_keep = 0.9


def adam_step(gradient, clip_scale, first, second, master, decay_weight):
    clipped = clip_scale * gradient
    first_new = beta_one * first + (1.0 - beta_one) * clipped
    second_new = beta_two * second + (1.0 - beta_two) * clipped * clipped
    direction = (
        first_new
        * (1.0 / (1.0 - beta_one**STEP))
        / (jnp.sqrt(second_new * (1.0 / (1.0 - beta_two**STEP))) + epsilon)
    )
    master_new = master - learn_rate * (direction + decay_weight * master)
    return (master_new, first_new, second_new)


def clip_factor(norm_total):
    return jnp.minimum(1.0, clip_rms * math.sqrt(FF * D + 4 * D) / jnp.sqrt(norm_total))


def arrange(blocks, extra):
    groups, cols = lax.axis_size("dp"), lax.axis_size("col")
    _, rows, width = blocks.shape
    span = cols * rows

    def body(blocks_ref, extra_ref, *refs):
        outs, held, sems = refs[:groups], refs[groups], refs[groups + 1]
        group, col = lax.axis_index("dp"), lax.axis_index("col")
        copies = [
            pltpu.make_async_copy(
                blocks_ref.at[(col ^ k) * groups + (group ^ s)],
                held.at[s * cols + k],
                sems.at[s * cols + k],
            )
            for s in range(groups)
            for k in range(cols)
        ]
        for copy in copies:
            copy.start()
        for s in range(groups):
            outs[s][span:] = extra_ref[...]
        for s in range(groups):
            for k in range(cols):
                copies[s * cols + k].wait()
                outs[s][k * rows : (k + 1) * rows] = held[s * cols + k]

    return pl.pallas_call(
        body,
        in_specs=[
            pl.BlockSpec(memory_space=pl.ANY),
            pl.BlockSpec(memory_space=pltpu.VMEM),
        ],
        out_specs=[pl.BlockSpec(memory_space=pltpu.VMEM)] * groups,
        out_shape=[
            jax.ShapeDtypeStruct((span + extra.shape[0], width), blocks.dtype)
        ]
        * groups,
        scratch_shapes=[
            pltpu.VMEM((groups * cols, rows, width), blocks.dtype),
            pltpu.SemaphoreType.DMA((groups * cols,)),
        ],
        compiler_params=pltpu.CompilerParams(vmem_limit_bytes=16 * 2**20),
        name="arrange",
    )(blocks, extra)


def by_column(states, cols):
    rows, columns = states[0].shape
    width = columns // cols
    count = len(states)

    def body(*refs):
        for i in range(count):
            refs[count][0, i] = refs[i][...]

    return pl.pallas_call(
        body,
        grid=(cols,),
        in_specs=[pl.BlockSpec((rows, width), lambda c: (0, c))] * count,
        out_specs=pl.BlockSpec((1, count, rows, width), lambda c: (c, 0, 0, 0)),
        out_shape=jax.ShapeDtypeStruct((cols, count, rows, width), states[0].dtype),
        compiler_params=pltpu.CompilerParams(vmem_limit_bytes=16 * 2**20),
        name="by_column",
    )(*states)


def flat_update(place, norm, gradient, states, ln_states):
    groups, cols, rows, width = gradient.shape
    state = pl.BlockSpec((rows, cols * width), lambda s, place: (place[0] ^ s, 0))
    whole = pl.BlockSpec(norm.shape, lambda s, place: (0, 0))
    ln = [pl.BlockSpec(x.shape, lambda s, place: (0, 0)) for x in ln_states]

    def body(place_ref, norm_ref, gradient_ref, *refs):
        refs = list(refs)
        state_refs, ln_refs = refs[:3], refs[3:8]
        out_refs, ln_out_refs = refs[8:11], refs[11:]
        clip_scale = clip_factor(jnp.sum(norm_ref[...], axis=1, keepdims=True))
        for column in range(cols):
            here = slice(column * width, (column + 1) * width)
            master, first, second = (ref[:, here] for ref in state_refs)
            results = adam_step(
                gradient_ref[0, place_ref[1] ^ column],
                clip_scale,
                first,
                second,
                master,
                decay_rate,
            )
            for out_ref, result in zip(out_refs, results):
                out_ref[:, here] = result

        @pl.when(pl.program_id(0) == 0)
        def _():
            ln_gradient, ln_master, ln_first, ln_second, ln_average = (
                ref[...] for ref in ln_refs
            )
            results = adam_step(
                ln_gradient, clip_scale, ln_first, ln_second, ln_master, 0.0
            )
            average = ema_keep * ln_average + (1.0 - ema_keep) * results[0]
            for out_ref, result in zip(ln_out_refs, (*results, average)):
                out_ref[...] = result

    return pl.pallas_call(
        body,
        grid_spec=pltpu.PrefetchScalarGridSpec(
            num_scalar_prefetch=1,
            grid=(groups,),
            in_specs=[
                whole,
                pl.BlockSpec((1, cols, rows, width), lambda s, place: (s, 0, 0, 0)),
            ]
            + [state] * 3
            + ln,
            out_specs=[state] * 3 + ln[1:],
        ),
        out_shape=[
            jax.ShapeDtypeStruct(x.shape, x.dtype) for x in (*states, *ln_states[1:])
        ],
        compiler_params=pltpu.CompilerParams(vmem_limit_bytes=16 * 2**20),
        name="flat_update",
    )(place, norm, gradient, *states, *ln_states)


def block_average(place, norm, gradient, states, average):
    groups, cols, rows, width = gradient.shape
    span = groups * rows

    def body(place_ref, norm_ref, gradient_ref, states_ref, average_ref, out_ref):
        clip_scale = clip_factor(jnp.sum(norm_ref[...], axis=1, keepdims=True))
        for group in range(groups):
            here = slice(group * rows, (group + 1) * rows)
            master, first, second = (states_ref[0, i, here] for i in range(3))
            master_new, _, _ = adam_step(
                gradient_ref[place_ref[0] ^ group, 0],
                clip_scale,
                first,
                second,
                master,
                decay_rate,
            )
            out_ref[here] = (
                ema_keep * average_ref[here] + (1.0 - ema_keep) * master_new
            )

    block = pl.BlockSpec((span, width), lambda c, place: (c, 0))
    return pl.pallas_call(
        body,
        grid_spec=pltpu.PrefetchScalarGridSpec(
            num_scalar_prefetch=1,
            grid=(cols,),
            in_specs=[
                pl.BlockSpec(norm.shape, lambda c, place: (0, 0)),
                pl.BlockSpec(
                    (groups, 1, rows, width),
                    lambda c, place: (0, place[1] ^ c, 0, 0),
                ),
                pl.BlockSpec((1, 3, span, width), lambda c, place: (c, 0, 0, 0)),
                block,
            ],
            out_specs=block,
        ),
        out_shape=jax.ShapeDtypeStruct(average.shape, average.dtype),
        compiler_params=pltpu.CompilerParams(vmem_limit_bytes=16 * 2**20),
        name="block_average",
    )(place, norm, gradient, states, average)


def tree_sum(terms):
    while len(terms) > 1:
        terms = [a + b for a, b in zip(terms[::2], terms[1::2])]
    return terms[0]


def send(held, axis, s):
    if s == 0:
        return held
    size = lax.axis_size(axis)
    return lax.ppermute(held, axis, [(i, i ^ s) for i in range(size)])


def exchange(held, axis):
    return [send(held, axis, s) for s in range(lax.axis_size(axis))]


def shards(
    grad_blocks,
    ln_grads,
    master,
    first_moment,
    second_moment,
    average,
    ln_master,
    ln_first,
    ln_second,
    ln_average,
):
    groups, row_count, cols = (lax.axis_size(name) for name in ("dp", "row", "col"))
    place = jnp.stack([lax.axis_index("dp"), lax.axis_index("col")]).astype(jnp.int32)
    _, rows, width = grad_blocks.shape
    flat = rows // cols
    piece_rows = flat // groups
    f32, f16 = jnp.float32, jnp.float16
    states = (master, first_moment, second_moment)

    ln_rows = ln_grads.shape[1]
    parts = arrange(
        grad_blocks.reshape(cols * groups, piece_rows, width),
        jnp.pad(ln_grads[0], ((0, -ln_rows % 16), (0, 0))),
    )
    parts = [send(part, "dp", s) for s, part in enumerate(parts)]

    block_states = lax.all_to_all(
        by_column(states, cols).astype(f16),
        "col",
        split_axis=0,
        concat_axis=0,
        tiled=True,
    )

    total = tree_sum([part.astype(f32) for part in parts])
    ln_gradient = total[cols * piece_rows :][:ln_rows]
    total = total[: cols * piece_rows].reshape(cols, piece_rows, width)
    norm = jnp.sum(total * total, axis=(0, 1)) + jnp.sum(
        ln_gradient * ln_gradient, axis=0
    ) / float(row_count * groups)
    norm = tree_sum(exchange(norm.reshape(1, width), "dp"))
    pieces = exchange(total.astype(f16), "dp")
    norm = lax.psum(norm, ("row", "col"))

    own, norm = lax.optimization_barrier((pieces[0], norm))
    others = jnp.stack(pieces[1:], axis=1)
    flat_own = jnp.stack([send(own[k], "col", k) for k in range(cols)])
    flat_others = jnp.stack([send(others[k], "col", k) for k in range(cols)], axis=1)
    average_new = block_average(
        place, norm, jnp.stack(pieces).astype(f32), block_states.astype(f32), average
    )
    gradient = jnp.concatenate([flat_own[None], flat_others]).astype(f32)
    average_new, gradient = lax.optimization_barrier((average_new, gradient))
    updated = flat_update(
        place,
        norm,
        gradient,
        states,
        (ln_gradient, ln_master, ln_first, ln_second, ln_average),
    )
    return (average_new, *updated)


def solution(mesh):
    placed = (
        P("dp", "row", "col"),
        P("dp", None, "col"),
        P(("row", "col"), None),
        P(("row", "col"), None),
        P(("row", "col"), None),
        P("row", "col"),
        P(None, "col"),
        P(None, "col"),
        P(None, "col"),
        P(None, "col"),
    )
    return jax.shard_map(
        shards,
        mesh=mesh,
        in_specs=placed,
        out_specs=(
            P("row", "col"),
            P(("row", "col"), None),
            P(("row", "col"), None),
            P(("row", "col"), None),
            P(None, "col"),
            P(None, "col"),
            P(None, "col"),
            P(None, "col"),
        ),
        check_vma=False,
    )
```

```python
import functools
import math

import jax
import jax.numpy as jnp
from jax import lax
from jax.experimental import pallas as pl
from jax.experimental.pallas import tpu as pltpu
from jax.sharding import PartitionSpec as P

D = 1024
FF = 4096
STEP = 20


beta_one = 0.9
beta_two = 0.95
learn_rate = 0.02
decay_rate = 0.1
epsilon = 1e-08
clip_rms = 1.0
ema_keep = 0.9


def adam_step(gradient, clip_scale, first, second, master, decay_weight):
    clipped = clip_scale * gradient
    first_new = beta_one * first + (1.0 - beta_one) * clipped
    second_new = beta_two * second + (1.0 - beta_two) * clipped * clipped
    direction = (
        first_new
        * (1.0 / (1.0 - beta_one**STEP))
        / (jnp.sqrt(second_new * (1.0 / (1.0 - beta_two**STEP))) + epsilon)
    )
    master_new = master - learn_rate * (direction + decay_weight * master)
    return (master_new, first_new, second_new)


def clip_factor(norm_total):
    return jnp.minimum(1.0, clip_rms * math.sqrt(FF * D + 4 * D) / jnp.sqrt(norm_total))


def arrange(blocks, extra):
    groups, cols = lax.axis_size("dp"), lax.axis_size("col")
    _, rows, width = blocks.shape
    span = cols * rows

    direct = rows % 16 == 0

    def body(blocks_ref, extra_ref, *refs):
        outs, held, sems = refs[:groups], refs[groups], refs[groups + 1]
        group, col = lax.axis_index("dp"), lax.axis_index("col")
        copies = [
            pltpu.make_async_copy(
                blocks_ref.at[(col ^ k) * groups + (group ^ s)],
                outs[s].at[k * rows : (k + 1) * rows]
                if direct
                else held.at[s * cols + k],
                sems.at[s * cols + k],
            )
            for s in range(groups)
            for k in range(cols)
        ]
        for copy in copies:
            copy.start()
        for s in range(groups):
            outs[s][span:] = extra_ref[...]
        for s in range(groups):
            for k in range(cols):
                copies[s * cols + k].wait()
                if not direct:
                    outs[s][k * rows : (k + 1) * rows] = held[s * cols + k]

    return pl.pallas_call(
        body,
        in_specs=[
            pl.BlockSpec(memory_space=pltpu.HBM),
            pl.BlockSpec(memory_space=pltpu.VMEM),
        ],
        out_specs=[pl.BlockSpec(memory_space=pltpu.VMEM)] * groups,
        out_shape=[
            jax.ShapeDtypeStruct((span + extra.shape[0], width), blocks.dtype)
        ]
        * groups,
        scratch_shapes=[
            pltpu.VMEM((1 if direct else groups * cols, rows, width), blocks.dtype),
            pltpu.SemaphoreType.DMA((groups * cols,)),
        ],
        compiler_params=pltpu.CompilerParams(vmem_limit_bytes=16 * 2**20),
        name="arrange",
    )(blocks, extra)


def by_column(states, cols):
    rows, columns = states[0].shape
    width = columns // cols
    count = len(states)

    def body(*refs):
        for i in range(count):
            refs[count][0, i] = refs[i][...]

    return pl.pallas_call(
        body,
        grid=(cols,),
        in_specs=[pl.BlockSpec((rows, width), lambda c: (0, c))] * count,
        out_specs=pl.BlockSpec((1, count, rows, width), lambda c: (c, 0, 0, 0)),
        out_shape=jax.ShapeDtypeStruct((cols, count, rows, width), states[0].dtype),
        compiler_params=pltpu.CompilerParams(vmem_limit_bytes=16 * 2**20),
        name="by_column",
    )(*states)


def flat_update(place, norm, gradient, states, ln_states):
    groups, cols, rows, width = gradient.shape
    state = pl.BlockSpec((rows, cols * width), lambda s, place: (place[0] ^ s, 0))
    whole = pl.BlockSpec(norm.shape, lambda s, place: (0, 0))
    ln = [pl.BlockSpec(x.shape, lambda s, place: (0, 0)) for x in ln_states]

    def body(place_ref, norm_ref, gradient_ref, *refs):
        refs = list(refs)
        state_refs, ln_refs = refs[:3], refs[3:8]
        out_refs, ln_out_refs = refs[8:11], refs[11:]
        clip_scale = clip_factor(jnp.sum(norm_ref[...], axis=1, keepdims=True))
        for column in range(cols):
            here = slice(column * width, (column + 1) * width)
            master, first, second = (ref[:, here] for ref in state_refs)
            results = adam_step(
                gradient_ref[0, place_ref[1] ^ column],
                clip_scale,
                first,
                second,
                master,
                decay_rate,
            )
            for out_ref, result in zip(out_refs, results):
                out_ref[:, here] = result

        @pl.when(pl.program_id(0) == 0)
        def _():
            ln_gradient, ln_master, ln_first, ln_second, ln_average = (
                ref[...] for ref in ln_refs
            )
            results = adam_step(
                ln_gradient, clip_scale, ln_first, ln_second, ln_master, 0.0
            )
            average = ema_keep * ln_average + (1.0 - ema_keep) * results[0]
            for out_ref, result in zip(ln_out_refs, (*results, average)):
                out_ref[...] = result

    return pl.pallas_call(
        body,
        grid_spec=pltpu.PrefetchScalarGridSpec(
            num_scalar_prefetch=1,
            grid=(groups,),
            in_specs=[
                whole,
                pl.BlockSpec((1, cols, rows, width), lambda s, place: (s, 0, 0, 0)),
            ]
            + [state] * 3
            + ln,
            out_specs=[state] * 3 + ln[1:],
        ),
        out_shape=[
            jax.ShapeDtypeStruct(x.shape, x.dtype) for x in (*states, *ln_states[1:])
        ],
        compiler_params=pltpu.CompilerParams(vmem_limit_bytes=16 * 2**20),
        name="flat_update",
    )(place, norm, gradient, *states, *ln_states)


def block_average(place, norm, gradient, states, average):
    groups, cols, rows, width = gradient.shape
    span = groups * rows

    def body(place_ref, norm_ref, gradient_ref, states_ref, average_ref, out_ref):
        clip_scale = clip_factor(jnp.sum(norm_ref[...], axis=1, keepdims=True))
        for group in range(groups):
            here = slice(group * rows, (group + 1) * rows)
            master, first, second = (states_ref[0, i, here] for i in range(3))
            master_new, _, _ = adam_step(
                gradient_ref[place_ref[0] ^ group, 0],
                clip_scale,
                first,
                second,
                master,
                decay_rate,
            )
            out_ref[here] = (
                ema_keep * average_ref[here] + (1.0 - ema_keep) * master_new
            )

    block = pl.BlockSpec((span, width), lambda c, place: (c, 0))
    return pl.pallas_call(
        body,
        grid_spec=pltpu.PrefetchScalarGridSpec(
            num_scalar_prefetch=1,
            grid=(cols,),
            in_specs=[
                pl.BlockSpec(norm.shape, lambda c, place: (0, 0)),
                pl.BlockSpec(
                    (groups, 1, rows, width),
                    lambda c, place: (0, place[1] ^ c, 0, 0),
                ),
                pl.BlockSpec((1, 3, span, width), lambda c, place: (c, 0, 0, 0)),
                block,
            ],
            out_specs=block,
        ),
        out_shape=jax.ShapeDtypeStruct(average.shape, average.dtype),
        compiler_params=pltpu.CompilerParams(vmem_limit_bytes=16 * 2**20),
        name="block_average",
    )(place, norm, gradient, states, average)


def tree_sum(terms):
    while len(terms) > 1:
        terms = [a + b for a, b in zip(terms[::2], terms[1::2])]
    return terms[0]


def send(held, axis, s):
    if s == 0:
        return held
    size = lax.axis_size(axis)
    return lax.ppermute(held, axis, [(i, i ^ s) for i in range(size)])


def butterfly_sum(held, axis):
    step = 1
    while step < lax.axis_size(axis):
        held = held + send(held, axis, step)
        step *= 2
    return held


def exchange(held, axis):
    return [send(held, axis, s) for s in range(lax.axis_size(axis))]


def shards(
    grad_blocks,
    ln_grads,
    master,
    first_moment,
    second_moment,
    average,
    ln_master,
    ln_first,
    ln_second,
    ln_average,
):
    groups, row_count, cols = (lax.axis_size(name) for name in ("dp", "row", "col"))
    place = jnp.stack([lax.axis_index("dp"), lax.axis_index("col")]).astype(jnp.int32)
    _, rows, width = grad_blocks.shape
    flat = rows // cols
    piece_rows = flat // groups
    f32, f16 = jnp.float32, jnp.float16
    states = (master, first_moment, second_moment)

    ln_rows = ln_grads.shape[1]
    parts = arrange(
        grad_blocks.reshape(cols * groups, piece_rows, width),
        jnp.pad(ln_grads[0], ((0, -ln_rows % 16), (0, 0))),
    )
    parts = [send(part, "dp", s) for s, part in enumerate(parts)]

    parts, outgoing = lax.optimization_barrier(
        (parts, by_column(states, cols).astype(f16))
    )
    block_states = lax.all_to_all(
        outgoing, "col", split_axis=0, concat_axis=0, tiled=True
    )

    total = tree_sum([part.astype(f32) for part in parts])
    ln_gradient = total[cols * piece_rows :][:ln_rows]
    total = total[: cols * piece_rows].reshape(cols, piece_rows, width)
    norm = jnp.sum(total * total, axis=(0, 1)) + jnp.sum(
        ln_gradient * ln_gradient, axis=0
    ) / float(row_count * groups)
    norm = tree_sum(exchange(norm.reshape(1, width), "dp"))
    pieces = exchange(total.astype(f16), "dp")
    own, norm = lax.optimization_barrier((pieces[0], norm))
    norm = butterfly_sum(butterfly_sum(norm, "row"), "col")

    others = jnp.stack(pieces[1:], axis=1)
    others, block_states = lax.optimization_barrier((others, block_states.astype(f32)))
    flat_own = jnp.stack([send(own[k], "col", k) for k in range(cols)])
    flat_others = jnp.stack([send(others[k], "col", k) for k in range(cols)], axis=1)
    average_new = block_average(
        place, norm, jnp.stack(pieces).astype(f32), block_states, average
    )
    gradient = jnp.concatenate([flat_own[None], flat_others]).astype(f32)
    average_new, gradient = lax.optimization_barrier((average_new, gradient))
    updated = flat_update(
        place,
        norm,
        gradient,
        states,
        (ln_gradient, ln_master, ln_first, ln_second, ln_average),
    )
    return (average_new, *updated)


def solution(mesh):
    placed = (
        P("dp", "row", "col"),
        P("dp", None, "col"),
        P(("row", "col"), None),
        P(("row", "col"), None),
        P(("row", "col"), None),
        P("row", "col"),
        P(None, "col"),
        P(None, "col"),
        P(None, "col"),
        P(None, "col"),
    )
    return jax.shard_map(
        shards,
        mesh=mesh,
        in_specs=placed,
        out_specs=(
            P("row", "col"),
            P(("row", "col"), None),
            P(("row", "col"), None),
            P(("row", "col"), None),
            P(None, "col"),
            P(None, "col"),
            P(None, "col"),
            P(None, "col"),
        ),
        check_vma=False,
    )
```

```python
import functools
import math

import jax
import jax.numpy as jnp
from jax import lax
from jax.experimental import pallas as pl
from jax.experimental.pallas import tpu as pltpu
from jax.sharding import PartitionSpec as P

D = 1024
FF = 4096
STEP = 20


beta_one = 0.9
beta_two = 0.95
learn_rate = 0.02
decay_rate = 0.1
epsilon = 1e-08
clip_rms = 1.0
ema_keep = 0.9


def adam_step(gradient, clip_scale, first, second, master, decay_weight):
    clipped = clip_scale * gradient
    first_new = beta_one * first + (1.0 - beta_one) * clipped
    second_new = beta_two * second + (1.0 - beta_two) * clipped * clipped
    direction = (
        first_new
        * (1.0 / (1.0 - beta_one**STEP))
        / (jnp.sqrt(second_new * (1.0 / (1.0 - beta_two**STEP))) + epsilon)
    )
    master_new = master - learn_rate * (direction + decay_weight * master)
    return (master_new, first_new, second_new)


def clip_factor(norm_total):
    return jnp.minimum(1.0, clip_rms * math.sqrt(FF * D + 4 * D) / jnp.sqrt(norm_total))


def arrange(blocks, extra):
    groups, cols = lax.axis_size("dp"), lax.axis_size("col")
    _, rows, width = blocks.shape
    span = cols * rows

    def body(blocks_ref, extra_ref, *outs):
        group, col = lax.axis_index("dp"), lax.axis_index("col")
        for s in range(groups):
            for k in range(cols):
                outs[s][k * rows : (k + 1) * rows] = blocks_ref[
                    (col ^ k) * groups + (group ^ s)
                ]
            outs[s][span:] = extra_ref[...]

    return pl.pallas_call(
        body,
        in_specs=[pl.BlockSpec(memory_space=pltpu.VMEM)] * 2,
        out_specs=[pl.BlockSpec(memory_space=pltpu.VMEM)] * groups,
        out_shape=[
            jax.ShapeDtypeStruct((span + extra.shape[0], width), blocks.dtype)
        ]
        * groups,
        compiler_params=pltpu.CompilerParams(vmem_limit_bytes=16 * 2**20),
        name="arrange",
    )(blocks, extra)


def by_column(states, cols):
    rows, columns = states[0].shape
    width = columns // cols
    count = len(states)

    def body(*refs):
        for i in range(count):
            refs[count][0, i] = refs[i][...]

    return pl.pallas_call(
        body,
        grid=(cols,),
        in_specs=[pl.BlockSpec((rows, width), lambda c: (0, c))] * count,
        out_specs=pl.BlockSpec((1, count, rows, width), lambda c: (c, 0, 0, 0)),
        out_shape=jax.ShapeDtypeStruct((cols, count, rows, width), states[0].dtype),
        compiler_params=pltpu.CompilerParams(vmem_limit_bytes=16 * 2**20),
        name="by_column",
    )(*states)


def flat_update(place, norm, gradient, states, ln_states):
    groups, cols, rows, width = gradient.shape
    state = pl.BlockSpec((rows, cols * width), lambda s, place: (place[0] ^ s, 0))
    whole = pl.BlockSpec(norm.shape, lambda s, place: (0, 0))
    ln = [pl.BlockSpec(x.shape, lambda s, place: (0, 0)) for x in ln_states]

    def body(place_ref, norm_ref, gradient_ref, *refs):
        refs = list(refs)
        state_refs, ln_refs = refs[:3], refs[3:8]
        out_refs, ln_out_refs = refs[8:11], refs[11:]
        clip_scale = clip_factor(jnp.sum(norm_ref[:1], axis=1, keepdims=True))
        for column in range(cols):
            here = slice(column * width, (column + 1) * width)
            master, first, second = (ref[:, here] for ref in state_refs)
            results = adam_step(
                gradient_ref[0, place_ref[1] ^ column],
                clip_scale,
                first,
                second,
                master,
                decay_rate,
            )
            for out_ref, result in zip(out_refs, results):
                out_ref[:, here] = result

        @pl.when(pl.program_id(0) == 0)
        def _():
            ln_gradient, ln_master, ln_first, ln_second, ln_average = (
                ref[...] for ref in ln_refs
            )
            results = adam_step(
                ln_gradient, clip_scale, ln_first, ln_second, ln_master, 0.0
            )
            average = ema_keep * ln_average + (1.0 - ema_keep) * results[0]
            for out_ref, result in zip(ln_out_refs, (*results, average)):
                out_ref[...] = result

    return pl.pallas_call(
        body,
        grid_spec=pltpu.PrefetchScalarGridSpec(
            num_scalar_prefetch=1,
            grid=(groups,),
            in_specs=[
                whole,
                pl.BlockSpec((1, cols, rows, width), lambda s, place: (s, 0, 0, 0)),
            ]
            + [state] * 3
            + ln,
            out_specs=[state] * 3 + ln[1:],
        ),
        out_shape=[
            jax.ShapeDtypeStruct(x.shape, x.dtype) for x in (*states, *ln_states[1:])
        ],
        compiler_params=pltpu.CompilerParams(vmem_limit_bytes=16 * 2**20),
        name="flat_update",
    )(place, norm, gradient, *states, *ln_states)


def block_average(place, norm, gradient, states, average):
    groups, cols, rows, width = gradient.shape
    span = groups * rows

    def body(
        place_ref, norm_ref, gradient_ref, states_ref, average_ref, out_ref, passed_ref
    ):
        passed_ref[...] = norm_ref[...]
        clip_scale = clip_factor(jnp.sum(norm_ref[:1], axis=1, keepdims=True))
        for group in range(groups):
            here = slice(group * rows, (group + 1) * rows)
            master, first, second = (states_ref[0, i, here] for i in range(3))
            master_new, _, _ = adam_step(
                gradient_ref[place_ref[0] ^ group, 0],
                clip_scale,
                first,
                second,
                master,
                decay_rate,
            )
            out_ref[here] = (
                ema_keep * average_ref[here] + (1.0 - ema_keep) * master_new
            )

    block = pl.BlockSpec((span, width), lambda c, place: (c, 0))
    return pl.pallas_call(
        body,
        grid_spec=pltpu.PrefetchScalarGridSpec(
            num_scalar_prefetch=1,
            grid=(cols,),
            in_specs=[
                pl.BlockSpec(norm.shape, lambda c, place: (0, 0)),
                pl.BlockSpec(
                    (groups, 1, rows, width),
                    lambda c, place: (0, place[1] ^ c, 0, 0),
                ),
                pl.BlockSpec((1, 3, span, width), lambda c, place: (c, 0, 0, 0)),
                block,
            ],
            out_specs=[block, pl.BlockSpec(norm.shape, lambda c, place: (0, 0))],
        ),
        out_shape=[
            jax.ShapeDtypeStruct(x.shape, x.dtype) for x in (average, norm)
        ],
        compiler_params=pltpu.CompilerParams(vmem_limit_bytes=16 * 2**20),
        name="block_average",
    )(place, norm, gradient, states, average)


def tree_sum(terms):
    while len(terms) > 1:
        terms = [a + b for a, b in zip(terms[::2], terms[1::2])]
    return terms[0]


def send(held, axis, s):
    if s == 0:
        return held
    size = lax.axis_size(axis)
    return lax.ppermute(held, axis, [(i, i ^ s) for i in range(size)])


def exchange(held, axis):
    return [send(held, axis, s) for s in range(lax.axis_size(axis))]


def shards(
    grad_blocks,
    ln_grads,
    master,
    first_moment,
    second_moment,
    average,
    ln_master,
    ln_first,
    ln_second,
    ln_average,
):
    groups, row_count, cols = (lax.axis_size(name) for name in ("dp", "row", "col"))
    place = jnp.stack([lax.axis_index("dp"), lax.axis_index("col")]).astype(jnp.int32)
    _, rows, width = grad_blocks.shape
    flat = rows // cols
    piece_rows = flat // groups
    f32, f16 = jnp.float32, jnp.float16
    states = (master, first_moment, second_moment)

    ln_rows = ln_grads.shape[1]
    parts = arrange(
        grad_blocks.reshape(cols * groups, piece_rows, width),
        jnp.pad(ln_grads[0], ((0, -ln_rows % 16), (0, 0))),
    )
    parts = [send(part, "dp", s) for s, part in enumerate(parts)]

    block_states = lax.all_to_all(
        by_column(states, cols).astype(f16),
        "col",
        split_axis=0,
        concat_axis=0,
        tiled=True,
    )

    total = tree_sum([part.astype(f32) for part in parts])
    ln_gradient = total[cols * piece_rows :][:ln_rows]
    total = total[: cols * piece_rows].reshape(cols, piece_rows, width)
    norm = jnp.sum(total * total, axis=(0, 1)) + jnp.sum(
        ln_gradient * ln_gradient, axis=0
    ) / float(row_count * groups)
    norm = tree_sum(exchange(norm.reshape(1, width), "dp"))
    pieces = exchange(total.astype(f16), "dp")
    norm = lax.psum(norm, ("row", "col"))

    own, norm, tie = lax.optimization_barrier(
        (pieces[0], norm, block_states[0, 0, :1].astype(f32))
    )
    norm = jnp.concatenate([norm, tie])
    others = jnp.stack(pieces[1:], axis=1)
    flat_own = jnp.stack([send(own[k], "col", k) for k in range(cols)])
    flat_others = jnp.stack([send(others[k], "col", k) for k in range(cols)], axis=1)
    average_new, norm = block_average(
        place, norm, jnp.stack(pieces).astype(f32), block_states.astype(f32), average
    )
    updated = flat_update(
        place,
        norm,
        jnp.concatenate([flat_own[None], flat_others]).astype(f32),
        states,
        (ln_gradient, ln_master, ln_first, ln_second, ln_average),
    )
    return (average_new, *updated)


def solution(mesh):
    placed = (
        P("dp", "row", "col"),
        P("dp", None, "col"),
        P(("row", "col"), None),
        P(("row", "col"), None),
        P(("row", "col"), None),
        P("row", "col"),
        P(None, "col"),
        P(None, "col"),
        P(None, "col"),
        P(None, "col"),
    )
    return jax.shard_map(
        shards,
        mesh=mesh,
        in_specs=placed,
        out_specs=(
            P("row", "col"),
            P(("row", "col"), None),
            P(("row", "col"), None),
            P(("row", "col"), None),
            P(None, "col"),
            P(None, "col"),
            P(None, "col"),
            P(None, "col"),
        ),
        check_vma=False,
    )
```

```python
import functools
import math

import jax
import jax.numpy as jnp
from jax import lax
from jax.experimental import pallas as pl
from jax.experimental.pallas import tpu as pltpu
from jax.sharding import PartitionSpec as P

D = 1024
FF = 4096
STEP = 20


beta_one = 0.9
beta_two = 0.95
learn_rate = 0.02
decay_rate = 0.1
epsilon = 1e-08
clip_rms = 1.0
ema_keep = 0.9


def adam_step(gradient, clip_scale, first, second, master, decay_weight):
    clipped = clip_scale * gradient
    first_new = beta_one * first + (1.0 - beta_one) * clipped
    second_new = beta_two * second + (1.0 - beta_two) * clipped * clipped
    direction = (
        first_new
        * (1.0 / (1.0 - beta_one**STEP))
        / (jnp.sqrt(second_new * (1.0 / (1.0 - beta_two**STEP))) + epsilon)
    )
    master_new = master - learn_rate * (direction + decay_weight * master)
    return (master_new, first_new, second_new)


def clip_factor(norm_total):
    return jnp.minimum(1.0, clip_rms * math.sqrt(FF * D + 4 * D) / jnp.sqrt(norm_total))


def arrange(blocks, extra):
    groups, cols = lax.axis_size("dp"), lax.axis_size("col")
    _, rows, width = blocks.shape
    span = cols * rows

    def body(blocks_ref, extra_ref, *outs):
        outs[groups][...] = jnp.zeros_like(outs[groups])
        group, col = lax.axis_index("dp"), lax.axis_index("col")
        for s in range(groups):
            for k in range(cols):
                outs[s][k * rows : (k + 1) * rows] = blocks_ref[
                    (col ^ k) * groups + (group ^ s)
                ]
            outs[s][span:] = extra_ref[...]

    return pl.pallas_call(
        body,
        in_specs=[pl.BlockSpec(memory_space=pltpu.VMEM)] * 2,
        out_specs=[pl.BlockSpec(memory_space=pltpu.VMEM)] * (groups + 1),
        out_shape=[
            jax.ShapeDtypeStruct((span + extra.shape[0], width), blocks.dtype)
        ]
        * groups
        + [jax.ShapeDtypeStruct((8, 128), jnp.float32)],
        compiler_params=pltpu.CompilerParams(vmem_limit_bytes=16 * 2**20),
        name="arrange",
    )(blocks, extra)


def by_column(states, cols, after):
    rows, columns = states[0].shape
    width = columns // cols
    count = len(states)

    def body(*refs):
        for i in range(count):
            refs[count + 1][0, i] = refs[i][...]

    return pl.pallas_call(
        body,
        grid=(cols,),
        in_specs=[pl.BlockSpec((rows, width), lambda c: (0, c))] * count
        + [pl.BlockSpec(after.shape, lambda c: (0, 0))],
        out_specs=pl.BlockSpec((1, count, rows, width), lambda c: (c, 0, 0, 0)),
        out_shape=jax.ShapeDtypeStruct((cols, count, rows, width), states[0].dtype),
        compiler_params=pltpu.CompilerParams(vmem_limit_bytes=16 * 2**20),
        name="by_column",
    )(*states, after)


def flat_update(place, norm, gradient, states, ln_states):
    groups, cols, rows, width = gradient.shape
    state = pl.BlockSpec((rows, cols * width), lambda s, place: (place[0] ^ s, 0))
    whole = pl.BlockSpec(norm.shape, lambda s, place: (0, 0))
    ln = [pl.BlockSpec(x.shape, lambda s, place: (0, 0)) for x in ln_states]

    def body(place_ref, norm_ref, gradient_ref, *refs):
        refs = list(refs)
        state_refs, ln_refs = refs[:3], refs[3:8]
        out_refs, ln_out_refs = refs[8:11], refs[11:]
        clip_scale = clip_factor(jnp.sum(norm_ref[:1], axis=1, keepdims=True))
        for column in range(cols):
            here = slice(column * width, (column + 1) * width)
            master, first, second = (ref[:, here] for ref in state_refs)
            results = adam_step(
                gradient_ref[0, place_ref[1] ^ column],
                clip_scale,
                first,
                second,
                master,
                decay_rate,
            )
            for out_ref, result in zip(out_refs, results):
                out_ref[:, here] = result

        @pl.when(pl.program_id(0) == 0)
        def _():
            ln_gradient, ln_master, ln_first, ln_second, ln_average = (
                ref[...] for ref in ln_refs
            )
            results = adam_step(
                ln_gradient, clip_scale, ln_first, ln_second, ln_master, 0.0
            )
            average = ema_keep * ln_average + (1.0 - ema_keep) * results[0]
            for out_ref, result in zip(ln_out_refs, (*results, average)):
                out_ref[...] = result

    return pl.pallas_call(
        body,
        grid_spec=pltpu.PrefetchScalarGridSpec(
            num_scalar_prefetch=1,
            grid=(groups,),
            in_specs=[
                whole,
                pl.BlockSpec((1, cols, rows, width), lambda s, place: (s, 0, 0, 0)),
            ]
            + [state] * 3
            + ln,
            out_specs=[state] * 3 + ln[1:],
        ),
        out_shape=[
            jax.ShapeDtypeStruct(x.shape, x.dtype) for x in (*states, *ln_states[1:])
        ],
        compiler_params=pltpu.CompilerParams(vmem_limit_bytes=16 * 2**20),
        name="flat_update",
    )(place, norm, gradient, *states, *ln_states)


def block_average(place, norm, gradient, states, average):
    groups, cols, rows, width = gradient.shape
    span = groups * rows

    def body(
        place_ref, norm_ref, gradient_ref, states_ref, average_ref, out_ref, passed_ref
    ):
        passed_ref[...] = norm_ref[...]
        clip_scale = clip_factor(jnp.sum(norm_ref[:1], axis=1, keepdims=True))
        for group in range(groups):
            here = slice(group * rows, (group + 1) * rows)
            master, first, second = (states_ref[0, i, here] for i in range(3))
            master_new, _, _ = adam_step(
                gradient_ref[place_ref[0] ^ group, 0],
                clip_scale,
                first,
                second,
                master,
                decay_rate,
            )
            out_ref[here] = (
                ema_keep * average_ref[here] + (1.0 - ema_keep) * master_new
            )

    block = pl.BlockSpec((span, width), lambda c, place: (c, 0))
    return pl.pallas_call(
        body,
        grid_spec=pltpu.PrefetchScalarGridSpec(
            num_scalar_prefetch=1,
            grid=(cols,),
            in_specs=[
                pl.BlockSpec(norm.shape, lambda c, place: (0, 0)),
                pl.BlockSpec(
                    (groups, 1, rows, width),
                    lambda c, place: (0, place[1] ^ c, 0, 0),
                ),
                pl.BlockSpec((1, 3, span, width), lambda c, place: (c, 0, 0, 0)),
                block,
            ],
            out_specs=[block, pl.BlockSpec(norm.shape, lambda c, place: (0, 0))],
        ),
        out_shape=[
            jax.ShapeDtypeStruct(x.shape, x.dtype) for x in (average, norm)
        ],
        compiler_params=pltpu.CompilerParams(vmem_limit_bytes=16 * 2**20),
        name="block_average",
    )(place, norm, gradient, states, average)


def tree_sum(terms):
    while len(terms) > 1:
        terms = [a + b for a, b in zip(terms[::2], terms[1::2])]
    return terms[0]


def send(held, axis, s):
    if s == 0:
        return held
    size = lax.axis_size(axis)
    return lax.ppermute(held, axis, [(i, i ^ s) for i in range(size)])


def exchange(held, axis):
    return [send(held, axis, s) for s in range(lax.axis_size(axis))]


def shards(
    grad_blocks,
    ln_grads,
    master,
    first_moment,
    second_moment,
    average,
    ln_master,
    ln_first,
    ln_second,
    ln_average,
):
    groups, row_count, cols = (lax.axis_size(name) for name in ("dp", "row", "col"))
    place = jnp.stack([lax.axis_index("dp"), lax.axis_index("col")]).astype(jnp.int32)
    _, rows, width = grad_blocks.shape
    flat = rows // cols
    piece_rows = flat // groups
    f32, f16 = jnp.float32, jnp.float16
    states = (master, first_moment, second_moment)

    ln_rows = ln_grads.shape[1]
    *parts, after = arrange(
        grad_blocks.reshape(cols * groups, piece_rows, width),
        jnp.pad(ln_grads[0], ((0, -ln_rows % 16), (0, 0))),
    )
    parts = [send(part, "dp", s) for s, part in enumerate(parts)]

    block_states = lax.all_to_all(
        by_column(states, cols, after).astype(f16),
        "col",
        split_axis=0,
        concat_axis=0,
        tiled=True,
    )

    total = tree_sum([part.astype(f32) for part in parts])
    ln_gradient = total[cols * piece_rows :][:ln_rows]
    total = total[: cols * piece_rows].reshape(cols, piece_rows, width)
    norm = jnp.sum(total * total, axis=(0, 1)) + jnp.sum(
        ln_gradient * ln_gradient, axis=0
    ) / float(row_count * groups)
    norm = tree_sum(exchange(norm.reshape(1, width), "dp"))
    pieces = exchange(total.astype(f16), "dp")
    own, norm = lax.optimization_barrier((pieces[0], norm))

    flat_own = [None, None] + [send(own[k], "col", k) for k in range(2, cols)]
    norm = lax.psum(norm, ("row", "col"))
    stacked = jnp.stack(pieces, axis=1)
    flat = [
        send(stacked[k], "col", k)
        if k < 2
        else jnp.concatenate([flat_own[k][None], send(stacked[k, 1:], "col", k)])
        for k in range(cols)
    ]
    norm, tie = lax.optimization_barrier((norm, block_states[0, 0, :1].astype(f32)))
    norm = jnp.concatenate([norm, tie])
    average_new, norm = block_average(
        place, norm, jnp.stack(pieces).astype(f32), block_states.astype(f32), average
    )
    updated = flat_update(
        place,
        norm,
        jnp.stack(flat, axis=1).astype(f32),
        states,
        (ln_gradient, ln_master, ln_first, ln_second, ln_average),
    )
    return (average_new, *updated)


def solution(mesh):
    placed = (
        P("dp", "row", "col"),
        P("dp", None, "col"),
        P(("row", "col"), None),
        P(("row", "col"), None),
        P(("row", "col"), None),
        P("row", "col"),
        P(None, "col"),
        P(None, "col"),
        P(None, "col"),
        P(None, "col"),
    )
    return jax.shard_map(
        shards,
        mesh=mesh,
        in_specs=placed,
        out_specs=(
            P("row", "col"),
            P(("row", "col"), None),
            P(("row", "col"), None),
            P(("row", "col"), None),
            P(None, "col"),
            P(None, "col"),
            P(None, "col"),
            P(None, "col"),
        ),
        check_vma=False,
    )
```

```python
import functools
import math

import jax
import jax.numpy as jnp
from jax import lax
from jax.experimental import pallas as pl
from jax.experimental.pallas import tpu as pltpu
from jax.sharding import PartitionSpec as P

D = 1024
FF = 4096
STEP = 20


beta_one = 0.9
beta_two = 0.95
learn_rate = 0.02
decay_rate = 0.1
epsilon = 1e-08
clip_rms = 1.0
ema_keep = 0.9


def adam_step(gradient, clip_scale, first, second, master, decay_weight):
    clipped = clip_scale * gradient
    first_new = beta_one * first + (1.0 - beta_one) * clipped
    second_new = beta_two * second + (1.0 - beta_two) * clipped * clipped
    direction = (
        first_new
        * (1.0 / (1.0 - beta_one**STEP))
        / (jnp.sqrt(second_new * (1.0 / (1.0 - beta_two**STEP))) + epsilon)
    )
    master_new = master - learn_rate * (direction + decay_weight * master)
    return (master_new, first_new, second_new)


def clip_factor(norm_total):
    return jnp.minimum(1.0, clip_rms * math.sqrt(FF * D + 4 * D) / jnp.sqrt(norm_total))


def arrange(blocks, extra):
    groups, cols = lax.axis_size("dp"), lax.axis_size("col")
    _, rows, width = blocks.shape
    span = cols * rows

    def body(blocks_ref, extra_ref, *outs):
        outs[groups][...] = jnp.zeros_like(outs[groups])
        group, col = lax.axis_index("dp"), lax.axis_index("col")
        for s in range(groups):
            for k in range(cols):
                outs[s][k * rows : (k + 1) * rows] = blocks_ref[
                    (col ^ k) * groups + (group ^ s)
                ]
            outs[s][span:] = extra_ref[...]

    return pl.pallas_call(
        body,
        in_specs=[pl.BlockSpec(memory_space=pltpu.VMEM)] * 2,
        out_specs=[pl.BlockSpec(memory_space=pltpu.VMEM)] * (groups + 1),
        out_shape=[
            jax.ShapeDtypeStruct((span + extra.shape[0], width), blocks.dtype)
        ]
        * groups
        + [jax.ShapeDtypeStruct((8, 128), jnp.float32)],
        compiler_params=pltpu.CompilerParams(vmem_limit_bytes=16 * 2**20),
        name="arrange",
    )(blocks, extra)


def by_column(states, cols, after):
    rows, columns = states[0].shape
    width = columns // cols
    count = len(states)

    def body(*refs):
        for i in range(count):
            refs[count + 1][0, i] = refs[i][...]

    return pl.pallas_call(
        body,
        grid=(cols,),
        in_specs=[pl.BlockSpec((rows, width), lambda c: (0, c))] * count
        + [pl.BlockSpec(after.shape, lambda c: (0, 0))],
        out_specs=pl.BlockSpec((1, count, rows, width), lambda c: (c, 0, 0, 0)),
        out_shape=jax.ShapeDtypeStruct((cols, count, rows, width), states[0].dtype),
        compiler_params=pltpu.CompilerParams(vmem_limit_bytes=16 * 2**20),
        name="by_column",
    )(*states, after)


def flat_update(place, norm, gradient, states, ln_states):
    groups, cols, rows, width = gradient.shape
    state = pl.BlockSpec((rows, cols * width), lambda s, place: (place[0] ^ s, 0))
    whole = pl.BlockSpec(norm.shape, lambda s, place: (0, 0))
    ln = [pl.BlockSpec(x.shape, lambda s, place: (0, 0)) for x in ln_states]

    def body(place_ref, norm_ref, gradient_ref, *refs):
        refs = list(refs)
        state_refs, ln_refs = refs[:3], refs[3:8]
        out_refs, ln_out_refs = refs[8:11], refs[11:]
        clip_scale = clip_factor(jnp.sum(norm_ref[:1], axis=1, keepdims=True))
        for column in range(cols):
            here = slice(column * width, (column + 1) * width)
            master, first, second = (ref[:, here] for ref in state_refs)
            results = adam_step(
                gradient_ref[0, place_ref[1] ^ column],
                clip_scale,
                first,
                second,
                master,
                decay_rate,
            )
            for out_ref, result in zip(out_refs, results):
                out_ref[:, here] = result

        @pl.when(pl.program_id(0) == 0)
        def _():
            ln_gradient, ln_master, ln_first, ln_second, ln_average = (
                ref[...] for ref in ln_refs
            )
            results = adam_step(
                ln_gradient, clip_scale, ln_first, ln_second, ln_master, 0.0
            )
            average = ema_keep * ln_average + (1.0 - ema_keep) * results[0]
            for out_ref, result in zip(ln_out_refs, (*results, average)):
                out_ref[...] = result

    return pl.pallas_call(
        body,
        grid_spec=pltpu.PrefetchScalarGridSpec(
            num_scalar_prefetch=1,
            grid=(groups,),
            in_specs=[
                whole,
                pl.BlockSpec((1, cols, rows, width), lambda s, place: (s, 0, 0, 0)),
            ]
            + [state] * 3
            + ln,
            out_specs=[state] * 3 + ln[1:],
        ),
        out_shape=[
            jax.ShapeDtypeStruct(x.shape, x.dtype) for x in (*states, *ln_states[1:])
        ],
        compiler_params=pltpu.CompilerParams(vmem_limit_bytes=16 * 2**20),
        name="flat_update",
    )(place, norm, gradient, *states, *ln_states)


def block_average(place, norm, gradient, states, average):
    groups, cols, rows, width = gradient.shape
    span = groups * rows

    def body(
        place_ref, norm_ref, gradient_ref, states_ref, average_ref, out_ref, passed_ref
    ):
        passed_ref[...] = norm_ref[...]
        clip_scale = clip_factor(jnp.sum(norm_ref[:1], axis=1, keepdims=True))
        for group in range(groups):
            here = slice(group * rows, (group + 1) * rows)
            master, first, second = (states_ref[0, i, here] for i in range(3))
            master_new, _, _ = adam_step(
                gradient_ref[place_ref[0] ^ group, 0],
                clip_scale,
                first,
                second,
                master,
                decay_rate,
            )
            out_ref[here] = (
                ema_keep * average_ref[here] + (1.0 - ema_keep) * master_new
            )

    block = pl.BlockSpec((span, width), lambda c, place: (c, 0))
    return pl.pallas_call(
        body,
        grid_spec=pltpu.PrefetchScalarGridSpec(
            num_scalar_prefetch=1,
            grid=(cols,),
            in_specs=[
                pl.BlockSpec(norm.shape, lambda c, place: (0, 0)),
                pl.BlockSpec(
                    (groups, 1, rows, width),
                    lambda c, place: (0, place[1] ^ c, 0, 0),
                ),
                pl.BlockSpec((1, 3, span, width), lambda c, place: (c, 0, 0, 0)),
                block,
            ],
            out_specs=[block, pl.BlockSpec(norm.shape, lambda c, place: (0, 0))],
        ),
        out_shape=[
            jax.ShapeDtypeStruct(x.shape, x.dtype) for x in (average, norm)
        ],
        compiler_params=pltpu.CompilerParams(vmem_limit_bytes=16 * 2**20),
        name="block_average",
    )(place, norm, gradient, states, average)


def tree_sum(terms):
    while len(terms) > 1:
        terms = [a + b for a, b in zip(terms[::2], terms[1::2])]
    return terms[0]


def send(held, axis, s):
    if s == 0:
        return held
    size = lax.axis_size(axis)
    return lax.ppermute(held, axis, [(i, i ^ s) for i in range(size)])


def butterfly_sum(held, axis, step=1):
    while step < lax.axis_size(axis):
        held = held + send(held, axis, step)
        step *= 2
    return held


def exchange(held, axis):
    return [send(held, axis, s) for s in range(lax.axis_size(axis))]


def shards(
    grad_blocks,
    ln_grads,
    master,
    first_moment,
    second_moment,
    average,
    ln_master,
    ln_first,
    ln_second,
    ln_average,
):
    groups, row_count, cols = (lax.axis_size(name) for name in ("dp", "row", "col"))
    place = jnp.stack([lax.axis_index("dp"), lax.axis_index("col")]).astype(jnp.int32)
    _, rows, width = grad_blocks.shape
    flat = rows // cols
    piece_rows = flat // groups
    f32, f16 = jnp.float32, jnp.float16
    states = (master, first_moment, second_moment)

    ln_rows = ln_grads.shape[1]
    *parts, after = arrange(
        grad_blocks.reshape(cols * groups, piece_rows, width),
        jnp.pad(ln_grads[0], ((0, -ln_rows % 16), (0, 0))),
    )
    parts = [send(part, "dp", s) for s, part in enumerate(parts)]

    block_states = lax.all_to_all(
        by_column(states, cols, after).astype(f16),
        "col",
        split_axis=0,
        concat_axis=0,
        tiled=True,
    )

    total = tree_sum([part.astype(f32) for part in parts])
    ln_gradient = total[cols * piece_rows :][:ln_rows]
    total = total[: cols * piece_rows].reshape(cols, piece_rows, width)
    pieces = exchange(total.astype(f16), "dp")

    norm = jnp.sum(ln_gradient * ln_gradient, axis=0) / float(row_count * groups // 2)
    norm = norm + tree_sum(
        [jnp.sum(jnp.square(x.astype(f32)), axis=(0, 1)) for x in pieces[:2]]
    )
    norm = jnp.stack([norm, block_states[0, 0, 0].astype(f32)])
    norm = butterfly_sum(norm, "row")
    norm = butterfly_sum(norm, "col")
    norm = butterfly_sum(norm, "dp", 2)

    half = groups // 2
    halves = [jnp.stack(x, axis=1) for x in (pieces[:half], pieces[half:])]
    flat = [
        send(jnp.stack(pieces, axis=1)[k], "col", k)
        if k < 2
        else jnp.concatenate([send(x[k], "col", k) for x in halves])
        for k in range(cols)
    ]
    average_new, norm = block_average(
        place, norm, jnp.stack(pieces).astype(f32), block_states.astype(f32), average
    )
    updated = flat_update(
        place,
        norm,
        jnp.stack(flat, axis=1).astype(f32),
        states,
        (ln_gradient, ln_master, ln_first, ln_second, ln_average),
    )
    return (average_new, *updated)


def solution(mesh):
    placed = (
        P("dp", "row", "col"),
        P("dp", None, "col"),
        P(("row", "col"), None),
        P(("row", "col"), None),
        P(("row", "col"), None),
        P("row", "col"),
        P(None, "col"),
        P(None, "col"),
        P(None, "col"),
        P(None, "col"),
    )
    return jax.shard_map(
        shards,
        mesh=mesh,
        in_specs=placed,
        out_specs=(
            P("row", "col"),
            P(("row", "col"), None),
            P(("row", "col"), None),
            P(("row", "col"), None),
            P(None, "col"),
            P(None, "col"),
            P(None, "col"),
            P(None, "col"),
        ),
        check_vma=False,
    )
```

```python
import functools
import math

import jax
import jax.numpy as jnp
from jax import lax
from jax.experimental import pallas as pl
from jax.experimental.pallas import tpu as pltpu
from jax.sharding import PartitionSpec as P

D = 1024
FF = 4096
STEP = 20


beta_one = 0.9
beta_two = 0.95
learn_rate = 0.02
decay_rate = 0.1
epsilon = 1e-08
clip_rms = 1.0
ema_keep = 0.9


def adam_step(gradient, clip_scale, first, second, master, decay_weight):
    clipped = clip_scale * gradient
    first_new = beta_one * first + (1.0 - beta_one) * clipped
    second_new = beta_two * second + (1.0 - beta_two) * clipped * clipped
    direction = (
        first_new
        * (1.0 / (1.0 - beta_one**STEP))
        / (jnp.sqrt(second_new * (1.0 / (1.0 - beta_two**STEP))) + epsilon)
    )
    master_new = master - learn_rate * (direction + decay_weight * master)
    return (master_new, first_new, second_new)


def clip_factor(norm_total):
    return jnp.minimum(1.0, clip_rms * math.sqrt(FF * D + 4 * D) / jnp.sqrt(norm_total))


def arrange(blocks, extra):
    groups, cols = lax.axis_size("dp"), lax.axis_size("col")
    _, rows, width = blocks.shape
    span = cols * rows

    def body(blocks_ref, extra_ref, out_ref, after_ref):
        after_ref[...] = jnp.zeros_like(after_ref)
        col = lax.axis_index("col")
        for d in range(groups):
            for k in range(cols):
                out_ref[d, k * rows : (k + 1) * rows] = blocks_ref[
                    (col ^ k) * groups + d
                ]
            out_ref[d, span:] = extra_ref[...]

    return pl.pallas_call(
        body,
        in_specs=[pl.BlockSpec(memory_space=pltpu.VMEM)] * 2,
        out_specs=[pl.BlockSpec(memory_space=pltpu.VMEM)] * 2,
        out_shape=[
            jax.ShapeDtypeStruct((groups, span + extra.shape[0], width), blocks.dtype),
            jax.ShapeDtypeStruct((8, 128), jnp.float32),
        ],
        compiler_params=pltpu.CompilerParams(vmem_limit_bytes=16 * 2**20),
        name="arrange",
    )(blocks, extra)


def by_column(place, states, cols, after):
    rows, columns = states[0].shape
    width = columns // cols
    count = len(states)

    def body(place_ref, *refs):
        for i in range(count):
            refs[count + 1][0, i] = refs[i][...]

    return pl.pallas_call(
        body,
        grid_spec=pltpu.PrefetchScalarGridSpec(
            num_scalar_prefetch=1,
            grid=(cols,),
            in_specs=[pl.BlockSpec((rows, width), lambda k, place: (0, place[0] ^ k))]
            * count
            + [pl.BlockSpec(after.shape, lambda k, place: (0, 0))],
            out_specs=pl.BlockSpec(
                (1, count, rows, width), lambda k, place: (k, 0, 0, 0)
            ),
        ),
        out_shape=jax.ShapeDtypeStruct((cols, count, rows, width), states[0].dtype),
        compiler_params=pltpu.CompilerParams(vmem_limit_bytes=16 * 2**20),
        name="by_column",
    )(place, *states, after)


def flat_update(place, norm, start, gradient, states, kept=(), ln_states=()):
    count, cols, rows, width = gradient.shape
    state = pl.BlockSpec((rows, cols * width), lambda d, place: (start + d, 0))
    ln = [pl.BlockSpec(x.shape, lambda d, place: (0, 0)) for x in ln_states]

    def body(place_ref, norm_ref, gradient_ref, *refs):
        refs = list(refs)
        take = lambda number: [refs.pop(0) for _ in range(number)]
        state_refs, _, ln_refs = take(3), take(len(kept)), take(len(ln))
        out_refs, ln_out_refs = take(3), refs
        clip_scale = clip_factor(jnp.sum(norm_ref[...], axis=1, keepdims=True))
        for column in range(cols):
            here = slice(column * width, (column + 1) * width)
            master, first, second = (ref[:, here] for ref in state_refs)
            results = adam_step(
                gradient_ref[0, place_ref[0] ^ column],
                clip_scale,
                first,
                second,
                master,
                decay_rate,
            )
            for out_ref, result in zip(out_refs, results):
                out_ref[:, here] = result

        if ln:

            @pl.when(pl.program_id(0) == 0)
            def _():
                ln_gradient, ln_master, ln_first, ln_second, ln_average = (
                    ref[...] for ref in ln_refs
                )
                results = adam_step(
                    ln_gradient, clip_scale, ln_first, ln_second, ln_master, 0.0
                )
                average = ema_keep * ln_average + (1.0 - ema_keep) * results[0]
                for out_ref, result in zip(ln_out_refs, (*results, average)):
                    out_ref[...] = result

    out = pl.pallas_call(
        body,
        grid_spec=pltpu.PrefetchScalarGridSpec(
            num_scalar_prefetch=1,
            grid=(count,),
            in_specs=[
                pl.BlockSpec(norm.shape, lambda d, place: (0, 0)),
                pl.BlockSpec((1, cols, rows, width), lambda d, place: (d, 0, 0, 0)),
            ]
            + [state] * 3
            + [pl.BlockSpec(memory_space=pl.ANY)] * len(kept)
            + ln,
            out_specs=[state] * 3 + ln[1:],
        ),
        out_shape=[
            jax.ShapeDtypeStruct(x.shape, x.dtype) for x in (*states, *ln_states[1:])
        ],
        input_output_aliases={6 + i: i for i in range(len(kept))},
        compiler_params=pltpu.CompilerParams(vmem_limit_bytes=16 * 2**20),
        name="flat_update",
    )(place, norm, gradient, *states, *kept, *ln_states)
    return out[:3], out[3:]


def block_average(place, norm, gradient, states, average):
    groups, cols, rows, width = gradient.shape
    span = groups * rows

    def body(
        place_ref, norm_ref, gradient_ref, states_ref, average_ref, out_ref, passed_ref
    ):
        passed_ref[...] = norm_ref[...]
        clip_scale = clip_factor(jnp.sum(norm_ref[...], axis=1, keepdims=True))
        for d in range(groups):
            here = slice(d * rows, (d + 1) * rows)
            master, first, second = (states_ref[0, i, here] for i in range(3))
            master_new, _, _ = adam_step(
                gradient_ref[d, 0], clip_scale, first, second, master, decay_rate
            )
            out_ref[here] = (
                ema_keep * average_ref[here] + (1.0 - ema_keep) * master_new
            )

    block = pl.BlockSpec((span, width), lambda k, place: (place[0] ^ k, 0))
    whole = pl.BlockSpec(norm.shape, lambda k, place: (0, 0))
    return pl.pallas_call(
        body,
        grid_spec=pltpu.PrefetchScalarGridSpec(
            num_scalar_prefetch=1,
            grid=(cols,),
            in_specs=[
                whole,
                pl.BlockSpec((groups, 1, rows, width), lambda k, place: (0, k, 0, 0)),
                pl.BlockSpec((1, 3, span, width), lambda k, place: (k, 0, 0, 0)),
                block,
            ],
            out_specs=[block, whole],
        ),
        out_shape=[jax.ShapeDtypeStruct(x.shape, x.dtype) for x in (average, norm)],
        compiler_params=pltpu.CompilerParams(vmem_limit_bytes=16 * 2**20),
        name="block_average",
    )(place, norm, gradient, states, average)


def send(held, axis, s):
    if s == 0:
        return held
    size = lax.axis_size(axis)
    return lax.ppermute(held, axis, [(i, i ^ s) for i in range(size)])


def butterfly_sum(held, axis):
    step = 1
    while step < lax.axis_size(axis):
        held = held + send(held, axis, step)
        step *= 2
    return held


def over_groups(held):
    return lax.all_to_all(held, "dp", split_axis=0, concat_axis=0, tiled=True)


def shards(
    grad_blocks,
    ln_grads,
    master,
    first_moment,
    second_moment,
    average,
    ln_master,
    ln_first,
    ln_second,
    ln_average,
):
    groups, row_count, cols = (lax.axis_size(name) for name in ("dp", "row", "col"))
    place = lax.axis_index("col").astype(jnp.int32).reshape(1)
    _, rows, width = grad_blocks.shape
    flat = rows // cols
    piece_rows = flat // groups
    f32, f16 = jnp.float32, jnp.float16
    states = (master, first_moment, second_moment)

    ln_rows = ln_grads.shape[1]
    parts, after = arrange(
        grad_blocks.reshape(cols * groups, piece_rows, width),
        jnp.pad(ln_grads[0], ((0, -ln_rows % 16), (0, 0))),
    )
    parts = over_groups(parts)

    block_states = by_column(place, states, cols, after).astype(f16)
    block_states = jnp.stack([send(block_states[k], "col", k) for k in range(cols)])

    total = jnp.sum(parts.astype(f32), axis=0)
    ln_gradient = total[cols * piece_rows :][:ln_rows]
    total = total[: cols * piece_rows].reshape(cols, piece_rows, width)
    pieces = over_groups(
        jnp.broadcast_to(total.astype(f16), (groups, *total.shape))
    )

    norm = jnp.sum(total * total, axis=(0, 1)) + jnp.sum(
        ln_gradient * ln_gradient, axis=0
    ) / float(row_count * groups)
    norm = butterfly_sum(norm.reshape(1, width), "row")
    norm = butterfly_sum(norm, "col")
    norm = butterfly_sum(norm, "dp")

    half = groups // 2
    near = [send(pieces[:, k], "col", k) for k in range(2)]
    halves = [
        jnp.stack(
            [x[at] for x in near]
            + [send(pieces[at, k], "col", k) for k in range(2, cols)],
            axis=1,
        )
        for at in (slice(0, half), slice(half, groups))
    ]
    average_new, norm = block_average(
        place, norm, pieces.astype(f32), block_states.astype(f32), average
    )
    updated, ln_updated = flat_update(
        place,
        norm,
        0,
        halves[0].astype(f32),
        states,
        ln_states=(ln_gradient, ln_master, ln_first, ln_second, ln_average),
    )
    updated, _ = flat_update(place, norm, half, halves[1].astype(f32), states, updated)
    return (average_new, *updated, *ln_updated)


def solution(mesh):
    placed = (
        P("dp", "row", "col"),
        P("dp", None, "col"),
        P(("row", "col"), None),
        P(("row", "col"), None),
        P(("row", "col"), None),
        P("row", "col"),
        P(None, "col"),
        P(None, "col"),
        P(None, "col"),
        P(None, "col"),
    )
    return jax.shard_map(
        shards,
        mesh=mesh,
        in_specs=placed,
        out_specs=(
            P("row", "col"),
            P(("row", "col"), None),
            P(("row", "col"), None),
            P(("row", "col"), None),
            P(None, "col"),
            P(None, "col"),
            P(None, "col"),
            P(None, "col"),
        ),
        check_vma=False,
    )
```

```python
import functools
import math

import jax
import jax.numpy as jnp
from jax import lax
from jax.experimental import pallas as pl
from jax.experimental.pallas import tpu as pltpu
from jax.sharding import PartitionSpec as P

D = 1024
FF = 4096
STEP = 20


beta_one = 0.9
beta_two = 0.95
learn_rate = 0.02
decay_rate = 0.1
epsilon = 1e-08
clip_rms = 1.0
ema_keep = 0.9


def adam_step(gradient, clip_scale, first, second, master, decay_weight):
    clipped = clip_scale * gradient
    first_new = beta_one * first + (1.0 - beta_one) * clipped
    second_new = beta_two * second + (1.0 - beta_two) * clipped * clipped
    direction = (
        first_new
        * (1.0 / (1.0 - beta_one**STEP))
        / (jnp.sqrt(second_new * (1.0 / (1.0 - beta_two**STEP))) + epsilon)
    )
    master_new = master - learn_rate * (direction + decay_weight * master)
    return (master_new, first_new, second_new)


def clip_factor(norm_total):
    return jnp.minimum(1.0, clip_rms * math.sqrt(FF * D + 4 * D) / jnp.sqrt(norm_total))


def arrange(blocks, extra):
    groups, cols = lax.axis_size("dp"), lax.axis_size("col")
    _, rows, width = blocks.shape
    span = cols * rows

    def body(blocks_ref, extra_ref, *outs):
        outs[groups][...] = jnp.zeros_like(outs[groups])
        group, col = lax.axis_index("dp"), lax.axis_index("col")
        for s in range(groups):
            for k in range(cols):
                outs[s][k * rows : (k + 1) * rows] = blocks_ref[
                    (col ^ k) * groups + (group ^ s)
                ]
            outs[s][span:] = extra_ref[...]

    return pl.pallas_call(
        body,
        in_specs=[pl.BlockSpec(memory_space=pltpu.VMEM)] * 2,
        out_specs=[pl.BlockSpec(memory_space=pltpu.VMEM)] * (groups + 1),
        out_shape=[
            jax.ShapeDtypeStruct((span + extra.shape[0], width), blocks.dtype)
        ]
        * groups
        + [jax.ShapeDtypeStruct((8, 128), jnp.float32)],
        compiler_params=pltpu.CompilerParams(vmem_limit_bytes=16 * 2**20),
        name="arrange",
    )(blocks, extra)


def by_column(place, states, cols, after):
    rows, columns = states[0].shape
    width = columns // cols
    count = len(states)

    def body(place_ref, *refs):
        for i in range(count):
            refs[count + 1][0, i] = refs[i][...]

    return pl.pallas_call(
        body,
        grid_spec=pltpu.PrefetchScalarGridSpec(
            num_scalar_prefetch=1,
            grid=(cols,),
            in_specs=[pl.BlockSpec((rows, width), lambda k, place: (0, place[0] ^ k))]
            * count
            + [pl.BlockSpec(after.shape, lambda k, place: (0, 0))],
            out_specs=pl.BlockSpec(
                (1, count, rows, width), lambda k, place: (k, 0, 0, 0)
            ),
        ),
        out_shape=jax.ShapeDtypeStruct((cols, count, rows, width), states[0].dtype),
        compiler_params=pltpu.CompilerParams(vmem_limit_bytes=16 * 2**20),
        name="by_column",
    )(place, *states, after)


def flat_update(place, norm, start, gradient, states, kept=(), ln_states=()):
    count, cols, rows, width = gradient.shape
    state = pl.BlockSpec((rows, cols * width), lambda d, place: (start + d, 0))
    ln = [pl.BlockSpec(x.shape, lambda d, place: (0, 0)) for x in ln_states]

    def body(place_ref, norm_ref, gradient_ref, *refs):
        refs = list(refs)
        take = lambda number: [refs.pop(0) for _ in range(number)]
        state_refs, _, ln_refs = take(3), take(len(kept)), take(len(ln))
        out_refs, ln_out_refs = take(3), refs
        clip_scale = clip_factor(jnp.sum(norm_ref[...], axis=1, keepdims=True))
        for column in range(cols):
            here = slice(column * width, (column + 1) * width)
            master, first, second = (ref[:, here] for ref in state_refs)
            results = adam_step(
                gradient_ref[0, place_ref[0] ^ column],
                clip_scale,
                first,
                second,
                master,
                decay_rate,
            )
            for out_ref, result in zip(out_refs, results):
                out_ref[:, here] = result

        if ln:

            @pl.when(pl.program_id(0) == 0)
            def _():
                ln_gradient, ln_master, ln_first, ln_second, ln_average = (
                    ref[...] for ref in ln_refs
                )
                results = adam_step(
                    ln_gradient, clip_scale, ln_first, ln_second, ln_master, 0.0
                )
                average = ema_keep * ln_average + (1.0 - ema_keep) * results[0]
                for out_ref, result in zip(ln_out_refs, (*results, average)):
                    out_ref[...] = result

    out = pl.pallas_call(
        body,
        grid_spec=pltpu.PrefetchScalarGridSpec(
            num_scalar_prefetch=1,
            grid=(count,),
            in_specs=[
                pl.BlockSpec(norm.shape, lambda d, place: (0, 0)),
                pl.BlockSpec((1, cols, rows, width), lambda d, place: (d, 0, 0, 0)),
            ]
            + [state] * 3
            + [pl.BlockSpec(memory_space=pl.ANY)] * len(kept)
            + ln,
            out_specs=[state] * 3 + ln[1:],
        ),
        out_shape=[
            jax.ShapeDtypeStruct(x.shape, x.dtype) for x in (*states, *ln_states[1:])
        ],
        input_output_aliases={6 + i: i for i in range(len(kept))},
        compiler_params=pltpu.CompilerParams(vmem_limit_bytes=16 * 2**20),
        name="flat_update",
    )(place, norm, gradient, *states, *kept, *ln_states)
    return out[:3], out[3:]


def block_average(place, norm, gradient, states, average):
    groups, cols, rows, width = gradient.shape
    span = groups * rows

    def body(
        place_ref, norm_ref, gradient_ref, states_ref, average_ref, out_ref, passed_ref
    ):
        passed_ref[...] = norm_ref[...]
        clip_scale = clip_factor(jnp.sum(norm_ref[...], axis=1, keepdims=True))
        for d in range(groups):
            here = slice(d * rows, (d + 1) * rows)
            master, first, second = (states_ref[0, i, here] for i in range(3))
            master_new, _, _ = adam_step(
                gradient_ref[d, 0], clip_scale, first, second, master, decay_rate
            )
            out_ref[here] = (
                ema_keep * average_ref[here] + (1.0 - ema_keep) * master_new
            )

    block = pl.BlockSpec((span, width), lambda k, place: (place[0] ^ k, 0))
    whole = pl.BlockSpec(norm.shape, lambda k, place: (0, 0))
    return pl.pallas_call(
        body,
        grid_spec=pltpu.PrefetchScalarGridSpec(
            num_scalar_prefetch=1,
            grid=(cols,),
            in_specs=[
                whole,
                pl.BlockSpec((groups, 1, rows, width), lambda k, place: (0, k, 0, 0)),
                pl.BlockSpec((1, 3, span, width), lambda k, place: (k, 0, 0, 0)),
                block,
            ],
            out_specs=[block, whole],
        ),
        out_shape=[jax.ShapeDtypeStruct(x.shape, x.dtype) for x in (average, norm)],
        compiler_params=pltpu.CompilerParams(vmem_limit_bytes=16 * 2**20),
        name="block_average",
    )(place, norm, gradient, states, average)


def send(held, axis, s):
    if s == 0:
        return held
    size = lax.axis_size(axis)
    return lax.ppermute(held, axis, [(i, i ^ s) for i in range(size)])


def butterfly_sum(held, axis):
    step = 1
    while step < lax.axis_size(axis):
        held = held + send(held, axis, step)
        step *= 2
    return held


def tree_sum(terms):
    while len(terms) > 1:
        terms = [a + b for a, b in zip(terms[::2], terms[1::2])]
    return terms[0]


def over_groups(held):
    return lax.all_to_all(held, "dp", split_axis=0, concat_axis=0, tiled=True)


def shards(
    grad_blocks,
    ln_grads,
    master,
    first_moment,
    second_moment,
    average,
    ln_master,
    ln_first,
    ln_second,
    ln_average,
):
    groups, row_count, cols = (lax.axis_size(name) for name in ("dp", "row", "col"))
    place = lax.axis_index("col").astype(jnp.int32).reshape(1)
    _, rows, width = grad_blocks.shape
    flat = rows // cols
    piece_rows = flat // groups
    f32, f16 = jnp.float32, jnp.float16
    states = (master, first_moment, second_moment)

    ln_rows = ln_grads.shape[1]
    *parts, after = arrange(
        grad_blocks.reshape(cols * groups, piece_rows, width),
        jnp.pad(ln_grads[0], ((0, -ln_rows % 16), (0, 0))),
    )
    parts = [send(part, "dp", s) for s, part in enumerate(parts)]

    block_states = by_column(place, states, cols, after).astype(f16)
    block_states = jnp.stack([send(block_states[k], "col", k) for k in range(cols)])

    total = tree_sum([part.astype(f32) for part in parts])
    ln_gradient = total[cols * piece_rows :][:ln_rows]
    total = total[: cols * piece_rows].reshape(cols, piece_rows, width)
    pieces = over_groups(
        jnp.broadcast_to(total.astype(f16), (groups, *total.shape))
    )

    norm = jnp.sum(total * total, axis=(0, 1)) + jnp.sum(
        ln_gradient * ln_gradient, axis=0
    ) / float(row_count * groups)
    norm = butterfly_sum(norm.reshape(1, width), "row")
    norm = butterfly_sum(norm, "col")
    norm = tree_sum([send(norm, "dp", s) for s in range(groups)])

    half = groups // 2
    near = [send(pieces[:, k], "col", k) for k in range(2)]
    halves = [
        jnp.stack(
            [x[at] for x in near]
            + [send(pieces[at, k], "col", k) for k in range(2, cols)],
            axis=1,
        )
        for at in (slice(0, half), slice(half, groups))
    ]
    average_new, norm = block_average(
        place, norm, pieces.astype(f32), block_states.astype(f32), average
    )
    updated, ln_updated = flat_update(
        place,
        norm,
        0,
        halves[0].astype(f32),
        states,
        ln_states=(ln_gradient, ln_master, ln_first, ln_second, ln_average),
    )
    updated, _ = flat_update(place, norm, half, halves[1].astype(f32), states, updated)
    return (average_new, *updated, *ln_updated)


def solution(mesh):
    placed = (
        P("dp", "row", "col"),
        P("dp", None, "col"),
        P(("row", "col"), None),
        P(("row", "col"), None),
        P(("row", "col"), None),
        P("row", "col"),
        P(None, "col"),
        P(None, "col"),
        P(None, "col"),
        P(None, "col"),
    )
    return jax.shard_map(
        shards,
        mesh=mesh,
        in_specs=placed,
        out_specs=(
            P("row", "col"),
            P(("row", "col"), None),
            P(("row", "col"), None),
            P(("row", "col"), None),
            P(None, "col"),
            P(None, "col"),
            P(None, "col"),
            P(None, "col"),
        ),
        check_vma=False,
    )
```

```python
import functools
import math

import jax
import jax.numpy as jnp
from jax import lax
from jax.experimental import pallas as pl
from jax.experimental.pallas import tpu as pltpu
from jax.sharding import PartitionSpec as P

D = 1024
FF = 4096
STEP = 20


beta_one = 0.9
beta_two = 0.95
learn_rate = 0.02
decay_rate = 0.1
epsilon = 1e-08
clip_rms = 1.0
ema_keep = 0.9


def adam_step(gradient, clip_scale, first, second, master, decay_weight):
    clipped = clip_scale * gradient
    first_new = beta_one * first + (1.0 - beta_one) * clipped
    second_new = beta_two * second + (1.0 - beta_two) * clipped * clipped
    direction = (
        first_new
        * (1.0 / (1.0 - beta_one**STEP))
        / (jnp.sqrt(second_new * (1.0 / (1.0 - beta_two**STEP))) + epsilon)
    )
    master_new = master - learn_rate * (direction + decay_weight * master)
    return (master_new, first_new, second_new)


def clip_factor(norm_total):
    return jnp.minimum(1.0, clip_rms * math.sqrt(FF * D + 4 * D) / jnp.sqrt(norm_total))


def arrange(blocks, extra):
    groups, cols = lax.axis_size("dp"), lax.axis_size("col")
    _, rows, width = blocks.shape
    span = cols * rows

    def body(blocks_ref, extra_ref, *outs):
        outs[groups][...] = jnp.zeros_like(outs[groups])
        group, col = lax.axis_index("dp"), lax.axis_index("col")
        for s in range(groups):
            for k in range(cols):
                outs[s][k * rows : (k + 1) * rows] = blocks_ref[
                    (col ^ k) * groups + (group ^ s)
                ]
            outs[s][span:] = extra_ref[...]

    return pl.pallas_call(
        body,
        in_specs=[pl.BlockSpec(memory_space=pltpu.VMEM)] * 2,
        out_specs=[pl.BlockSpec(memory_space=pltpu.VMEM)] * (groups + 1),
        out_shape=[
            jax.ShapeDtypeStruct((span + extra.shape[0], width), blocks.dtype)
        ]
        * groups
        + [jax.ShapeDtypeStruct((8, 128), jnp.float32)],
        compiler_params=pltpu.CompilerParams(vmem_limit_bytes=16 * 2**20),
        name="arrange",
    )(blocks, extra)


def by_column(place, states, cols, after):
    rows, columns = states[0].shape
    width = columns // cols
    count = len(states)

    def body(place_ref, *refs):
        for i in range(count):
            refs[count + 1][0, i] = refs[i][...]

    return pl.pallas_call(
        body,
        grid_spec=pltpu.PrefetchScalarGridSpec(
            num_scalar_prefetch=1,
            grid=(cols,),
            in_specs=[pl.BlockSpec((rows, width), lambda k, place: (0, place[0] ^ k))]
            * count
            + [pl.BlockSpec(after.shape, lambda k, place: (0, 0))],
            out_specs=pl.BlockSpec(
                (1, count, rows, width), lambda k, place: (k, 0, 0, 0)
            ),
        ),
        out_shape=jax.ShapeDtypeStruct((cols, count, rows, width), states[0].dtype),
        compiler_params=pltpu.CompilerParams(vmem_limit_bytes=16 * 2**20),
        name="by_column",
    )(place, *states, after)


def flat_update(place, norm, start, gradient, states, kept=(), ln_states=()):
    count, cols, rows, width = gradient.shape
    state = pl.BlockSpec((rows, cols * width), lambda d, place: (start + d, 0))
    ln = [pl.BlockSpec(x.shape, lambda d, place: (0, 0)) for x in ln_states]

    def body(place_ref, norm_ref, gradient_ref, *refs):
        refs = list(refs)
        take = lambda number: [refs.pop(0) for _ in range(number)]
        state_refs, _, ln_refs = take(3), take(len(kept)), take(len(ln))
        out_refs, ln_out_refs = take(3), refs
        clip_scale = clip_factor(jnp.sum(norm_ref[:1], axis=1, keepdims=True))
        for column in range(cols):
            here = slice(column * width, (column + 1) * width)
            master, first, second = (ref[:, here] for ref in state_refs)
            results = adam_step(
                gradient_ref[0, place_ref[0] ^ column],
                clip_scale,
                first,
                second,
                master,
                decay_rate,
            )
            for out_ref, result in zip(out_refs, results):
                out_ref[:, here] = result

        if ln:

            @pl.when(pl.program_id(0) == 0)
            def _():
                ln_gradient, ln_master, ln_first, ln_second, ln_average = (
                    ref[...] for ref in ln_refs
                )
                results = adam_step(
                    ln_gradient, clip_scale, ln_first, ln_second, ln_master, 0.0
                )
                average = ema_keep * ln_average + (1.0 - ema_keep) * results[0]
                for out_ref, result in zip(ln_out_refs, (*results, average)):
                    out_ref[...] = result

    out = pl.pallas_call(
        body,
        grid_spec=pltpu.PrefetchScalarGridSpec(
            num_scalar_prefetch=1,
            grid=(count,),
            in_specs=[
                pl.BlockSpec(norm.shape, lambda d, place: (0, 0)),
                pl.BlockSpec((1, cols, rows, width), lambda d, place: (d, 0, 0, 0)),
            ]
            + [state] * 3
            + [pl.BlockSpec(memory_space=pl.ANY)] * len(kept)
            + ln,
            out_specs=[state] * 3 + ln[1:],
        ),
        out_shape=[
            jax.ShapeDtypeStruct(x.shape, x.dtype) for x in (*states, *ln_states[1:])
        ],
        input_output_aliases={6 + i: i for i in range(len(kept))},
        compiler_params=pltpu.CompilerParams(vmem_limit_bytes=16 * 2**20),
        name="flat_update",
    )(place, norm, gradient, *states, *kept, *ln_states)
    return out[:3], out[3:]


def block_average(place, norm, gradient, states, average):
    groups, cols, rows, width = gradient.shape
    span = groups * rows

    def body(
        place_ref, norm_ref, gradient_ref, states_ref, average_ref, out_ref, passed_ref
    ):
        passed_ref[...] = norm_ref[...]
        clip_scale = clip_factor(jnp.sum(norm_ref[:1], axis=1, keepdims=True))
        for d in range(groups):
            here = slice(d * rows, (d + 1) * rows)
            master, first, second = (states_ref[0, i, here] for i in range(3))
            master_new, _, _ = adam_step(
                gradient_ref[d, 0], clip_scale, first, second, master, decay_rate
            )
            out_ref[here] = (
                ema_keep * average_ref[here] + (1.0 - ema_keep) * master_new
            )

    block = pl.BlockSpec((span, width), lambda k, place: (place[0] ^ k, 0))
    whole = pl.BlockSpec(norm.shape, lambda k, place: (0, 0))
    return pl.pallas_call(
        body,
        grid_spec=pltpu.PrefetchScalarGridSpec(
            num_scalar_prefetch=1,
            grid=(cols,),
            in_specs=[
                whole,
                pl.BlockSpec((groups, 1, rows, width), lambda k, place: (0, k, 0, 0)),
                pl.BlockSpec((1, 3, span, width), lambda k, place: (k, 0, 0, 0)),
                block,
            ],
            out_specs=[block, whole],
        ),
        out_shape=[jax.ShapeDtypeStruct(x.shape, x.dtype) for x in (average, norm)],
        compiler_params=pltpu.CompilerParams(vmem_limit_bytes=16 * 2**20),
        name="block_average",
    )(place, norm, gradient, states, average)


def send(held, axis, s):
    if s == 0:
        return held
    size = lax.axis_size(axis)
    return lax.ppermute(held, axis, [(i, i ^ s) for i in range(size)])


def butterfly_sum(held, axis):
    step = 1
    while step < lax.axis_size(axis):
        held = held + send(held, axis, step)
        step *= 2
    return held


def tree_sum(terms):
    while len(terms) > 1:
        terms = [a + b for a, b in zip(terms[::2], terms[1::2])]
    return terms[0]


def over_groups(held):
    return lax.all_to_all(held, "dp", split_axis=0, concat_axis=0, tiled=True)


def shards(
    grad_blocks,
    ln_grads,
    master,
    first_moment,
    second_moment,
    average,
    ln_master,
    ln_first,
    ln_second,
    ln_average,
):
    groups, row_count, cols = (lax.axis_size(name) for name in ("dp", "row", "col"))
    place = lax.axis_index("col").astype(jnp.int32).reshape(1)
    _, rows, width = grad_blocks.shape
    flat = rows // cols
    piece_rows = flat // groups
    f32, f16 = jnp.float32, jnp.float16
    states = (master, first_moment, second_moment)

    ln_rows = ln_grads.shape[1]
    *parts, after = arrange(
        grad_blocks.reshape(cols * groups, piece_rows, width),
        jnp.pad(ln_grads[0], ((0, -ln_rows % 16), (0, 0))),
    )
    parts = [send(part, "dp", s) for s, part in enumerate(parts)]

    block_states = by_column(place, states, cols, after).astype(f16)
    parts[0], tie = lax.optimization_barrier((parts[0], block_states[0, 0, :1]))
    block_states = [send(block_states[k], "col", k) for k in range(cols)]

    total = tree_sum([part.astype(f32) for part in parts])
    ln_gradient = total[cols * piece_rows :][:ln_rows]
    total = total[: cols * piece_rows].reshape(cols, piece_rows, width)
    pieces = over_groups(
        jnp.broadcast_to(total.astype(f16), (groups, *total.shape))
    )

    norm = jnp.sum(total * total, axis=(0, 1)) + jnp.sum(
        ln_gradient * ln_gradient, axis=0
    ) / float(row_count * groups)
    norm = butterfly_sum(norm.reshape(1, width), "row")
    norm = butterfly_sum(norm, "col")
    norm = jnp.concatenate([norm] + [x[0, :1].astype(f32) for x in block_states] + [tie.astype(f32)])
    norm = tree_sum([send(norm, "dp", s) for s in range(groups)])

    half = groups // 2
    near = [send(pieces[:, k], "col", k) for k in range(2)]
    halves = [
        jnp.stack(
            [x[at] for x in near]
            + [send(pieces[at, k], "col", k) for k in range(2, cols)],
            axis=1,
        )
        for at in (slice(0, half), slice(half, groups))
    ]
    average_new, norm = block_average(
        place, norm, pieces.astype(f32), jnp.stack(block_states).astype(f32), average
    )
    updated, ln_updated = flat_update(
        place,
        norm,
        0,
        halves[0].astype(f32),
        states,
        ln_states=(ln_gradient, ln_master, ln_first, ln_second, ln_average),
    )
    updated, _ = flat_update(place, norm, half, halves[1].astype(f32), states, updated)
    return (average_new, *updated, *ln_updated)


def solution(mesh):
    placed = (
        P("dp", "row", "col"),
        P("dp", None, "col"),
        P(("row", "col"), None),
        P(("row", "col"), None),
        P(("row", "col"), None),
        P("row", "col"),
        P(None, "col"),
        P(None, "col"),
        P(None, "col"),
        P(None, "col"),
    )
    return jax.shard_map(
        shards,
        mesh=mesh,
        in_specs=placed,
        out_specs=(
            P("row", "col"),
            P(("row", "col"), None),
            P(("row", "col"), None),
            P(("row", "col"), None),
            P(None, "col"),
            P(None, "col"),
            P(None, "col"),
            P(None, "col"),
        ),
        check_vma=False,
    )
```

```python
import functools
import math

import jax
import jax.numpy as jnp
from jax import lax
from jax.experimental import pallas as pl
from jax.experimental.pallas import tpu as pltpu
from jax.sharding import PartitionSpec as P

D = 1024
FF = 4096
STEP = 20


beta_one = 0.9
beta_two = 0.95
learn_rate = 0.02
decay_rate = 0.1
epsilon = 1e-08
clip_rms = 1.0
ema_keep = 0.9


def adam_step(gradient, clip_scale, first, second, master, decay_weight):
    clipped = clip_scale * gradient
    first_new = beta_one * first + (1.0 - beta_one) * clipped
    second_new = beta_two * second + (1.0 - beta_two) * clipped * clipped
    direction = (
        first_new
        * (1.0 / (1.0 - beta_one**STEP))
        / (jnp.sqrt(second_new * (1.0 / (1.0 - beta_two**STEP))) + epsilon)
    )
    master_new = master - learn_rate * (direction + decay_weight * master)
    return (master_new, first_new, second_new)


def clip_factor(norm_total):
    return jnp.minimum(1.0, clip_rms * math.sqrt(FF * D + 4 * D) / jnp.sqrt(norm_total))


def cost(moved, steps):
    return pl.CostEstimate(
        flops=20 * steps, bytes_accessed=4 * moved, transcendentals=2 * steps
    )


def arrange(blocks, extra):
    groups, cols = lax.axis_size("dp"), lax.axis_size("col")
    _, rows, width = blocks.shape
    span = cols * rows

    def body(blocks_ref, extra_ref, *outs):
        outs[groups][...] = jnp.zeros_like(outs[groups])
        group, col = lax.axis_index("dp"), lax.axis_index("col")
        for s in range(groups):
            for k in range(cols):
                outs[s][k * rows : (k + 1) * rows] = blocks_ref[
                    (col ^ k) * groups + (group ^ s)
                ]
            outs[s][span:] = extra_ref[...]

    return pl.pallas_call(
        body,
        in_specs=[pl.BlockSpec(memory_space=pltpu.VMEM)] * 2,
        out_specs=[pl.BlockSpec(memory_space=pltpu.VMEM)] * (groups + 1),
        out_shape=[
            jax.ShapeDtypeStruct((span + extra.shape[0], width), blocks.dtype)
        ]
        * groups
        + [jax.ShapeDtypeStruct((8, 128), jnp.float32)],
        compiler_params=pltpu.CompilerParams(vmem_limit_bytes=16 * 2**20),
        name="arrange",
    )(blocks, extra)


def by_column(place, states, cols, after):
    rows, columns = states[0].shape
    width = columns // cols
    count = len(states)

    def body(place_ref, *refs):
        for i in range(count):
            refs[count + 1][0, i] = refs[i][...]

    return pl.pallas_call(
        body,
        grid_spec=pltpu.PrefetchScalarGridSpec(
            num_scalar_prefetch=1,
            grid=(cols,),
            in_specs=[pl.BlockSpec((rows, width), lambda k, place: (0, place[0] ^ k))]
            * count
            + [pl.BlockSpec(after.shape, lambda k, place: (0, 0))],
            out_specs=pl.BlockSpec(
                (1, count, rows, width), lambda k, place: (k, 0, 0, 0)
            ),
        ),
        out_shape=jax.ShapeDtypeStruct((cols, count, rows, width), states[0].dtype),
        compiler_params=pltpu.CompilerParams(vmem_limit_bytes=16 * 2**20),
        cost_estimate=cost(2 * count * rows * columns, 0),
        name="by_column",
    )(place, *states, after)


def flat_update(place, norm, start, gradient, states, kept=(), ln_states=()):
    count, cols, rows, width = gradient.shape
    state = pl.BlockSpec((rows, cols * width), lambda d, place: (start + d, 0))
    ln = [pl.BlockSpec(x.shape, lambda d, place: (0, 0)) for x in ln_states]

    def body(place_ref, norm_ref, gradient_ref, *refs):
        refs = list(refs)
        take = lambda number: [refs.pop(0) for _ in range(number)]
        state_refs, _, ln_refs = take(3), take(len(kept)), take(len(ln))
        out_refs, ln_out_refs = take(3), refs
        clip_scale = clip_factor(jnp.sum(norm_ref[...], axis=1, keepdims=True))
        for column in range(cols):
            here = slice(column * width, (column + 1) * width)
            master, first, second = (ref[:, here] for ref in state_refs)
            results = adam_step(
                gradient_ref[0, place_ref[0] ^ column],
                clip_scale,
                first,
                second,
                master,
                decay_rate,
            )
            for out_ref, result in zip(out_refs, results):
                out_ref[:, here] = result

        if ln:

            @pl.when(pl.program_id(0) == 0)
            def _():
                ln_gradient, ln_master, ln_first, ln_second, ln_average = (
                    ref[...] for ref in ln_refs
                )
                results = adam_step(
                    ln_gradient, clip_scale, ln_first, ln_second, ln_master, 0.0
                )
                average = ema_keep * ln_average + (1.0 - ema_keep) * results[0]
                for out_ref, result in zip(ln_out_refs, (*results, average)):
                    out_ref[...] = result

    out = pl.pallas_call(
        body,
        grid_spec=pltpu.PrefetchScalarGridSpec(
            num_scalar_prefetch=1,
            grid=(count,),
            in_specs=[
                pl.BlockSpec(norm.shape, lambda d, place: (0, 0)),
                pl.BlockSpec((1, cols, rows, width), lambda d, place: (d, 0, 0, 0)),
            ]
            + [state] * 3
            + [pl.BlockSpec(memory_space=pl.ANY)] * len(kept)
            + ln,
            out_specs=[state] * 3 + ln[1:],
        ),
        out_shape=[
            jax.ShapeDtypeStruct(x.shape, x.dtype) for x in (*states, *ln_states[1:])
        ],
        input_output_aliases={6 + i: i for i in range(len(kept))},
        compiler_params=pltpu.CompilerParams(vmem_limit_bytes=16 * 2**20),
        cost_estimate=cost(7 * gradient.size, gradient.size),
        name="flat_update",
    )(place, norm, gradient, *states, *kept, *ln_states)
    return out[:3], out[3:]


def block_average(place, norm, blocks, average):
    cols, count, span, width = blocks.shape

    def body(place_ref, norm_ref, blocks_ref, average_ref, out_ref, passed_ref):
        passed_ref[...] = norm_ref[...]
        clip_scale = clip_factor(jnp.sum(norm_ref[...], axis=1, keepdims=True))
        master, first, second, gradient = (blocks_ref[0, i] for i in range(count))
        master_new, _, _ = adam_step(
            gradient, clip_scale, first, second, master, decay_rate
        )
        out_ref[...] = ema_keep * average_ref[...] + (1.0 - ema_keep) * master_new

    block = pl.BlockSpec((span, width), lambda k, place: (place[0] ^ k, 0))
    whole = pl.BlockSpec(norm.shape, lambda k, place: (0, 0))
    return pl.pallas_call(
        body,
        grid_spec=pltpu.PrefetchScalarGridSpec(
            num_scalar_prefetch=1,
            grid=(cols,),
            in_specs=[
                whole,
                pl.BlockSpec((1, count, span, width), lambda k, place: (k, 0, 0, 0)),
                block,
            ],
            out_specs=[block, whole],
        ),
        out_shape=[jax.ShapeDtypeStruct(x.shape, x.dtype) for x in (average, norm)],
        compiler_params=pltpu.CompilerParams(vmem_limit_bytes=16 * 2**20),
        cost_estimate=cost(6 * average.size, average.size),
        name="block_average",
    )(place, norm, blocks, average)


def send(held, axis, s):
    if s == 0:
        return held
    size = lax.axis_size(axis)
    return lax.ppermute(held, axis, [(i, i ^ s) for i in range(size)])


def butterfly_sum(held, axis):
    step = 1
    while step < lax.axis_size(axis):
        held = held + send(held, axis, step)
        step *= 2
    return held


def tree_sum(terms):
    while len(terms) > 1:
        terms = [a + b for a, b in zip(terms[::2], terms[1::2])]
    return terms[0]


def over_groups(held):
    return lax.all_to_all(held, "dp", split_axis=0, concat_axis=0, tiled=True)


def shards(
    grad_blocks,
    ln_grads,
    master,
    first_moment,
    second_moment,
    average,
    ln_master,
    ln_first,
    ln_second,
    ln_average,
):
    groups, row_count, cols = (lax.axis_size(name) for name in ("dp", "row", "col"))
    place = lax.axis_index("col").astype(jnp.int32).reshape(1)
    _, rows, width = grad_blocks.shape
    flat = rows // cols
    piece_rows = flat // groups
    f32, f16 = jnp.float32, jnp.float16
    states = (master, first_moment, second_moment)

    ln_rows = ln_grads.shape[1]
    *parts, after = arrange(
        grad_blocks.reshape(cols * groups, piece_rows, width),
        jnp.pad(ln_grads[0], ((0, -ln_rows % 16), (0, 0))),
    )
    parts = [send(part, "dp", s) for s, part in enumerate(parts)]

    block_states = by_column(place, states, cols, after).astype(f16)
    parts[0], _ = lax.optimization_barrier((parts[0], block_states[0, 0, :1]))
    block_states = [send(block_states[k], "col", k) for k in range(cols)]

    total = tree_sum([part.astype(f32) for part in parts])
    ln_gradient = total[cols * piece_rows :][:ln_rows]
    total = total[: cols * piece_rows].reshape(cols, piece_rows, width)
    pieces = over_groups(
        jnp.broadcast_to(total.astype(f16), (groups, *total.shape))
    )

    norm = jnp.sum(total * total, axis=(0, 1)) + jnp.sum(
        ln_gradient * ln_gradient, axis=0
    ) / float(row_count * groups)
    norm = butterfly_sum(norm.reshape(1, width), "row")
    norm = butterfly_sum(norm, "col")
    norm = tree_sum([send(norm, "dp", s) for s in range(groups)])

    half = groups // 2
    near = [send(pieces[:, k], "col", k) for k in range(2)]
    halves = [
        jnp.stack(
            [x[at] for x in near]
            + [send(pieces[at, k], "col", k) for k in range(2, cols)],
            axis=1,
        )
        for at in (slice(0, half), slice(half, groups))
    ]
    blocks = [
        jnp.concatenate([x, pieces[:, k].reshape(1, flat, width)])
        for k, x in enumerate(block_states)
    ]
    average_new, norm = block_average(
        place, norm, jnp.stack(blocks).astype(f32), average
    )
    updated, ln_updated = flat_update(
        place,
        norm,
        0,
        halves[0].astype(f32),
        states,
        ln_states=(ln_gradient, ln_master, ln_first, ln_second, ln_average),
    )
    updated, _ = flat_update(place, norm, half, halves[1].astype(f32), states, updated)
    return (average_new, *updated, *ln_updated)


def solution(mesh):
    placed = (
        P("dp", "row", "col"),
        P("dp", None, "col"),
        P(("row", "col"), None),
        P(("row", "col"), None),
        P(("row", "col"), None),
        P("row", "col"),
        P(None, "col"),
        P(None, "col"),
        P(None, "col"),
        P(None, "col"),
    )
    return jax.shard_map(
        shards,
        mesh=mesh,
        in_specs=placed,
        out_specs=(
            P("row", "col"),
            P(("row", "col"), None),
            P(("row", "col"), None),
            P(("row", "col"), None),
            P(None, "col"),
            P(None, "col"),
            P(None, "col"),
            P(None, "col"),
        ),
        check_vma=False,
    )
```

```python
import functools
import math

import jax
import jax.numpy as jnp
from jax import lax
from jax.experimental import pallas as pl
from jax.experimental.pallas import tpu as pltpu
from jax.sharding import PartitionSpec as P

D = 1024
FF = 4096
STEP = 20


beta_one = 0.9
beta_two = 0.95
learn_rate = 0.02
decay_rate = 0.1
epsilon = 1e-08
clip_rms = 1.0
ema_keep = 0.9


def adam_step(gradient, clip_scale, first, second, master, decay_weight):
    clipped = clip_scale * gradient
    first_new = beta_one * first + (1.0 - beta_one) * clipped
    second_new = beta_two * second + (1.0 - beta_two) * clipped * clipped
    direction = (
        first_new
        * (1.0 / (1.0 - beta_one**STEP))
        / (jnp.sqrt(second_new * (1.0 / (1.0 - beta_two**STEP))) + epsilon)
    )
    master_new = master - learn_rate * (direction + decay_weight * master)
    return (master_new, first_new, second_new)


def clip_factor(norm_total):
    return jnp.minimum(1.0, clip_rms * math.sqrt(FF * D + 4 * D) / jnp.sqrt(norm_total))


def cost(moved, steps):
    return pl.CostEstimate(
        flops=20 * steps, bytes_accessed=4 * moved, transcendentals=2 * steps
    )


def arrange(blocks, extra):
    groups, cols = lax.axis_size("dp"), lax.axis_size("col")
    _, rows, width = blocks.shape
    span = cols * rows

    def body(blocks_ref, extra_ref, *outs):
        outs[groups][...] = jnp.zeros_like(outs[groups])
        group, col = lax.axis_index("dp"), lax.axis_index("col")
        for s in range(groups):
            for k in range(cols):
                outs[s][k * rows : (k + 1) * rows] = blocks_ref[
                    (col ^ k) * groups + (group ^ s)
                ]
            outs[s][span:] = extra_ref[...]

    return pl.pallas_call(
        body,
        in_specs=[pl.BlockSpec(memory_space=pltpu.VMEM)] * 2,
        out_specs=[pl.BlockSpec(memory_space=pltpu.VMEM)] * (groups + 1),
        out_shape=[
            jax.ShapeDtypeStruct((span + extra.shape[0], width), blocks.dtype)
        ]
        * groups
        + [jax.ShapeDtypeStruct((8, 128), jnp.float32)],
        compiler_params=pltpu.CompilerParams(vmem_limit_bytes=16 * 2**20),
        name="arrange",
    )(blocks, extra)


def by_column(place, states, cols, after):
    rows, columns = states[0].shape
    width = columns // cols
    count = len(states)

    def body(place_ref, *refs):
        for i in range(count):
            refs[count + 1][0, i] = refs[i][...]
        refs[count + 2][...] = jnp.ones((8, 128), jnp.float32)

    return pl.pallas_call(
        body,
        grid_spec=pltpu.PrefetchScalarGridSpec(
            num_scalar_prefetch=1,
            grid=(cols,),
            in_specs=[pl.BlockSpec((rows, width), lambda k, place: (0, place[0] ^ k))]
            * count
            + [pl.BlockSpec(after.shape, lambda k, place: (0, 0))],
            out_specs=[
                pl.BlockSpec((1, count, rows, width), lambda k, place: (k, 0, 0, 0)),
                pl.BlockSpec((8, 128), lambda k, place: (0, 0)),
            ],
        ),
        out_shape=[
            jax.ShapeDtypeStruct((cols, count, rows, width), states[0].dtype),
            jax.ShapeDtypeStruct((8, 128), jnp.float32),
        ],
        compiler_params=pltpu.CompilerParams(vmem_limit_bytes=16 * 2**20),
        cost_estimate=cost(2 * count * rows * columns, 0),
        name="by_column",
    )(place, *states, after)


def flat_update(place, norm, start, gradient, states, kept=(), ln_states=()):
    count, cols, rows, width = gradient.shape
    state = pl.BlockSpec((rows, cols * width), lambda d, place: (start + d, 0))
    ln = [pl.BlockSpec(x.shape, lambda d, place: (0, 0)) for x in ln_states]

    def body(place_ref, norm_ref, gradient_ref, *refs):
        refs = list(refs)
        take = lambda number: [refs.pop(0) for _ in range(number)]
        state_refs, _, ln_refs = take(3), take(len(kept)), take(len(ln))
        out_refs, one_ref, ln_out_refs = take(3), take(1)[0], refs
        one_ref[...] = jnp.ones((8, 128), jnp.float32)
        clip_scale = clip_factor(jnp.sum(norm_ref[...], axis=1, keepdims=True))
        for column in range(cols):
            here = slice(column * width, (column + 1) * width)
            master, first, second = (ref[:, here] for ref in state_refs)
            results = adam_step(
                gradient_ref[0, place_ref[0] ^ column],
                clip_scale,
                first,
                second,
                master,
                decay_rate,
            )
            for out_ref, result in zip(out_refs, results):
                out_ref[:, here] = result

        if ln:

            @pl.when(pl.program_id(0) == 0)
            def _():
                ln_gradient, ln_master, ln_first, ln_second, ln_average = (
                    ref[...] for ref in ln_refs
                )
                results = adam_step(
                    ln_gradient, clip_scale, ln_first, ln_second, ln_master, 0.0
                )
                average = ema_keep * ln_average + (1.0 - ema_keep) * results[0]
                for out_ref, result in zip(ln_out_refs, (*results, average)):
                    out_ref[...] = result

    out = pl.pallas_call(
        body,
        grid_spec=pltpu.PrefetchScalarGridSpec(
            num_scalar_prefetch=1,
            grid=(count,),
            in_specs=[
                pl.BlockSpec(norm.shape, lambda d, place: (0, 0)),
                pl.BlockSpec((1, cols, rows, width), lambda d, place: (d, 0, 0, 0)),
            ]
            + [state] * 3
            + [pl.BlockSpec(memory_space=pl.ANY)] * len(kept)
            + ln,
            out_specs=[state] * 3
            + [pl.BlockSpec((8, 128), lambda d, place: (0, 0))]
            + ln[1:],
        ),
        out_shape=[jax.ShapeDtypeStruct(x.shape, x.dtype) for x in states]
        + [jax.ShapeDtypeStruct((8, 128), jnp.float32)]
        + [jax.ShapeDtypeStruct(x.shape, x.dtype) for x in ln_states[1:]],
        input_output_aliases={6 + i: i for i in range(len(kept))},
        compiler_params=pltpu.CompilerParams(vmem_limit_bytes=16 * 2**20),
        cost_estimate=cost(7 * gradient.size, gradient.size),
        name="flat_update",
    )(place, norm, gradient, *states, *kept, *ln_states)
    return out[:3], out[3][0, 0], out[4:]


def block_average(place, norm, gradient, states, average):
    groups, cols, rows, width = gradient.shape
    span = groups * rows

    def body(
        place_ref, norm_ref, gradient_ref, states_ref, average_ref, out_ref, passed_ref
    ):
        passed_ref[...] = norm_ref[...]
        clip_scale = clip_factor(jnp.sum(norm_ref[...], axis=1, keepdims=True))
        for d in range(groups):
            here = slice(d * rows, (d + 1) * rows)
            master, first, second = (states_ref[0, i, here] for i in range(3))
            master_new, _, _ = adam_step(
                gradient_ref[d, 0], clip_scale, first, second, master, decay_rate
            )
            out_ref[here] = (
                ema_keep * average_ref[here] + (1.0 - ema_keep) * master_new
            )

    block = pl.BlockSpec((span, width), lambda k, place: (place[0] ^ k, 0))
    whole = pl.BlockSpec(norm.shape, lambda k, place: (0, 0))
    return pl.pallas_call(
        body,
        grid_spec=pltpu.PrefetchScalarGridSpec(
            num_scalar_prefetch=1,
            grid=(cols,),
            in_specs=[
                whole,
                pl.BlockSpec((groups, 1, rows, width), lambda k, place: (0, k, 0, 0)),
                pl.BlockSpec((1, 3, span, width), lambda k, place: (k, 0, 0, 0)),
                block,
            ],
            out_specs=[block, whole],
        ),
        out_shape=[jax.ShapeDtypeStruct(x.shape, x.dtype) for x in (average, norm)],
        compiler_params=pltpu.CompilerParams(vmem_limit_bytes=16 * 2**20),
        cost_estimate=cost(6 * average.size, average.size),
        name="block_average",
    )(place, norm, gradient, states, average)


def send(held, axis, s):
    if s == 0:
        return held
    size = lax.axis_size(axis)
    return lax.ppermute(held, axis, [(i, i ^ s) for i in range(size)])


def butterfly_sum(held, axis):
    step = 1
    while step < lax.axis_size(axis):
        held = held + send(held, axis, step)
        step *= 2
    return held


def tree_sum(terms):
    while len(terms) > 1:
        terms = [a + b for a, b in zip(terms[::2], terms[1::2])]
    return terms[0]


def over_groups(held):
    return lax.all_to_all(held, "dp", split_axis=0, concat_axis=0, tiled=True)


def shards(
    grad_blocks,
    ln_grads,
    master,
    first_moment,
    second_moment,
    average,
    ln_master,
    ln_first,
    ln_second,
    ln_average,
):
    groups, row_count, cols = (lax.axis_size(name) for name in ("dp", "row", "col"))
    place = lax.axis_index("col").astype(jnp.int32).reshape(1)
    _, rows, width = grad_blocks.shape
    flat = rows // cols
    piece_rows = flat // groups
    f32, f16 = jnp.float32, jnp.float16
    states = (master, first_moment, second_moment)

    ln_rows = ln_grads.shape[1]
    *parts, after = arrange(
        grad_blocks.reshape(cols * groups, piece_rows, width),
        jnp.pad(ln_grads[0], ((0, -ln_rows % 16), (0, 0))),
    )
    parts = [send(part, "dp", s) for s, part in enumerate(parts)]

    block_states, one = by_column(place, states, cols, after)
    block_states = block_states.astype(f16)
    block_states = [send(block_states[k], "col", k) for k in range(cols)]

    total = tree_sum([part.astype(f32) for part in parts]) * one[0, 0]
    ln_gradient = total[cols * piece_rows :][:ln_rows]
    total = total[: cols * piece_rows].reshape(cols, piece_rows, width)
    pieces = over_groups(
        jnp.broadcast_to(total.astype(f16), (groups, *total.shape))
    )

    norm = jnp.sum(total * total, axis=(0, 1)) + jnp.sum(
        ln_gradient * ln_gradient, axis=0
    ) / float(row_count * groups)
    norm = butterfly_sum(norm.reshape(1, width), "row")
    norm = butterfly_sum(norm, "col")
    norm = tree_sum([send(norm, "dp", s) for s in range(groups)])

    half = groups // 2
    near = [send(pieces[:, k], "col", k) for k in range(2)]
    halves = [
        jnp.stack(
            [x[at] for x in near]
            + [send(pieces[at, k], "col", k) for k in range(2, cols)],
            axis=1,
        )
        for at in (slice(0, half), slice(half, groups))
    ]
    one = 1.0 + 0.0 * pieces[0, 0, 0, 0].astype(f32)
    average_new, norm = block_average(
        place,
        norm,
        pieces.astype(f32),
        jnp.stack(block_states).astype(f32) * one,
        average,
    )
    updated, one, ln_updated = flat_update(
        place,
        norm,
        0,
        halves[0].astype(f32),
        states,
        ln_states=(ln_gradient, ln_master, ln_first, ln_second, ln_average),
    )
    updated, _, _ = flat_update(
        place, norm, half, halves[1].astype(f32) * one, states, updated
    )
    return (average_new, *updated, *ln_updated)


def solution(mesh):
    placed = (
        P("dp", "row", "col"),
        P("dp", None, "col"),
        P(("row", "col"), None),
        P(("row", "col"), None),
        P(("row", "col"), None),
        P("row", "col"),
        P(None, "col"),
        P(None, "col"),
        P(None, "col"),
        P(None, "col"),
    )
    return jax.shard_map(
        shards,
        mesh=mesh,
        in_specs=placed,
        out_specs=(
            P("row", "col"),
            P(("row", "col"), None),
            P(("row", "col"), None),
            P(("row", "col"), None),
            P(None, "col"),
            P(None, "col"),
            P(None, "col"),
            P(None, "col"),
        ),
        check_vma=False,
    )
```

```python
import functools
import math

import jax
import jax.numpy as jnp
from jax import lax
from jax.experimental import pallas as pl
from jax.experimental.pallas import tpu as pltpu
from jax.sharding import PartitionSpec as P

D = 1024
FF = 4096
STEP = 20


beta_one = 0.9
beta_two = 0.95
learn_rate = 0.02
decay_rate = 0.1
epsilon = 1e-08
clip_rms = 1.0
ema_keep = 0.9


def adam_step(gradient, clip_scale, first, second, master, decay_weight):
    clipped = clip_scale * gradient
    first_new = beta_one * first + (1.0 - beta_one) * clipped
    second_new = beta_two * second + (1.0 - beta_two) * clipped * clipped
    direction = (
        first_new
        * (1.0 / (1.0 - beta_one**STEP))
        / (jnp.sqrt(second_new * (1.0 / (1.0 - beta_two**STEP))) + epsilon)
    )
    master_new = master - learn_rate * (direction + decay_weight * master)
    return (master_new, first_new, second_new)


def clip_factor(norm_total):
    return jnp.minimum(1.0, clip_rms * math.sqrt(FF * D + 4 * D) / jnp.sqrt(norm_total))


def cost(moved, steps):
    return pl.CostEstimate(
        flops=20 * steps, bytes_accessed=4 * moved, transcendentals=2 * steps
    )


def arrange(blocks, extra):
    groups, cols = lax.axis_size("dp"), lax.axis_size("col")
    _, rows, width = blocks.shape
    span = cols * rows

    def body(blocks_ref, extra_ref, *outs):
        outs[groups][...] = jnp.zeros_like(outs[groups])
        group, col = lax.axis_index("dp"), lax.axis_index("col")
        for s in range(groups):
            for k in range(cols):
                outs[s][k * rows : (k + 1) * rows] = blocks_ref[
                    (col ^ k) * groups + (group ^ s)
                ]
            outs[s][span:] = extra_ref[...]

    return pl.pallas_call(
        body,
        in_specs=[pl.BlockSpec(memory_space=pltpu.VMEM)] * 2,
        out_specs=[pl.BlockSpec(memory_space=pltpu.VMEM)] * (groups + 1),
        out_shape=[
            jax.ShapeDtypeStruct((span + extra.shape[0], width), blocks.dtype)
        ]
        * groups
        + [jax.ShapeDtypeStruct((8, 128), jnp.float32)],
        compiler_params=pltpu.CompilerParams(vmem_limit_bytes=16 * 2**20),
        name="arrange",
    )(blocks, extra)


def by_column(place, states, cols, after):
    rows, columns = states[0].shape
    width = columns // cols
    count = len(states)

    def body(place_ref, *refs):
        for i in range(count):
            refs[count + 1][0, i] = refs[i][...]

    return pl.pallas_call(
        body,
        grid_spec=pltpu.PrefetchScalarGridSpec(
            num_scalar_prefetch=1,
            grid=(cols,),
            in_specs=[pl.BlockSpec((rows, width), lambda k, place: (0, place[0] ^ k))]
            * count
            + [pl.BlockSpec(after.shape, lambda k, place: (0, 0))],
            out_specs=pl.BlockSpec(
                (1, count, rows, width), lambda k, place: (k, 0, 0, 0)
            ),
        ),
        out_shape=jax.ShapeDtypeStruct((cols, count, rows, width), states[0].dtype),
        compiler_params=pltpu.CompilerParams(vmem_limit_bytes=16 * 2**20),
        cost_estimate=cost(2 * count * rows * columns, 0),
        name="by_column",
    )(place, *states, after)


def flat_update(place, norm, start, gradient, states, kept=(), ln_states=()):
    count, cols, rows, width = gradient.shape
    state = pl.BlockSpec((rows, cols * width), lambda d, place: (start + d, 0))
    ln = [pl.BlockSpec(x.shape, lambda d, place: (0, 0)) for x in ln_states]

    def body(place_ref, norm_ref, gradient_ref, *refs):
        refs = list(refs)
        take = lambda number: [refs.pop(0) for _ in range(number)]
        state_refs, _, ln_refs = take(3), take(len(kept)), take(len(ln))
        out_refs, one_ref, ln_out_refs = take(3), take(1)[0], refs
        one_ref[...] = jnp.ones((8, 128), jnp.float32)
        clip_scale = clip_factor(jnp.sum(norm_ref[...], axis=1, keepdims=True))
        for column in range(cols):
            here = slice(column * width, (column + 1) * width)
            master, first, second = (ref[:, here] for ref in state_refs)
            results = adam_step(
                gradient_ref[0, place_ref[0] ^ column],
                clip_scale,
                first,
                second,
                master,
                decay_rate,
            )
            for out_ref, result in zip(out_refs, results):
                out_ref[:, here] = result

        if ln:

            @pl.when(pl.program_id(0) == 0)
            def _():
                ln_gradient, ln_master, ln_first, ln_second, ln_average = (
                    ref[...] for ref in ln_refs
                )
                results = adam_step(
                    ln_gradient, clip_scale, ln_first, ln_second, ln_master, 0.0
                )
                average = ema_keep * ln_average + (1.0 - ema_keep) * results[0]
                for out_ref, result in zip(ln_out_refs, (*results, average)):
                    out_ref[...] = result

    out = pl.pallas_call(
        body,
        grid_spec=pltpu.PrefetchScalarGridSpec(
            num_scalar_prefetch=1,
            grid=(count,),
            in_specs=[
                pl.BlockSpec(norm.shape, lambda d, place: (0, 0)),
                pl.BlockSpec((1, cols, rows, width), lambda d, place: (d, 0, 0, 0)),
            ]
            + [state] * 3
            + [pl.BlockSpec(memory_space=pl.ANY)] * len(kept)
            + ln,
            out_specs=[state] * 3
            + [pl.BlockSpec((8, 128), lambda d, place: (0, 0))]
            + ln[1:],
        ),
        out_shape=[jax.ShapeDtypeStruct(x.shape, x.dtype) for x in states]
        + [jax.ShapeDtypeStruct((8, 128), jnp.float32)]
        + [jax.ShapeDtypeStruct(x.shape, x.dtype) for x in ln_states[1:]],
        input_output_aliases={6 + i: i for i in range(len(kept))},
        compiler_params=pltpu.CompilerParams(vmem_limit_bytes=16 * 2**20),
        cost_estimate=cost(7 * gradient.size, gradient.size),
        name="flat_update",
    )(place, norm, gradient, *states, *kept, *ln_states)
    return out[:3], out[3][0, 0], out[4:]


def block_average(place, norm, gradient, states, average):
    groups, cols, rows, width = gradient.shape
    span = groups * rows

    def body(
        place_ref, norm_ref, gradient_ref, states_ref, average_ref, out_ref, passed_ref
    ):
        passed_ref[...] = norm_ref[...]
        clip_scale = clip_factor(jnp.sum(norm_ref[...], axis=1, keepdims=True))
        for d in range(groups):
            here = slice(d * rows, (d + 1) * rows)
            master, first, second = (states_ref[0, i, here] for i in range(3))
            master_new, _, _ = adam_step(
                gradient_ref[d, 0], clip_scale, first, second, master, decay_rate
            )
            out_ref[here] = (
                ema_keep * average_ref[here] + (1.0 - ema_keep) * master_new
            )

    block = pl.BlockSpec((span, width), lambda k, place: (place[0] ^ k, 0))
    whole = pl.BlockSpec(norm.shape, lambda k, place: (0, 0))
    return pl.pallas_call(
        body,
        grid_spec=pltpu.PrefetchScalarGridSpec(
            num_scalar_prefetch=1,
            grid=(cols,),
            in_specs=[
                whole,
                pl.BlockSpec((groups, 1, rows, width), lambda k, place: (0, k, 0, 0)),
                pl.BlockSpec((1, 3, span, width), lambda k, place: (k, 0, 0, 0)),
                block,
            ],
            out_specs=[block, whole],
        ),
        out_shape=[jax.ShapeDtypeStruct(x.shape, x.dtype) for x in (average, norm)],
        compiler_params=pltpu.CompilerParams(vmem_limit_bytes=16 * 2**20),
        cost_estimate=cost(6 * average.size, average.size),
        name="block_average",
    )(place, norm, gradient, states, average)


def send(held, axis, s):
    if s == 0:
        return held
    size = lax.axis_size(axis)
    return lax.ppermute(held, axis, [(i, i ^ s) for i in range(size)])


def butterfly_sum(held, axis):
    step = 1
    while step < lax.axis_size(axis):
        held = held + send(held, axis, step)
        step *= 2
    return held


def tree_sum(terms):
    while len(terms) > 1:
        terms = [a + b for a, b in zip(terms[::2], terms[1::2])]
    return terms[0]


def over_groups(held):
    return lax.all_to_all(held, "dp", split_axis=0, concat_axis=0, tiled=True)


def shards(
    grad_blocks,
    ln_grads,
    master,
    first_moment,
    second_moment,
    average,
    ln_master,
    ln_first,
    ln_second,
    ln_average,
):
    groups, row_count, cols = (lax.axis_size(name) for name in ("dp", "row", "col"))
    place = lax.axis_index("col").astype(jnp.int32).reshape(1)
    _, rows, width = grad_blocks.shape
    flat = rows // cols
    piece_rows = flat // groups
    f32, f16 = jnp.float32, jnp.float16
    states = (master, first_moment, second_moment)

    ln_rows = ln_grads.shape[1]
    *parts, after = arrange(
        grad_blocks.reshape(cols * groups, piece_rows, width),
        jnp.pad(ln_grads[0], ((0, -ln_rows % 16), (0, 0))),
    )
    parts = [send(part, "dp", s) for s, part in enumerate(parts)]

    block_states = by_column(place, states, cols, after).astype(f16)
    parts[0], tie = lax.optimization_barrier((parts[0], block_states[0, 0, :1]))
    block_states = [send(block_states[k], "col", k) for k in range(cols)]

    total = tree_sum([part.astype(f32) for part in parts])
    ln_gradient = total[cols * piece_rows :][:ln_rows]
    total = total[: cols * piece_rows].reshape(cols, piece_rows, width)
    pieces = over_groups(
        jnp.broadcast_to(total.astype(f16), (groups, *total.shape))
    )

    norm = jnp.sum(total * total, axis=(0, 1)) + jnp.sum(
        ln_gradient * ln_gradient, axis=0
    ) / float(row_count * groups)
    norm = norm.reshape(1, width) + 0.0 * tie.astype(f32)
    norm = butterfly_sum(norm, "row")
    norm = butterfly_sum(norm, "col")
    norm = tree_sum([send(norm, "dp", s) for s in range(groups)])

    half = groups // 2
    near = [send(pieces[:, k], "col", k) for k in range(2)]
    halves = [
        jnp.stack(
            [x[at] for x in near]
            + [send(pieces[at, k], "col", k) for k in range(2, cols)],
            axis=1,
        )
        for at in (slice(0, half), slice(half, groups))
    ]
    average_new, norm = block_average(
        place,
        norm,
        pieces.astype(f32),
        jnp.stack(block_states).astype(f32) + 0.0 * norm,
        average,
    )
    updated, one, ln_updated = flat_update(
        place,
        norm,
        0,
        halves[0].astype(f32),
        states,
        ln_states=(ln_gradient, ln_master, ln_first, ln_second, ln_average),
    )
    updated, _, _ = flat_update(
        place, norm, half, halves[1].astype(f32) * one, states, updated
    )
    return (average_new, *updated, *ln_updated)


def solution(mesh):
    placed = (
        P("dp", "row", "col"),
        P("dp", None, "col"),
        P(("row", "col"), None),
        P(("row", "col"), None),
        P(("row", "col"), None),
        P("row", "col"),
        P(None, "col"),
        P(None, "col"),
        P(None, "col"),
        P(None, "col"),
    )
    return jax.shard_map(
        shards,
        mesh=mesh,
        in_specs=placed,
        out_specs=(
            P("row", "col"),
            P(("row", "col"), None),
            P(("row", "col"), None),
            P(("row", "col"), None),
            P(None, "col"),
            P(None, "col"),
            P(None, "col"),
            P(None, "col"),
        ),
        check_vma=False,
    )
```

```python
import functools
import math

import jax
import jax.numpy as jnp
from jax import lax
from jax.experimental import pallas as pl
from jax.experimental.pallas import tpu as pltpu
from jax.sharding import PartitionSpec as P

D = 1024
FF = 4096
STEP = 20


beta_one = 0.9
beta_two = 0.95
learn_rate = 0.02
decay_rate = 0.1
epsilon = 1e-08
clip_rms = 1.0
ema_keep = 0.9


def adam_step(gradient, clip_scale, first, second, master, decay_weight):
    clipped = clip_scale * gradient
    first_new = beta_one * first + (1.0 - beta_one) * clipped
    second_new = beta_two * second + (1.0 - beta_two) * clipped * clipped
    direction = (
        first_new
        * (1.0 / (1.0 - beta_one**STEP))
        / (jnp.sqrt(second_new * (1.0 / (1.0 - beta_two**STEP))) + epsilon)
    )
    master_new = master - learn_rate * (direction + decay_weight * master)
    return (master_new, first_new, second_new)


def clip_factor(norm_total):
    return jnp.minimum(1.0, clip_rms * math.sqrt(FF * D + 4 * D) / jnp.sqrt(norm_total))


def cost(moved, steps):
    return pl.CostEstimate(
        flops=20 * steps, bytes_accessed=4 * moved, transcendentals=2 * steps
    )


def arrange(blocks, extra):
    groups, cols = lax.axis_size("dp"), lax.axis_size("col")
    _, rows, width = blocks.shape
    span = cols * rows

    def body(blocks_ref, extra_ref, *outs):
        outs[groups][...] = jnp.zeros_like(outs[groups])
        group, col = lax.axis_index("dp"), lax.axis_index("col")
        for s in range(groups):
            for k in range(cols):
                outs[s][k * rows : (k + 1) * rows] = blocks_ref[
                    (col ^ k) * groups + (group ^ s)
                ]
            outs[s][span:] = extra_ref[...]

    return pl.pallas_call(
        body,
        in_specs=[pl.BlockSpec(memory_space=pltpu.VMEM)] * 2,
        out_specs=[pl.BlockSpec(memory_space=pltpu.VMEM)] * (groups + 1),
        out_shape=[
            jax.ShapeDtypeStruct((span + extra.shape[0], width), blocks.dtype)
        ]
        * groups
        + [jax.ShapeDtypeStruct((8, 128), jnp.float32)],
        compiler_params=pltpu.CompilerParams(vmem_limit_bytes=16 * 2**20),
        name="arrange",
    )(blocks, extra)


def by_column(place, states, cols, after):
    rows, columns = states[0].shape
    width = columns // cols
    count = len(states)

    def body(place_ref, *refs):
        for i in range(count):
            refs[count + 1][0, i] = refs[i][...]

    return pl.pallas_call(
        body,
        grid_spec=pltpu.PrefetchScalarGridSpec(
            num_scalar_prefetch=1,
            grid=(cols,),
            in_specs=[pl.BlockSpec((rows, width), lambda k, place: (0, place[0] ^ k))]
            * count
            + [pl.BlockSpec(after.shape, lambda k, place: (0, 0))],
            out_specs=pl.BlockSpec(
                (1, count, rows, width), lambda k, place: (k, 0, 0, 0)
            ),
        ),
        out_shape=jax.ShapeDtypeStruct((cols, count, rows, width), states[0].dtype),
        compiler_params=pltpu.CompilerParams(vmem_limit_bytes=16 * 2**20),
        cost_estimate=cost(2 * count * rows * columns, 0),
        name="by_column",
    )(place, *states, after)


def flat_update(place, norm, start, gradient, states, kept=(), ln_states=()):
    count, cols, rows, width = gradient.shape
    state = pl.BlockSpec((rows, cols * width), lambda d, place: (start + d, 0))
    ln = [pl.BlockSpec(x.shape, lambda d, place: (0, 0)) for x in ln_states]

    def body(place_ref, norm_ref, gradient_ref, *refs):
        refs = list(refs)
        take = lambda number: [refs.pop(0) for _ in range(number)]
        state_refs, _, ln_refs = take(3), take(len(kept)), take(len(ln))
        out_refs, one_ref, ln_out_refs = take(3), take(1)[0], refs
        one_ref[...] = jnp.ones((8, 128), jnp.float32)
        clip_scale = clip_factor(jnp.sum(norm_ref[...], axis=1, keepdims=True))
        for column in range(cols):
            here = slice(column * width, (column + 1) * width)
            master, first, second = (ref[:, here] for ref in state_refs)
            results = adam_step(
                gradient_ref[0, place_ref[0] ^ column],
                clip_scale,
                first,
                second,
                master,
                decay_rate,
            )
            for out_ref, result in zip(out_refs, results):
                out_ref[:, here] = result

        if ln:

            @pl.when(pl.program_id(0) == 0)
            def _():
                ln_gradient, ln_master, ln_first, ln_second, ln_average = (
                    ref[...] for ref in ln_refs
                )
                results = adam_step(
                    ln_gradient, clip_scale, ln_first, ln_second, ln_master, 0.0
                )
                average = ema_keep * ln_average + (1.0 - ema_keep) * results[0]
                for out_ref, result in zip(ln_out_refs, (*results, average)):
                    out_ref[...] = result

    out = pl.pallas_call(
        body,
        grid_spec=pltpu.PrefetchScalarGridSpec(
            num_scalar_prefetch=1,
            grid=(count,),
            in_specs=[
                pl.BlockSpec(norm.shape, lambda d, place: (0, 0)),
                pl.BlockSpec((1, cols, rows, width), lambda d, place: (d, 0, 0, 0)),
            ]
            + [state] * 3
            + [pl.BlockSpec(memory_space=pl.ANY)] * len(kept)
            + ln,
            out_specs=[state] * 3
            + [pl.BlockSpec((8, 128), lambda d, place: (0, 0))]
            + ln[1:],
        ),
        out_shape=[jax.ShapeDtypeStruct(x.shape, x.dtype) for x in states]
        + [jax.ShapeDtypeStruct((8, 128), jnp.float32)]
        + [jax.ShapeDtypeStruct(x.shape, x.dtype) for x in ln_states[1:]],
        input_output_aliases={6 + i: i for i in range(len(kept))},
        compiler_params=pltpu.CompilerParams(vmem_limit_bytes=16 * 2**20),
        cost_estimate=cost(7 * gradient.size, gradient.size),
        name="flat_update",
    )(place, norm, gradient, *states, *kept, *ln_states)
    return out[:3], out[3][0, 0], out[4:]


def block_average(place, norm, gradient, states, average):
    groups, cols, rows, width = gradient.shape
    span = groups * rows

    def body(
        place_ref, norm_ref, gradient_ref, states_ref, average_ref, out_ref, passed_ref
    ):
        passed_ref[...] = norm_ref[...]
        clip_scale = clip_factor(jnp.sum(norm_ref[...], axis=1, keepdims=True))
        for d in range(groups):
            here = slice(d * rows, (d + 1) * rows)
            master, first, second = (states_ref[0, i, here] for i in range(3))
            master_new, _, _ = adam_step(
                gradient_ref[d, 0], clip_scale, first, second, master, decay_rate
            )
            out_ref[here] = (
                ema_keep * average_ref[here] + (1.0 - ema_keep) * master_new
            )

    block = pl.BlockSpec((span, width), lambda k, place: (place[0] ^ k, 0))
    whole = pl.BlockSpec(norm.shape, lambda k, place: (0, 0))
    return pl.pallas_call(
        body,
        grid_spec=pltpu.PrefetchScalarGridSpec(
            num_scalar_prefetch=1,
            grid=(cols,),
            in_specs=[
                whole,
                pl.BlockSpec((groups, 1, rows, width), lambda k, place: (0, k, 0, 0)),
                pl.BlockSpec((1, 3, span, width), lambda k, place: (k, 0, 0, 0)),
                block,
            ],
            out_specs=[block, whole],
        ),
        out_shape=[jax.ShapeDtypeStruct(x.shape, x.dtype) for x in (average, norm)],
        compiler_params=pltpu.CompilerParams(vmem_limit_bytes=16 * 2**20),
        cost_estimate=cost(6 * average.size, average.size),
        name="block_average",
    )(place, norm, gradient, states, average)


def send(held, axis, s):
    if s == 0:
        return held
    size = lax.axis_size(axis)
    return lax.ppermute(held, axis, [(i, i ^ s) for i in range(size)])


def butterfly_sum(held, axis):
    step = 1
    while step < lax.axis_size(axis):
        held = held + send(held, axis, step)
        step *= 2
    return held


def tree_sum(terms):
    while len(terms) > 1:
        terms = [a + b for a, b in zip(terms[::2], terms[1::2])]
    return terms[0]


def over_groups(held):
    return lax.all_to_all(held, "dp", split_axis=0, concat_axis=0, tiled=True)


def shards(
    grad_blocks,
    ln_grads,
    master,
    first_moment,
    second_moment,
    average,
    ln_master,
    ln_first,
    ln_second,
    ln_average,
):
    groups, row_count, cols = (lax.axis_size(name) for name in ("dp", "row", "col"))
    place = lax.axis_index("col").astype(jnp.int32).reshape(1)
    _, rows, width = grad_blocks.shape
    flat = rows // cols
    piece_rows = flat // groups
    f32, f16 = jnp.float32, jnp.float16
    states = (master, first_moment, second_moment)

    ln_rows = ln_grads.shape[1]
    *parts, after = arrange(
        grad_blocks.reshape(cols * groups, piece_rows, width),
        jnp.pad(ln_grads[0], ((0, -ln_rows % 16), (0, 0))),
    )
    parts = [send(part, "dp", s) for s, part in enumerate(parts)]

    block_states = by_column(place, states, cols, after).astype(f16)
    parts[0], tie = lax.optimization_barrier((parts[0], block_states[0, 0, :1]))
    block_states = [send(block_states[k], "col", k) for k in range(cols)]

    total = tree_sum([part.astype(f32) for part in parts])
    ln_gradient = total[cols * piece_rows :][:ln_rows]
    total = total[: cols * piece_rows].reshape(cols, piece_rows, width)
    pieces = over_groups(
        jnp.broadcast_to(total.astype(f16), (groups, *total.shape))
    )

    norm = jnp.sum(total * total, axis=(0, 1)) + jnp.sum(
        ln_gradient * ln_gradient, axis=0
    ) / float(row_count * groups)
    norm = norm.reshape(1, width) + 0.0 * tie.astype(f32)
    norm = butterfly_sum(norm, "row")
    norm = butterfly_sum(norm, "col")
    norm = norm + 0.0 * sum(x[0, :1].astype(f32) for x in block_states[1:])
    norm = tree_sum([send(norm, "dp", s) for s in range(groups)])

    half = groups // 2
    near = [send(pieces[:, k], "col", k) for k in range(2)]
    halves = [
        jnp.stack(
            [x[at] for x in near]
            + [send(pieces[at, k], "col", k) for k in range(2, cols)],
            axis=1,
        )
        for at in (slice(0, half), slice(half, groups))
    ]
    average_new, norm = block_average(
        place,
        norm,
        pieces.astype(f32),
        jnp.stack(block_states).astype(f32) + 0.0 * near[1][0, :1].astype(f32),
        average,
    )
    updated, one, ln_updated = flat_update(
        place,
        norm,
        0,
        halves[0].astype(f32),
        states,
        ln_states=(ln_gradient, ln_master, ln_first, ln_second, ln_average),
    )
    updated, _, _ = flat_update(
        place, norm, half, halves[1].astype(f32) * one, states, updated
    )
    return (average_new, *updated, *ln_updated)


def solution(mesh):
    placed = (
        P("dp", "row", "col"),
        P("dp", None, "col"),
        P(("row", "col"), None),
        P(("row", "col"), None),
        P(("row", "col"), None),
        P("row", "col"),
        P(None, "col"),
        P(None, "col"),
        P(None, "col"),
        P(None, "col"),
    )
    return jax.shard_map(
        shards,
        mesh=mesh,
        in_specs=placed,
        out_specs=(
            P("row", "col"),
            P(("row", "col"), None),
            P(("row", "col"), None),
            P(("row", "col"), None),
            P(None, "col"),
            P(None, "col"),
            P(None, "col"),
            P(None, "col"),
        ),
        check_vma=False,
    )
```

```python
import functools
import math

import jax
import jax.numpy as jnp
from jax import lax
from jax.experimental import pallas as pl
from jax.experimental.pallas import tpu as pltpu
from jax.sharding import PartitionSpec as P

D = 1024
FF = 4096
STEP = 20


beta_one = 0.9
beta_two = 0.95
learn_rate = 0.02
decay_rate = 0.1
epsilon = 1e-08
clip_rms = 1.0
ema_keep = 0.9


def adam_step(gradient, clip_scale, first, second, master, decay_weight):
    clipped = clip_scale * gradient
    first_new = beta_one * first + (1.0 - beta_one) * clipped
    second_new = beta_two * second + (1.0 - beta_two) * clipped * clipped
    direction = (
        first_new
        * (1.0 / (1.0 - beta_one**STEP))
        / (jnp.sqrt(second_new * (1.0 / (1.0 - beta_two**STEP))) + epsilon)
    )
    master_new = master - learn_rate * (direction + decay_weight * master)
    return (master_new, first_new, second_new)


def clip_factor(norm_total):
    return jnp.minimum(1.0, clip_rms * math.sqrt(FF * D + 4 * D) / jnp.sqrt(norm_total))


def arrange(blocks, extra):
    groups, cols = lax.axis_size("dp"), lax.axis_size("col")
    _, rows, width = blocks.shape
    span = cols * rows

    def body(blocks_ref, extra_ref, *outs):
        outs[groups][...] = jnp.zeros_like(outs[groups])
        group, col = lax.axis_index("dp"), lax.axis_index("col")
        for s in range(groups):
            for k in range(cols):
                outs[s][k * rows : (k + 1) * rows] = blocks_ref[
                    (col ^ k) * groups + (group ^ s)
                ]
            outs[s][span:] = extra_ref[...]

    return pl.pallas_call(
        body,
        in_specs=[pl.BlockSpec(memory_space=pltpu.VMEM)] * 2,
        out_specs=[pl.BlockSpec(memory_space=pltpu.VMEM)] * (groups + 1),
        out_shape=[
            jax.ShapeDtypeStruct((span + extra.shape[0], width), blocks.dtype)
        ]
        * groups
        + [jax.ShapeDtypeStruct((8, 128), jnp.float32)],
        compiler_params=pltpu.CompilerParams(vmem_limit_bytes=16 * 2**20),
        name="arrange",
    )(blocks, extra)


def by_column(place, states, cols, after):
    rows, columns = states[0].shape
    width = columns // cols
    count = len(states)

    def body(place_ref, *refs):
        for i in range(count):
            refs[count + 1][0, i] = refs[i][...]

    return pl.pallas_call(
        body,
        grid_spec=pltpu.PrefetchScalarGridSpec(
            num_scalar_prefetch=1,
            grid=(cols,),
            in_specs=[pl.BlockSpec((rows, width), lambda k, place: (0, place[0] ^ k))]
            * count
            + [pl.BlockSpec(after.shape, lambda k, place: (0, 0))],
            out_specs=pl.BlockSpec(
                (1, count, rows, width), lambda k, place: (k, 0, 0, 0)
            ),
        ),
        out_shape=jax.ShapeDtypeStruct((cols, count, rows, width), states[0].dtype),
        compiler_params=pltpu.CompilerParams(vmem_limit_bytes=16 * 2**20),
        name="by_column",
    )(place, *states, after)


def flat_update(place, norm, start, gradient, states, kept=(), ln_states=()):
    count, cols, rows, width = gradient.shape
    state = pl.BlockSpec((rows, cols * width), lambda d, place: (start + d, 0))
    ln = [pl.BlockSpec(x.shape, lambda d, place: (0, 0)) for x in ln_states]

    def body(place_ref, norm_ref, gradient_ref, *refs):
        refs = list(refs)
        take = lambda number: [refs.pop(0) for _ in range(number)]
        state_refs, _, ln_refs = take(3), take(len(kept)), take(len(ln))
        out_refs, one_ref, ln_out_refs = take(3), take(1)[0], refs
        one_ref[...] = jnp.ones((8, 128), jnp.float32)
        clip_scale = clip_factor(jnp.sum(norm_ref[:1], axis=1, keepdims=True))
        for column in range(cols):
            here = slice(column * width, (column + 1) * width)
            master, first, second = (ref[:, here] for ref in state_refs)
            results = adam_step(
                gradient_ref[0, place_ref[0] ^ column],
                clip_scale,
                first,
                second,
                master,
                decay_rate,
            )
            for out_ref, result in zip(out_refs, results):
                out_ref[:, here] = result

        if ln:

            @pl.when(pl.program_id(0) == 0)
            def _():
                ln_gradient, ln_master, ln_first, ln_second, ln_average = (
                    ref[...] for ref in ln_refs
                )
                results = adam_step(
                    ln_gradient, clip_scale, ln_first, ln_second, ln_master, 0.0
                )
                average = ema_keep * ln_average + (1.0 - ema_keep) * results[0]
                for out_ref, result in zip(ln_out_refs, (*results, average)):
                    out_ref[...] = result

    out = pl.pallas_call(
        body,
        grid_spec=pltpu.PrefetchScalarGridSpec(
            num_scalar_prefetch=1,
            grid=(count,),
            in_specs=[
                pl.BlockSpec(norm.shape, lambda d, place: (0, 0)),
                pl.BlockSpec((1, cols, rows, width), lambda d, place: (d, 0, 0, 0)),
            ]
            + [state] * 3
            + [pl.BlockSpec(memory_space=pl.ANY)] * len(kept)
            + ln,
            out_specs=[state] * 3
            + [pl.BlockSpec((8, 128), lambda d, place: (0, 0))]
            + ln[1:],
        ),
        out_shape=[jax.ShapeDtypeStruct(x.shape, x.dtype) for x in states]
        + [jax.ShapeDtypeStruct((8, 128), jnp.float32)]
        + [jax.ShapeDtypeStruct(x.shape, x.dtype) for x in ln_states[1:]],
        input_output_aliases={6 + i: i for i in range(len(kept))},
        compiler_params=pltpu.CompilerParams(vmem_limit_bytes=16 * 2**20),
        name="flat_update",
    )(place, norm, gradient, *states, *kept, *ln_states)
    return out[:3], out[3][0, 0], out[4:]


def block_average(place, norm, gradient, states, average):
    groups, cols, rows, width = gradient.shape
    span = groups * rows

    def body(
        place_ref, norm_ref, gradient_ref, states_ref, average_ref, out_ref, passed_ref
    ):
        passed_ref[...] = norm_ref[...]
        clip_scale = clip_factor(jnp.sum(norm_ref[:1], axis=1, keepdims=True))
        for d in range(groups):
            here = slice(d * rows, (d + 1) * rows)
            master, first, second = (states_ref[0, i, here] for i in range(3))
            master_new, _, _ = adam_step(
                gradient_ref[d, 0], clip_scale, first, second, master, decay_rate
            )
            out_ref[here] = (
                ema_keep * average_ref[here] + (1.0 - ema_keep) * master_new
            )

    block = pl.BlockSpec((span, width), lambda k, place: (place[0] ^ k, 0))
    whole = pl.BlockSpec(norm.shape, lambda k, place: (0, 0))
    return pl.pallas_call(
        body,
        grid_spec=pltpu.PrefetchScalarGridSpec(
            num_scalar_prefetch=1,
            grid=(cols,),
            in_specs=[
                whole,
                pl.BlockSpec((groups, 1, rows, width), lambda k, place: (0, k, 0, 0)),
                pl.BlockSpec((1, 3, span, width), lambda k, place: (k, 0, 0, 0)),
                block,
            ],
            out_specs=[block, whole],
        ),
        out_shape=[jax.ShapeDtypeStruct(x.shape, x.dtype) for x in (average, norm)],
        compiler_params=pltpu.CompilerParams(vmem_limit_bytes=16 * 2**20),
        name="block_average",
    )(place, norm, gradient, states, average)


def send(held, axis, s):
    if s == 0:
        return held
    size = lax.axis_size(axis)
    return lax.ppermute(held, axis, [(i, i ^ s) for i in range(size)])


def butterfly_sum(held, axis):
    step = 1
    while step < lax.axis_size(axis):
        held = held + send(held, axis, step)
        step *= 2
    return held


def tree_sum(terms):
    while len(terms) > 1:
        terms = [a + b for a, b in zip(terms[::2], terms[1::2])]
    return terms[0]


def over_groups(held):
    return lax.all_to_all(held, "dp", split_axis=0, concat_axis=0, tiled=True)


def shards(
    grad_blocks,
    ln_grads,
    master,
    first_moment,
    second_moment,
    average,
    ln_master,
    ln_first,
    ln_second,
    ln_average,
):
    groups, row_count, cols = (lax.axis_size(name) for name in ("dp", "row", "col"))
    place = lax.axis_index("col").astype(jnp.int32).reshape(1)
    _, rows, width = grad_blocks.shape
    flat = rows // cols
    piece_rows = flat // groups
    f32, f16 = jnp.float32, jnp.float16
    states = (master, first_moment, second_moment)

    ln_rows = ln_grads.shape[1]
    *parts, after = arrange(
        grad_blocks.reshape(cols * groups, piece_rows, width),
        jnp.pad(ln_grads[0], ((0, -ln_rows % 16), (0, 0))),
    )
    parts = [send(part, "dp", s) for s, part in enumerate(parts)]

    block_states = by_column(place, states, cols, after).astype(f16)
    parts[0], tie = lax.optimization_barrier((parts[0], block_states[0, 0, :1]))
    block_states = [send(block_states[k], "col", k) for k in range(cols)]

    total = tree_sum([part.astype(f32) for part in parts])
    ln_gradient = total[cols * piece_rows :][:ln_rows]
    total = total[: cols * piece_rows].reshape(cols, piece_rows, width)
    pieces = over_groups(
        jnp.broadcast_to(total.astype(f16), (groups, *total.shape))
    )

    norm = jnp.sum(total * total, axis=(0, 1)) + jnp.sum(
        ln_gradient * ln_gradient, axis=0
    ) / float(row_count * groups)
    norm = butterfly_sum(norm.reshape(1, width), "row")
    norm = butterfly_sum(norm, "col")
    norm = norm + 0.0 * sum(x[0, :1].astype(f32) for x in (*block_states, tie[None]))
    norm = tree_sum([send(norm, "dp", s) for s in range(groups)])

    half = groups // 2
    near = [send(pieces[:, k], "col", k) for k in range(2)]
    halves = [
        jnp.stack(
            [x[at] for x in near]
            + [send(pieces[at, k], "col", k) for k in range(2, cols)],
            axis=1,
        )
        for at in (slice(0, half), slice(half, groups))
    ]
    average_new, norm = block_average(
        place, norm, pieces.astype(f32), jnp.stack(block_states).astype(f32) + 0.0 * norm[:1], average
    )
    updated, one, ln_updated = flat_update(
        place,
        norm,
        0,
        halves[0].astype(f32),
        states,
        ln_states=(ln_gradient, ln_master, ln_first, ln_second, ln_average),
    )
    updated, _, _ = flat_update(
        place, norm, half, halves[1].astype(f32) * one, states, updated
    )
    return (average_new, *updated, *ln_updated)


def solution(mesh):
    placed = (
        P("dp", "row", "col"),
        P("dp", None, "col"),
        P(("row", "col"), None),
        P(("row", "col"), None),
        P(("row", "col"), None),
        P("row", "col"),
        P(None, "col"),
        P(None, "col"),
        P(None, "col"),
        P(None, "col"),
    )
    return jax.shard_map(
        shards,
        mesh=mesh,
        in_specs=placed,
        out_specs=(
            P("row", "col"),
            P(("row", "col"), None),
            P(("row", "col"), None),
            P(("row", "col"), None),
            P(None, "col"),
            P(None, "col"),
            P(None, "col"),
            P(None, "col"),
        ),
        check_vma=False,
    )
```

```python
import functools
import math

import jax
import jax.numpy as jnp
from jax import lax
from jax.experimental import pallas as pl
from jax.experimental.pallas import tpu as pltpu
from jax.sharding import PartitionSpec as P

D = 1024
FF = 4096
STEP = 20


beta_one = 0.9
beta_two = 0.95
learn_rate = 0.02
decay_rate = 0.1
epsilon = 1e-08
clip_rms = 1.0
ema_keep = 0.9


def adam_step(gradient, clip_scale, first, second, master, decay_weight):
    clipped = clip_scale * gradient
    first_new = beta_one * first + (1.0 - beta_one) * clipped
    second_new = beta_two * second + (1.0 - beta_two) * clipped * clipped
    direction = (
        first_new
        * (1.0 / (1.0 - beta_one**STEP))
        / (jnp.sqrt(second_new * (1.0 / (1.0 - beta_two**STEP))) + epsilon)
    )
    master_new = master - learn_rate * (direction + decay_weight * master)
    return (master_new, first_new, second_new)


def clip_factor(norm_total):
    return jnp.minimum(1.0, clip_rms * math.sqrt(FF * D + 4 * D) / jnp.sqrt(norm_total))


def arrange(blocks, extra):
    groups, cols = lax.axis_size("dp"), lax.axis_size("col")
    _, rows, width = blocks.shape
    span = cols * rows

    def body(blocks_ref, extra_ref, *outs):
        outs[groups][...] = jnp.zeros_like(outs[groups])
        group, col = lax.axis_index("dp"), lax.axis_index("col")
        for s in range(groups):
            for k in range(cols):
                outs[s][k * rows : (k + 1) * rows] = blocks_ref[
                    (col ^ k) * groups + (group ^ s)
                ]
            outs[s][span:] = extra_ref[...]

    return pl.pallas_call(
        body,
        in_specs=[pl.BlockSpec(memory_space=pltpu.VMEM)] * 2,
        out_specs=[pl.BlockSpec(memory_space=pltpu.VMEM)] * (groups + 1),
        out_shape=[
            jax.ShapeDtypeStruct((span + extra.shape[0], width), blocks.dtype)
        ]
        * groups
        + [jax.ShapeDtypeStruct((8, 128), jnp.float32)],
        compiler_params=pltpu.CompilerParams(vmem_limit_bytes=16 * 2**20),
        name="arrange",
    )(blocks, extra)


def by_column(place, states, cols, after):
    rows, columns = states[0].shape
    width = columns // cols
    count = len(states)

    def body(place_ref, *refs):
        for i in range(count):
            refs[count + 1][0, i] = refs[i][...]

    return pl.pallas_call(
        body,
        grid_spec=pltpu.PrefetchScalarGridSpec(
            num_scalar_prefetch=1,
            grid=(cols,),
            in_specs=[pl.BlockSpec((rows, width), lambda k, place: (0, place[0] ^ k))]
            * count
            + [pl.BlockSpec(after.shape, lambda k, place: (0, 0))],
            out_specs=pl.BlockSpec(
                (1, count, rows, width), lambda k, place: (k, 0, 0, 0)
            ),
        ),
        out_shape=jax.ShapeDtypeStruct((cols, count, rows, width), states[0].dtype),
        compiler_params=pltpu.CompilerParams(vmem_limit_bytes=16 * 2**20),
        name="by_column",
    )(place, *states, after)


def flat_update(place, norm, start, gradient, states, kept=(), ln_states=()):
    count, cols, rows, width = gradient.shape
    state = pl.BlockSpec((rows, cols * width), lambda d, place: (start + d, 0))
    ln = [pl.BlockSpec(x.shape, lambda d, place: (0, 0)) for x in ln_states]

    def body(place_ref, norm_ref, gradient_ref, *refs):
        refs = list(refs)
        take = lambda number: [refs.pop(0) for _ in range(number)]
        state_refs, _, ln_refs = take(3), take(len(kept)), take(len(ln))
        out_refs, one_ref, ln_out_refs = take(3), take(1)[0], refs
        one_ref[...] = jnp.ones((8, 128), jnp.float32)
        clip_scale = clip_factor(jnp.sum(norm_ref[:1], axis=1, keepdims=True))
        for column in range(cols):
            here = slice(column * width, (column + 1) * width)
            master, first, second = (ref[:, here] for ref in state_refs)
            results = adam_step(
                gradient_ref[0, place_ref[0] ^ column],
                clip_scale,
                first,
                second,
                master,
                decay_rate,
            )
            for out_ref, result in zip(out_refs, results):
                out_ref[:, here] = result

        if ln:

            @pl.when(pl.program_id(0) == 0)
            def _():
                ln_gradient, ln_master, ln_first, ln_second, ln_average = (
                    ref[...] for ref in ln_refs
                )
                results = adam_step(
                    ln_gradient, clip_scale, ln_first, ln_second, ln_master, 0.0
                )
                average = ema_keep * ln_average + (1.0 - ema_keep) * results[0]
                for out_ref, result in zip(ln_out_refs, (*results, average)):
                    out_ref[...] = result

    out = pl.pallas_call(
        body,
        grid_spec=pltpu.PrefetchScalarGridSpec(
            num_scalar_prefetch=1,
            grid=(count,),
            in_specs=[
                pl.BlockSpec(norm.shape, lambda d, place: (0, 0)),
                pl.BlockSpec((1, cols, rows, width), lambda d, place: (d, 0, 0, 0)),
            ]
            + [state] * 3
            + [pl.BlockSpec(memory_space=pl.ANY)] * len(kept)
            + ln,
            out_specs=[state] * 3
            + [pl.BlockSpec((8, 128), lambda d, place: (0, 0))]
            + ln[1:],
        ),
        out_shape=[jax.ShapeDtypeStruct(x.shape, x.dtype) for x in states]
        + [jax.ShapeDtypeStruct((8, 128), jnp.float32)]
        + [jax.ShapeDtypeStruct(x.shape, x.dtype) for x in ln_states[1:]],
        input_output_aliases={6 + i: i for i in range(len(kept))},
        compiler_params=pltpu.CompilerParams(vmem_limit_bytes=16 * 2**20),
        name="flat_update",
    )(place, norm, gradient, *states, *kept, *ln_states)
    return out[:3], out[3][0, 0], out[4:]


def block_average(place, norm, gradient, states, average):
    groups, cols, rows, width = gradient.shape
    span = groups * rows

    def body(
        place_ref, norm_ref, gradient_ref, states_ref, average_ref, out_ref, passed_ref
    ):
        passed_ref[...] = norm_ref[...]
        clip_scale = clip_factor(jnp.sum(norm_ref[:1], axis=1, keepdims=True))
        for d in range(groups):
            here = slice(d * rows, (d + 1) * rows)
            master, first, second = (states_ref[0, i, here] for i in range(3))
            master_new, _, _ = adam_step(
                gradient_ref[d, 0], clip_scale, first, second, master, decay_rate
            )
            out_ref[here] = (
                ema_keep * average_ref[here] + (1.0 - ema_keep) * master_new
            )

    block = pl.BlockSpec((span, width), lambda k, place: (place[0] ^ k, 0))
    whole = pl.BlockSpec(norm.shape, lambda k, place: (0, 0))
    return pl.pallas_call(
        body,
        grid_spec=pltpu.PrefetchScalarGridSpec(
            num_scalar_prefetch=1,
            grid=(cols,),
            in_specs=[
                whole,
                pl.BlockSpec((groups, 1, rows, width), lambda k, place: (0, k, 0, 0)),
                pl.BlockSpec((1, 3, span, width), lambda k, place: (k, 0, 0, 0)),
                block,
            ],
            out_specs=[block, whole],
        ),
        out_shape=[jax.ShapeDtypeStruct(x.shape, x.dtype) for x in (average, norm)],
        compiler_params=pltpu.CompilerParams(vmem_limit_bytes=16 * 2**20),
        name="block_average",
    )(place, norm, gradient, states, average)


def send(held, axis, s):
    if s == 0:
        return held
    size = lax.axis_size(axis)
    return lax.ppermute(held, axis, [(i, i ^ s) for i in range(size)])


def butterfly_sum(held, axis):
    step = 1
    while step < lax.axis_size(axis):
        held = held + send(held, axis, step)
        step *= 2
    return held


def tree_sum(terms):
    while len(terms) > 1:
        terms = [a + b for a, b in zip(terms[::2], terms[1::2])]
    return terms[0]


def over_groups(held):
    return lax.all_to_all(held, "dp", split_axis=0, concat_axis=0, tiled=True)


def shards(
    grad_blocks,
    ln_grads,
    master,
    first_moment,
    second_moment,
    average,
    ln_master,
    ln_first,
    ln_second,
    ln_average,
):
    groups, row_count, cols = (lax.axis_size(name) for name in ("dp", "row", "col"))
    place = lax.axis_index("col").astype(jnp.int32).reshape(1)
    _, rows, width = grad_blocks.shape
    flat = rows // cols
    piece_rows = flat // groups
    f32, f16 = jnp.float32, jnp.float16
    states = (master, first_moment, second_moment)

    ln_rows = ln_grads.shape[1]
    *parts, after = arrange(
        grad_blocks.reshape(cols * groups, piece_rows, width),
        jnp.pad(ln_grads[0], ((0, -ln_rows % 16), (0, 0))),
    )
    parts = [send(part, "dp", s) for s, part in enumerate(parts)]

    block_states = by_column(place, states, cols, after).astype(f16)
    block_states = [send(block_states[k], "col", k) for k in range(cols)]
    parts[0], tie = lax.optimization_barrier((parts[0], block_states[1][0, :1]))

    total = tree_sum([part.astype(f32) for part in parts])
    ln_gradient = total[cols * piece_rows :][:ln_rows]
    total = total[: cols * piece_rows].reshape(cols, piece_rows, width)
    pieces = over_groups(
        jnp.broadcast_to(total.astype(f16), (groups, *total.shape))
    )

    norm = jnp.sum(total * total, axis=(0, 1)) + jnp.sum(
        ln_gradient * ln_gradient, axis=0
    ) / float(row_count * groups)
    norm = butterfly_sum(norm.reshape(1, width), "row")
    step = 1
    while step < cols:
        if 2 * step == cols:
            norm = norm + 0.0 * sum(
                x[0, :1].astype(f32) for x in (tie[None], *block_states[2:])
            )
        norm = norm + send(norm, "col", step)
        step *= 2
    norm = tree_sum([send(norm, "dp", s) for s in range(groups)])

    half = groups // 2
    near = [send(pieces[:, k], "col", k) for k in range(2)]
    halves = [
        jnp.stack(
            [x[at] for x in near]
            + [send(pieces[at, k], "col", k) for k in range(2, cols)],
            axis=1,
        )
        for at in (slice(0, half), slice(half, groups))
    ]
    average_new, norm = block_average(
        place, norm, pieces.astype(f32), jnp.stack(block_states).astype(f32), average
    )
    updated, one, ln_updated = flat_update(
        place,
        norm,
        0,
        halves[0].astype(f32),
        states,
        ln_states=(ln_gradient, ln_master, ln_first, ln_second, ln_average),
    )
    updated, _, _ = flat_update(
        place, norm, half, halves[1].astype(f32) * one, states, updated
    )
    return (average_new, *updated, *ln_updated)


def solution(mesh):
    placed = (
        P("dp", "row", "col"),
        P("dp", None, "col"),
        P(("row", "col"), None),
        P(("row", "col"), None),
        P(("row", "col"), None),
        P("row", "col"),
        P(None, "col"),
        P(None, "col"),
        P(None, "col"),
        P(None, "col"),
    )
    return jax.shard_map(
        shards,
        mesh=mesh,
        in_specs=placed,
        out_specs=(
            P("row", "col"),
            P(("row", "col"), None),
            P(("row", "col"), None),
            P(("row", "col"), None),
            P(None, "col"),
            P(None, "col"),
            P(None, "col"),
            P(None, "col"),
        ),
        check_vma=False,
    )
```

```python
import functools
import math

import jax
import jax.numpy as jnp
from jax import lax
from jax.experimental import pallas as pl
from jax.experimental.pallas import tpu as pltpu
from jax.sharding import PartitionSpec as P

D = 1024
FF = 4096
STEP = 20


beta_one = 0.9
beta_two = 0.95
learn_rate = 0.02
decay_rate = 0.1
epsilon = 1e-08
clip_rms = 1.0
ema_keep = 0.9


def adam_step(gradient, clip_scale, first, second, master, decay_weight):
    clipped = clip_scale * gradient
    first_new = beta_one * first + (1.0 - beta_one) * clipped
    second_new = beta_two * second + (1.0 - beta_two) * clipped * clipped
    direction = (
        first_new
        * (1.0 / (1.0 - beta_one**STEP))
        / (jnp.sqrt(second_new * (1.0 / (1.0 - beta_two**STEP))) + epsilon)
    )
    master_new = master - learn_rate * (direction + decay_weight * master)
    return (master_new, first_new, second_new)


def clip_factor(norm_total):
    return jnp.minimum(1.0, clip_rms * math.sqrt(FF * D + 4 * D) / jnp.sqrt(norm_total))


def arrange(blocks, extra):
    groups, cols = lax.axis_size("dp"), lax.axis_size("col")
    _, rows, width = blocks.shape
    span = cols * rows

    def body(blocks_ref, extra_ref, *outs):
        outs[groups][...] = jnp.zeros_like(outs[groups])
        group, col = lax.axis_index("dp"), lax.axis_index("col")
        for s in range(groups):
            for k in range(cols):
                outs[s][k * rows : (k + 1) * rows] = blocks_ref[
                    (col ^ k) * groups + (group ^ s)
                ]
            outs[s][span:] = extra_ref[...]

    return pl.pallas_call(
        body,
        in_specs=[pl.BlockSpec(memory_space=pltpu.VMEM)] * 2,
        out_specs=[pl.BlockSpec(memory_space=pltpu.VMEM)] * (groups + 1),
        out_shape=[
            jax.ShapeDtypeStruct((span + extra.shape[0], width), blocks.dtype)
        ]
        * groups
        + [jax.ShapeDtypeStruct((8, 128), jnp.float32)],
        compiler_params=pltpu.CompilerParams(vmem_limit_bytes=16 * 2**20),
        name="arrange",
    )(blocks, extra)


def by_column(states, cols, after):
    rows, columns = states[0].shape
    width = columns // cols
    count = len(states)

    def body(*refs):
        for i in range(count):
            refs[count + 1][0, i] = refs[i][...]

    return pl.pallas_call(
        body,
        grid=(cols,),
        in_specs=[pl.BlockSpec((rows, width), lambda c: (0, c))] * count
        + [pl.BlockSpec(after.shape, lambda c: (0, 0))],
        out_specs=pl.BlockSpec((1, count, rows, width), lambda c: (c, 0, 0, 0)),
        out_shape=jax.ShapeDtypeStruct((cols, count, rows, width), states[0].dtype),
        compiler_params=pltpu.CompilerParams(vmem_limit_bytes=16 * 2**20),
        name="by_column",
    )(*states, after)


def flat_update(place, norm, gradient, states, ln_states):
    groups, cols, rows, width = gradient.shape
    state = pl.BlockSpec((rows, cols * width), lambda s, place: (place[0] ^ s, 0))
    whole = pl.BlockSpec(norm.shape, lambda s, place: (0, 0))
    ln = [pl.BlockSpec(x.shape, lambda s, place: (0, 0)) for x in ln_states]

    def body(place_ref, norm_ref, gradient_ref, *refs):
        refs = list(refs)
        state_refs, ln_refs = refs[:3], refs[3:8]
        out_refs, ln_out_refs = refs[8:11], refs[11:]
        clip_scale = clip_factor(
            jnp.sum(
                jnp.sum(norm_ref[...], axis=0, keepdims=True), axis=1, keepdims=True
            )
        )
        for column in range(cols):
            here = slice(column * width, (column + 1) * width)
            master, first, second = (ref[:, here] for ref in state_refs)
            results = adam_step(
                gradient_ref[0, place_ref[1] ^ column],
                clip_scale,
                first,
                second,
                master,
                decay_rate,
            )
            for out_ref, result in zip(out_refs, results):
                out_ref[:, here] = result

        @pl.when(pl.program_id(0) == 0)
        def _():
            ln_gradient, ln_master, ln_first, ln_second, ln_average = (
                ref[...] for ref in ln_refs
            )
            results = adam_step(
                ln_gradient, clip_scale, ln_first, ln_second, ln_master, 0.0
            )
            average = ema_keep * ln_average + (1.0 - ema_keep) * results[0]
            for out_ref, result in zip(ln_out_refs, (*results, average)):
                out_ref[...] = result

    return pl.pallas_call(
        body,
        grid_spec=pltpu.PrefetchScalarGridSpec(
            num_scalar_prefetch=1,
            grid=(groups,),
            in_specs=[
                whole,
                pl.BlockSpec((1, cols, rows, width), lambda s, place: (s, 0, 0, 0)),
            ]
            + [state] * 3
            + ln,
            out_specs=[state] * 3 + ln[1:],
        ),
        out_shape=[
            jax.ShapeDtypeStruct(x.shape, x.dtype) for x in (*states, *ln_states[1:])
        ],
        compiler_params=pltpu.CompilerParams(vmem_limit_bytes=16 * 2**20),
        name="flat_update",
    )(place, norm, gradient, *states, *ln_states)


def block_average(place, norm, gradient, states, average):
    groups, cols, rows, width = gradient.shape
    span = groups * rows

    def body(
        place_ref, norm_ref, gradient_ref, states_ref, average_ref, out_ref, passed_ref
    ):
        passed_ref[...] = norm_ref[...]
        clip_scale = clip_factor(
            jnp.sum(
                jnp.sum(norm_ref[...], axis=0, keepdims=True), axis=1, keepdims=True
            )
        )
        for group in range(groups):
            here = slice(group * rows, (group + 1) * rows)
            master, first, second = (states_ref[0, i, here] for i in range(3))
            master_new, _, _ = adam_step(
                gradient_ref[place_ref[0] ^ group, 0],
                clip_scale,
                first,
                second,
                master,
                decay_rate,
            )
            out_ref[here] = (
                ema_keep * average_ref[here] + (1.0 - ema_keep) * master_new
            )

    block = pl.BlockSpec((span, width), lambda c, place: (c, 0))
    return pl.pallas_call(
        body,
        grid_spec=pltpu.PrefetchScalarGridSpec(
            num_scalar_prefetch=1,
            grid=(cols,),
            in_specs=[
                pl.BlockSpec(norm.shape, lambda c, place: (0, 0)),
                pl.BlockSpec(
                    (groups, 1, rows, width),
                    lambda c, place: (0, place[1] ^ c, 0, 0),
                ),
                pl.BlockSpec((1, 3, span, width), lambda c, place: (c, 0, 0, 0)),
                block,
            ],
            out_specs=[block, pl.BlockSpec(norm.shape, lambda c, place: (0, 0))],
        ),
        out_shape=[
            jax.ShapeDtypeStruct(x.shape, x.dtype) for x in (average, norm)
        ],
        compiler_params=pltpu.CompilerParams(vmem_limit_bytes=16 * 2**20),
        name="block_average",
    )(place, norm, gradient, states, average)


def tree_sum(terms):
    while len(terms) > 1:
        terms = [a + b for a, b in zip(terms[::2], terms[1::2])]
    return terms[0]


def send(held, axis, s):
    if s == 0:
        return held
    size = lax.axis_size(axis)
    return lax.ppermute(held, axis, [(i, i ^ s) for i in range(size)])


def exchange(held, axis):
    return [send(held, axis, s) for s in range(lax.axis_size(axis))]


def shards(
    grad_blocks,
    ln_grads,
    master,
    first_moment,
    second_moment,
    average,
    ln_master,
    ln_first,
    ln_second,
    ln_average,
):
    groups, row_count, cols = (lax.axis_size(name) for name in ("dp", "row", "col"))
    place = jnp.stack([lax.axis_index("dp"), lax.axis_index("col")]).astype(jnp.int32)
    _, rows, width = grad_blocks.shape
    flat = rows // cols
    piece_rows = flat // groups
    f32, f16 = jnp.float32, jnp.float16
    states = (master, first_moment, second_moment)

    ln_rows = ln_grads.shape[1]
    *parts, after = arrange(
        grad_blocks.reshape(cols * groups, piece_rows, width),
        jnp.pad(ln_grads[0], ((0, -ln_rows % 16), (0, 0))),
    )
    parts = [send(part, "dp", s) for s, part in enumerate(parts)]

    block_states = lax.all_to_all(
        by_column(states, cols, after).astype(f16),
        "col",
        split_axis=0,
        concat_axis=0,
        tiled=True,
    )

    total = tree_sum([part.astype(f32) for part in parts])
    ln_gradient = total[cols * piece_rows :][:ln_rows]
    total = total[: cols * piece_rows].reshape(cols, piece_rows, width)
    norm = jnp.sum(total * total, axis=(0, 1)) + jnp.sum(
        ln_gradient * ln_gradient, axis=0
    ) / float(row_count * groups)
    norm = tree_sum(exchange(norm.reshape(1, width), "dp"))
    pieces = exchange(total.astype(f16), "dp")
    own, norm = lax.optimization_barrier((pieces[0], norm))

    flat_own = [None, None] + [send(own[k], "col", k) for k in range(2, cols)]
    norm = lax.all_gather(norm, ("row", "col"), tiled=True)
    stacked = jnp.stack(pieces, axis=1)
    flat = [
        send(stacked[k], "col", k)
        if k < 2
        else jnp.concatenate([flat_own[k][None], send(stacked[k, 1:], "col", k)])
        for k in range(cols)
    ]
    average_new, norm = block_average(
        place, norm, jnp.stack(pieces).astype(f32), block_states.astype(f32), average
    )
    updated = flat_update(
        place,
        norm,
        jnp.stack(flat, axis=1).astype(f32) + 0.0 * norm[:1],
        states,
        (ln_gradient, ln_master, ln_first, ln_second, ln_average),
    )
    return (average_new, *updated)


def solution(mesh):
    placed = (
        P("dp", "row", "col"),
        P("dp", None, "col"),
        P(("row", "col"), None),
        P(("row", "col"), None),
        P(("row", "col"), None),
        P("row", "col"),
        P(None, "col"),
        P(None, "col"),
        P(None, "col"),
        P(None, "col"),
    )
    return jax.shard_map(
        shards,
        mesh=mesh,
        in_specs=placed,
        out_specs=(
            P("row", "col"),
            P(("row", "col"), None),
            P(("row", "col"), None),
            P(("row", "col"), None),
            P(None, "col"),
            P(None, "col"),
            P(None, "col"),
            P(None, "col"),
        ),
        check_vma=False,
    )
```

```python
import functools
import math

import jax
import jax.numpy as jnp
from jax import lax
from jax.experimental import pallas as pl
from jax.experimental.pallas import tpu as pltpu
from jax.sharding import PartitionSpec as P

D = 1024
FF = 4096
STEP = 20


beta_one = 0.9
beta_two = 0.95
learn_rate = 0.02
decay_rate = 0.1
epsilon = 1e-08
clip_rms = 1.0
ema_keep = 0.9


def adam_step(gradient, clip_scale, first, second, master, decay_weight):
    clipped = clip_scale * gradient
    first_new = beta_one * first + (1.0 - beta_one) * clipped
    second_new = beta_two * second + (1.0 - beta_two) * clipped * clipped
    direction = (
        first_new
        * (1.0 / (1.0 - beta_one**STEP))
        / (jnp.sqrt(second_new * (1.0 / (1.0 - beta_two**STEP))) + epsilon)
    )
    master_new = master - learn_rate * (direction + decay_weight * master)
    return (master_new, first_new, second_new)


def clip_factor(norm_total):
    return jnp.minimum(1.0, clip_rms * math.sqrt(FF * D + 4 * D) / jnp.sqrt(norm_total))


def arrange(blocks, extra):
    groups, cols = lax.axis_size("dp"), lax.axis_size("col")
    _, rows, width = blocks.shape
    span = cols * rows

    def body(blocks_ref, extra_ref, *outs):
        outs[groups][...] = jnp.zeros_like(outs[groups])
        group, col = lax.axis_index("dp"), lax.axis_index("col")
        for s in range(groups):
            for k in range(cols):
                outs[s][k * rows : (k + 1) * rows] = blocks_ref[
                    (col ^ k) * groups + (group ^ s)
                ]
            outs[s][span:] = extra_ref[...]

    return pl.pallas_call(
        body,
        in_specs=[pl.BlockSpec(memory_space=pltpu.VMEM)] * 2,
        out_specs=[pl.BlockSpec(memory_space=pltpu.VMEM)] * (groups + 1),
        out_shape=[
            jax.ShapeDtypeStruct((span + extra.shape[0], width), blocks.dtype)
        ]
        * groups
        + [jax.ShapeDtypeStruct((8, 128), jnp.float32)],
        compiler_params=pltpu.CompilerParams(vmem_limit_bytes=16 * 2**20),
        name="arrange",
    )(blocks, extra)


def by_column(states, cols, after):
    rows, columns = states[0].shape
    width = columns // cols
    count = len(states)

    def body(*refs):
        for i in range(count):
            refs[count + 1][0, i] = refs[i][...]

    return pl.pallas_call(
        body,
        grid=(cols,),
        in_specs=[pl.BlockSpec((rows, width), lambda c: (0, c))] * count
        + [pl.BlockSpec(after.shape, lambda c: (0, 0))],
        out_specs=pl.BlockSpec((1, count, rows, width), lambda c: (c, 0, 0, 0)),
        out_shape=jax.ShapeDtypeStruct((cols, count, rows, width), states[0].dtype),
        compiler_params=pltpu.CompilerParams(vmem_limit_bytes=16 * 2**20),
        name="by_column",
    )(*states, after)


def flat_update(place, norm, gradient, states, ln_states):
    groups, cols, rows, width = gradient.shape
    state = pl.BlockSpec((rows, cols * width), lambda s, place: (place[0] ^ s, 0))
    whole = pl.BlockSpec(norm.shape, lambda s, place: (0, 0))
    ln = [pl.BlockSpec(x.shape, lambda s, place: (0, 0)) for x in ln_states]

    def body(place_ref, norm_ref, gradient_ref, *refs):
        refs = list(refs)
        state_refs, ln_refs = refs[:3], refs[3:8]
        out_refs, ln_out_refs = refs[8:11], refs[11:]
        clip_scale = clip_factor(
            jnp.sum(
                jnp.sum(norm_ref[...], axis=0, keepdims=True), axis=1, keepdims=True
            )
        )
        for column in range(cols):
            here = slice(column * width, (column + 1) * width)
            master, first, second = (ref[:, here] for ref in state_refs)
            results = adam_step(
                gradient_ref[0, place_ref[1] ^ column],
                clip_scale,
                first,
                second,
                master,
                decay_rate,
            )
            for out_ref, result in zip(out_refs, results):
                out_ref[:, here] = result

        @pl.when(pl.program_id(0) == 0)
        def _():
            ln_gradient, ln_master, ln_first, ln_second, ln_average = (
                ref[...] for ref in ln_refs
            )
            results = adam_step(
                ln_gradient, clip_scale, ln_first, ln_second, ln_master, 0.0
            )
            average = ema_keep * ln_average + (1.0 - ema_keep) * results[0]
            for out_ref, result in zip(ln_out_refs, (*results, average)):
                out_ref[...] = result

    return pl.pallas_call(
        body,
        grid_spec=pltpu.PrefetchScalarGridSpec(
            num_scalar_prefetch=1,
            grid=(groups,),
            in_specs=[
                whole,
                pl.BlockSpec((1, cols, rows, width), lambda s, place: (s, 0, 0, 0)),
            ]
            + [state] * 3
            + ln,
            out_specs=[state] * 3 + ln[1:],
        ),
        out_shape=[
            jax.ShapeDtypeStruct(x.shape, x.dtype) for x in (*states, *ln_states[1:])
        ],
        compiler_params=pltpu.CompilerParams(vmem_limit_bytes=16 * 2**20),
        name="flat_update",
    )(place, norm, gradient, *states, *ln_states)


def block_average(place, norm, gradient, states, average):
    groups, cols, rows, width = gradient.shape
    span = groups * rows

    def body(
        place_ref, norm_ref, gradient_ref, states_ref, average_ref, out_ref, passed_ref
    ):
        passed_ref[...] = norm_ref[...]
        clip_scale = clip_factor(
            jnp.sum(
                jnp.sum(norm_ref[...], axis=0, keepdims=True), axis=1, keepdims=True
            )
        )
        for group in range(groups):
            here = slice(group * rows, (group + 1) * rows)
            master, first, second = (states_ref[0, i, here] for i in range(3))
            master_new, _, _ = adam_step(
                gradient_ref[place_ref[0] ^ group, 0],
                clip_scale,
                first,
                second,
                master,
                decay_rate,
            )
            out_ref[here] = (
                ema_keep * average_ref[here] + (1.0 - ema_keep) * master_new
            )

    block = pl.BlockSpec((span, width), lambda c, place: (c, 0))
    return pl.pallas_call(
        body,
        grid_spec=pltpu.PrefetchScalarGridSpec(
            num_scalar_prefetch=1,
            grid=(cols,),
            in_specs=[
                pl.BlockSpec(norm.shape, lambda c, place: (0, 0)),
                pl.BlockSpec(
                    (groups, 1, rows, width),
                    lambda c, place: (0, place[1] ^ c, 0, 0),
                ),
                pl.BlockSpec((1, 3, span, width), lambda c, place: (c, 0, 0, 0)),
                block,
            ],
            out_specs=[block, pl.BlockSpec(norm.shape, lambda c, place: (0, 0))],
        ),
        out_shape=[
            jax.ShapeDtypeStruct(x.shape, x.dtype) for x in (average, norm)
        ],
        compiler_params=pltpu.CompilerParams(vmem_limit_bytes=16 * 2**20),
        name="block_average",
    )(place, norm, gradient, states, average)


def tree_sum(terms):
    while len(terms) > 1:
        terms = [a + b for a, b in zip(terms[::2], terms[1::2])]
    return terms[0]


def send(held, axis, s):
    if s == 0:
        return held
    size = lax.axis_size(axis)
    return lax.ppermute(held, axis, [(i, i ^ s) for i in range(size)])


def exchange(held, axis):
    return [send(held, axis, s) for s in range(lax.axis_size(axis))]


def shards(
    grad_blocks,
    ln_grads,
    master,
    first_moment,
    second_moment,
    average,
    ln_master,
    ln_first,
    ln_second,
    ln_average,
):
    groups, row_count, cols = (lax.axis_size(name) for name in ("dp", "row", "col"))
    place = jnp.stack([lax.axis_index("dp"), lax.axis_index("col")]).astype(jnp.int32)
    _, rows, width = grad_blocks.shape
    flat = rows // cols
    piece_rows = flat // groups
    f32, f16 = jnp.float32, jnp.float16
    states = (master, first_moment, second_moment)

    ln_rows = ln_grads.shape[1]
    *parts, after = arrange(
        grad_blocks.reshape(cols * groups, piece_rows, width),
        jnp.pad(ln_grads[0], ((0, -ln_rows % 16), (0, 0))),
    )
    parts = [send(part, "dp", s) for s, part in enumerate(parts)]

    block_states = lax.all_to_all(
        by_column(states, cols, after).astype(f16),
        "col",
        split_axis=0,
        concat_axis=0,
        tiled=True,
    )

    total = tree_sum([part.astype(f32) for part in parts])
    ln_gradient = total[cols * piece_rows :][:ln_rows]
    total = total[: cols * piece_rows].reshape(cols, piece_rows, width)
    norm = jnp.sum(total * total, axis=(0, 1)) + jnp.sum(
        ln_gradient * ln_gradient, axis=0
    ) / float(row_count * groups)
    pieces = exchange(total.astype(f16), "dp")

    flat = [[send(pieces[0][k], "col", k)] for k in range(2, cols)]
    norm = lax.all_gather(
        norm.reshape(1, width), ("dp", "row", "col"), tiled=True
    )
    stacked = jnp.stack(pieces, axis=1)
    flat = [[send(stacked[k], "col", k)] for k in range(2)] + [
        own + [send(stacked[k, 1:], "col", k)] for k, own in enumerate(flat, 2)
    ]
    average_new, norm = block_average(
        place, norm, jnp.stack(pieces).astype(f32), block_states.astype(f32), average
    )
    zero = 0.0 * norm[:1]
    gradient = jnp.stack(
        [
            jnp.concatenate(
                [x.reshape(-1, piece_rows, width).astype(f32) + zero for x in parts]
            )
            for parts in flat
        ],
        axis=1,
    )
    updated = flat_update(
        place,
        norm,
        gradient,
        states,
        (ln_gradient, ln_master, ln_first, ln_second, ln_average),
    )
    return (average_new, *updated)


def solution(mesh):
    placed = (
        P("dp", "row", "col"),
        P("dp", None, "col"),
        P(("row", "col"), None),
        P(("row", "col"), None),
        P(("row", "col"), None),
        P("row", "col"),
        P(None, "col"),
        P(None, "col"),
        P(None, "col"),
        P(None, "col"),
    )
    return jax.shard_map(
        shards,
        mesh=mesh,
        in_specs=placed,
        out_specs=(
            P("row", "col"),
            P(("row", "col"), None),
            P(("row", "col"), None),
            P(("row", "col"), None),
            P(None, "col"),
            P(None, "col"),
            P(None, "col"),
            P(None, "col"),
        ),
        check_vma=False,
    )
```

```python
import functools
import math

import jax
import jax.numpy as jnp
from jax import lax
from jax.experimental import pallas as pl
from jax.experimental.pallas import tpu as pltpu
from jax.sharding import PartitionSpec as P

D = 1024
FF = 4096
STEP = 20


beta_one = 0.9
beta_two = 0.95
learn_rate = 0.02
decay_rate = 0.1
epsilon = 1e-08
clip_rms = 1.0
ema_keep = 0.9


def adam_step(gradient, clip_scale, first, second, master, decay_weight):
    clipped = clip_scale * gradient
    first_new = beta_one * first + (1.0 - beta_one) * clipped
    second_new = beta_two * second + (1.0 - beta_two) * clipped * clipped
    direction = (
        first_new
        * (1.0 / (1.0 - beta_one**STEP))
        / (jnp.sqrt(second_new * (1.0 / (1.0 - beta_two**STEP))) + epsilon)
    )
    master_new = master - learn_rate * (direction + decay_weight * master)
    return (master_new, first_new, second_new)


def clip_factor(norm_total):
    return jnp.minimum(1.0, clip_rms * math.sqrt(FF * D + 4 * D) / jnp.sqrt(norm_total))


def arrange(blocks, extra):
    groups, cols = lax.axis_size("dp"), lax.axis_size("col")
    _, rows, width = blocks.shape
    span = cols * rows

    def body(blocks_ref, extra_ref, *outs):
        outs[groups][...] = jnp.zeros_like(outs[groups])
        group, col = lax.axis_index("dp"), lax.axis_index("col")
        for s in range(groups):
            for k in range(cols):
                outs[s][k * rows : (k + 1) * rows] = blocks_ref[
                    (col ^ k) * groups + (group ^ s)
                ]
            outs[s][span:] = extra_ref[...]

    return pl.pallas_call(
        body,
        in_specs=[pl.BlockSpec(memory_space=pltpu.VMEM)] * 2,
        out_specs=[pl.BlockSpec(memory_space=pltpu.VMEM)] * (groups + 1),
        out_shape=[
            jax.ShapeDtypeStruct((span + extra.shape[0], width), blocks.dtype)
        ]
        * groups
        + [jax.ShapeDtypeStruct((8, 128), jnp.float32)],
        compiler_params=pltpu.CompilerParams(vmem_limit_bytes=16 * 2**20),
        name="arrange",
    )(blocks, extra)


def by_column(states, cols, after):
    rows, columns = states[0].shape
    width = columns // cols
    count = len(states)

    def body(*refs):
        for i in range(count):
            refs[count + 1][0, i] = refs[i][...]

    return pl.pallas_call(
        body,
        grid=(cols,),
        in_specs=[pl.BlockSpec((rows, width), lambda c: (0, c))] * count
        + [pl.BlockSpec(after.shape, lambda c: (0, 0))],
        out_specs=pl.BlockSpec((1, count, rows, width), lambda c: (c, 0, 0, 0)),
        out_shape=jax.ShapeDtypeStruct((cols, count, rows, width), states[0].dtype),
        compiler_params=pltpu.CompilerParams(vmem_limit_bytes=16 * 2**20),
        name="by_column",
    )(*states, after)


def hand_on(norm):
    def body(norm_ref, out_ref):
        out_ref[...] = norm_ref[...]

    return pl.pallas_call(
        body,
        out_shape=jax.ShapeDtypeStruct(norm.shape, norm.dtype),
        cost_estimate=pl.CostEstimate(
            flops=0, bytes_accessed=60000000, transcendentals=0
        ),
        name="hand_on",
    )(norm)


def clip_of(norm_ref):
    rows = jnp.sum(norm_ref[...], axis=0, keepdims=True)
    return clip_factor(jnp.sum(rows, axis=1, keepdims=True))


def flat_update(place, norm, start, gradient, states, kept=(), ln_states=()):
    count, cols, rows, width = gradient.shape
    state = pl.BlockSpec(
        (rows, cols * width), lambda s, place: (place[0] ^ (start + s), 0)
    )
    whole = pl.BlockSpec(norm.shape, lambda s, place: (0, 0))
    ln = [pl.BlockSpec(x.shape, lambda s, place: (0, 0)) for x in ln_states]

    def body(place_ref, norm_ref, gradient_ref, *refs):
        refs = list(refs)
        take = lambda number: [refs.pop(0) for _ in range(number)]
        state_refs, _, ln_refs = take(3), take(len(kept)), take(len(ln))
        out_refs, passed_ref, ln_out_refs = take(3), take(1)[0], refs
        passed_ref[...] = norm_ref[...]
        clip_scale = clip_of(norm_ref)
        for column in range(cols):
            here = slice(column * width, (column + 1) * width)
            master, first, second = (ref[:, here] for ref in state_refs)
            results = adam_step(
                gradient_ref[0, place_ref[1] ^ column],
                clip_scale,
                first,
                second,
                master,
                decay_rate,
            )
            for out_ref, result in zip(out_refs, results):
                out_ref[:, here] = result

        if ln:

            @pl.when(pl.program_id(0) == 0)
            def _():
                ln_gradient, ln_master, ln_first, ln_second, ln_average = (
                    ref[...] for ref in ln_refs
                )
                results = adam_step(
                    ln_gradient, clip_scale, ln_first, ln_second, ln_master, 0.0
                )
                average = ema_keep * ln_average + (1.0 - ema_keep) * results[0]
                for out_ref, result in zip(ln_out_refs, (*results, average)):
                    out_ref[...] = result

    out = pl.pallas_call(
        body,
        grid_spec=pltpu.PrefetchScalarGridSpec(
            num_scalar_prefetch=1,
            grid=(count,),
            in_specs=[
                whole,
                pl.BlockSpec((1, cols, rows, width), lambda s, place: (s, 0, 0, 0)),
            ]
            + [state] * 3
            + [pl.BlockSpec(memory_space=pl.ANY)] * len(kept)
            + ln,
            out_specs=[state] * 3 + [whole] + ln[1:],
        ),
        out_shape=[
            jax.ShapeDtypeStruct(x.shape, x.dtype)
            for x in (*states, norm, *ln_states[1:])
        ],
        input_output_aliases={6 + i: i for i in range(len(kept))},
        compiler_params=pltpu.CompilerParams(vmem_limit_bytes=16 * 2**20),
        name="flat_update",
    )(place, norm, gradient, *states, *kept, *ln_states)
    return out[:3], out[3], out[4:]


def block_average(place, norm, gradient, states, average):
    groups, cols, rows, width = gradient.shape
    span = groups * rows

    def body(
        place_ref, norm_ref, gradient_ref, states_ref, average_ref, out_ref, passed_ref
    ):
        passed_ref[...] = norm_ref[...]
        clip_scale = clip_of(norm_ref)
        for group in range(groups):
            here = slice(group * rows, (group + 1) * rows)
            master, first, second = (states_ref[0, i, here] for i in range(3))
            master_new, _, _ = adam_step(
                gradient_ref[place_ref[0] ^ group, 0],
                clip_scale,
                first,
                second,
                master,
                decay_rate,
            )
            out_ref[here] = (
                ema_keep * average_ref[here] + (1.0 - ema_keep) * master_new
            )

    block = pl.BlockSpec((span, width), lambda c, place: (c, 0))
    return pl.pallas_call(
        body,
        grid_spec=pltpu.PrefetchScalarGridSpec(
            num_scalar_prefetch=1,
            grid=(cols,),
            in_specs=[
                pl.BlockSpec(norm.shape, lambda c, place: (0, 0)),
                pl.BlockSpec(
                    (groups, 1, rows, width),
                    lambda c, place: (0, place[1] ^ c, 0, 0),
                ),
                pl.BlockSpec((1, 3, span, width), lambda c, place: (c, 0, 0, 0)),
                block,
            ],
            out_specs=[block, pl.BlockSpec(norm.shape, lambda c, place: (0, 0))],
        ),
        out_shape=[
            jax.ShapeDtypeStruct(x.shape, x.dtype) for x in (average, norm)
        ],
        compiler_params=pltpu.CompilerParams(vmem_limit_bytes=16 * 2**20),
        name="block_average",
    )(place, norm, gradient, states, average)


def tree_sum(terms):
    while len(terms) > 1:
        terms = [a + b for a, b in zip(terms[::2], terms[1::2])]
    return terms[0]


def send(held, axis, s):
    if s == 0:
        return held
    size = lax.axis_size(axis)
    return lax.ppermute(held, axis, [(i, i ^ s) for i in range(size)])


def exchange(held, axis):
    return [send(held, axis, s) for s in range(lax.axis_size(axis))]


def shards(
    grad_blocks,
    ln_grads,
    master,
    first_moment,
    second_moment,
    average,
    ln_master,
    ln_first,
    ln_second,
    ln_average,
):
    groups, row_count, cols = (lax.axis_size(name) for name in ("dp", "row", "col"))
    place = jnp.stack([lax.axis_index("dp"), lax.axis_index("col")]).astype(jnp.int32)
    _, rows, width = grad_blocks.shape
    flat = rows // cols
    piece_rows = flat // groups
    f32, f16 = jnp.float32, jnp.float16
    states = (master, first_moment, second_moment)

    ln_rows = ln_grads.shape[1]
    *parts, after = arrange(
        grad_blocks.reshape(cols * groups, piece_rows, width),
        jnp.pad(ln_grads[0], ((0, -ln_rows % 16), (0, 0))),
    )
    parts = [send(part, "dp", s) for s, part in enumerate(parts)]

    block_states = lax.all_to_all(
        by_column(states, cols, after).astype(f16),
        "col",
        split_axis=0,
        concat_axis=0,
        tiled=True,
    )

    total = tree_sum([part.astype(f32) for part in parts])
    ln_gradient = total[cols * piece_rows :][:ln_rows]
    total = total[: cols * piece_rows].reshape(cols, piece_rows, width)
    norm = jnp.sum(total * total, axis=(0, 1)) + jnp.sum(
        ln_gradient * ln_gradient, axis=0
    ) / float(row_count * groups)
    norm = tree_sum(exchange(norm.reshape(1, width), "dp"))
    pieces = exchange(total.astype(f16), "dp")
    norm = lax.all_gather(hand_on(norm), ("row", "col"), tiled=True)

    half = groups // 2
    near = [send(jnp.stack([x[k] for x in pieces]), "col", k) for k in range(2)]
    halves = [
        [x[at] for x in near]
        + [
            send(jnp.stack([x[k] for x in pieces[at]]), "col", k)
            for k in range(2, cols)
        ]
        for at in (slice(0, half), slice(half, groups))
    ]
    average_new, norm = block_average(
        place, norm, jnp.stack(pieces).astype(f32), block_states.astype(f32), average
    )
    updated, norm, ln_updated = flat_update(
        place,
        norm,
        0,
        jnp.stack(halves[0], axis=1).astype(f32) + 0.0 * norm[:1],
        states,
        ln_states=(ln_gradient, ln_master, ln_first, ln_second, ln_average),
    )
    updated, _, _ = flat_update(
        place,
        norm,
        half,
        jnp.stack(halves[1], axis=1).astype(f32) + 0.0 * norm[:1],
        states,
        updated,
    )
    return (average_new, *updated, *ln_updated)


def solution(mesh):
    placed = (
        P("dp", "row", "col"),
        P("dp", None, "col"),
        P(("row", "col"), None),
        P(("row", "col"), None),
        P(("row", "col"), None),
        P("row", "col"),
        P(None, "col"),
        P(None, "col"),
        P(None, "col"),
        P(None, "col"),
    )
    return jax.shard_map(
        shards,
        mesh=mesh,
        in_specs=placed,
        out_specs=(
            P("row", "col"),
            P(("row", "col"), None),
            P(("row", "col"), None),
            P(("row", "col"), None),
            P(None, "col"),
            P(None, "col"),
            P(None, "col"),
            P(None, "col"),
        ),
        check_vma=False,
    )
```

```python
import functools
import math

import jax
import jax.numpy as jnp
from jax import lax
from jax.experimental import pallas as pl
from jax.experimental.pallas import tpu as pltpu
from jax.sharding import PartitionSpec as P

D = 1024
FF = 4096
STEP = 20


beta_one = 0.9
beta_two = 0.95
learn_rate = 0.02
decay_rate = 0.1
epsilon = 1e-08
clip_rms = 1.0
ema_keep = 0.9


def adam_step(gradient, clip_scale, first, second, master, decay_weight):
    clipped = clip_scale * gradient
    first_new = beta_one * first + (1.0 - beta_one) * clipped
    second_new = beta_two * second + (1.0 - beta_two) * clipped * clipped
    direction = (
        first_new
        * (1.0 / (1.0 - beta_one**STEP))
        / (jnp.sqrt(second_new * (1.0 / (1.0 - beta_two**STEP))) + epsilon)
    )
    master_new = master - learn_rate * (direction + decay_weight * master)
    return (master_new, first_new, second_new)


def clip_factor(norm_total):
    return jnp.minimum(1.0, clip_rms * math.sqrt(FF * D + 4 * D) / jnp.sqrt(norm_total))


def arrange(blocks, extra):
    groups, cols = lax.axis_size("dp"), lax.axis_size("col")
    _, rows, width = blocks.shape
    span = cols * rows

    def body(blocks_ref, extra_ref, *outs):
        outs[groups][...] = jnp.zeros_like(outs[groups])
        group, col = lax.axis_index("dp"), lax.axis_index("col")
        for s in range(groups):
            for k in range(cols):
                outs[s][k * rows : (k + 1) * rows] = blocks_ref[
                    (col ^ k) * groups + (group ^ s)
                ]
            outs[s][span:] = extra_ref[...]

    return pl.pallas_call(
        body,
        in_specs=[pl.BlockSpec(memory_space=pltpu.VMEM)] * 2,
        out_specs=[pl.BlockSpec(memory_space=pltpu.VMEM)] * (groups + 1),
        out_shape=[
            jax.ShapeDtypeStruct((span + extra.shape[0], width), blocks.dtype)
        ]
        * groups
        + [jax.ShapeDtypeStruct((8, 128), jnp.float32)],
        compiler_params=pltpu.CompilerParams(vmem_limit_bytes=16 * 2**20),
        name="arrange",
    )(blocks, extra)


def by_column(states, cols, after):
    rows, columns = states[0].shape
    width = columns // cols
    count = len(states)

    def body(*refs):
        for i in range(count):
            refs[count + 1][0, i] = refs[i][...]

    return pl.pallas_call(
        body,
        grid=(cols,),
        in_specs=[pl.BlockSpec((rows, width), lambda c: (0, c))] * count
        + [pl.BlockSpec(after.shape, lambda c: (0, 0))],
        out_specs=pl.BlockSpec((1, count, rows, width), lambda c: (c, 0, 0, 0)),
        out_shape=jax.ShapeDtypeStruct((cols, count, rows, width), states[0].dtype),
        compiler_params=pltpu.CompilerParams(vmem_limit_bytes=16 * 2**20),
        name="by_column",
    )(*(pltpu.with_memory_space_constraint(x, pltpu.HBM) for x in states), after)


def hand_on(norm):
    def body(norm_ref, out_ref):
        out_ref[...] = norm_ref[...]

    return pl.pallas_call(
        body,
        out_shape=jax.ShapeDtypeStruct(norm.shape, norm.dtype),
        cost_estimate=pl.CostEstimate(
            flops=0, bytes_accessed=60000000, transcendentals=0
        ),
        name="hand_on",
    )(norm)


def clip_of(norm_ref):
    rows = jnp.sum(norm_ref[...], axis=0, keepdims=True)
    return clip_factor(jnp.sum(rows, axis=1, keepdims=True))


def flat_update(place, norm, gradient, states, ln_states):
    groups, cols, rows, width = gradient.shape
    state = pl.BlockSpec((rows, cols * width), lambda s, place: (place[0] ^ s, 0))
    whole = pl.BlockSpec(norm.shape, lambda s, place: (0, 0))
    ln = [pl.BlockSpec(x.shape, lambda s, place: (0, 0)) for x in ln_states]

    def body(place_ref, norm_ref, gradient_ref, *refs):
        refs = list(refs)
        state_refs, ln_refs = refs[:3], refs[3:8]
        out_refs, ln_out_refs = refs[8:11], refs[11:]
        clip_scale = clip_of(norm_ref)
        for column in range(cols):
            here = slice(column * width, (column + 1) * width)
            master, first, second = (ref[:, here] for ref in state_refs)
            results = adam_step(
                gradient_ref[0, place_ref[1] ^ column],
                clip_scale,
                first,
                second,
                master,
                decay_rate,
            )
            for out_ref, result in zip(out_refs, results):
                out_ref[:, here] = result

        @pl.when(pl.program_id(0) == 0)
        def _():
            ln_gradient, ln_master, ln_first, ln_second, ln_average = (
                ref[...] for ref in ln_refs
            )
            results = adam_step(
                ln_gradient, clip_scale, ln_first, ln_second, ln_master, 0.0
            )
            average = ema_keep * ln_average + (1.0 - ema_keep) * results[0]
            for out_ref, result in zip(ln_out_refs, (*results, average)):
                out_ref[...] = result

    return pl.pallas_call(
        body,
        grid_spec=pltpu.PrefetchScalarGridSpec(
            num_scalar_prefetch=1,
            grid=(groups,),
            in_specs=[
                whole,
                pl.BlockSpec((1, cols, rows, width), lambda s, place: (s, 0, 0, 0)),
            ]
            + [state] * 3
            + ln,
            out_specs=[state] * 3 + ln[1:],
        ),
        out_shape=[
            jax.ShapeDtypeStruct(x.shape, x.dtype) for x in (*states, *ln_states[1:])
        ],
        compiler_params=pltpu.CompilerParams(vmem_limit_bytes=16 * 2**20),
        name="flat_update",
    )(place, norm, gradient, *states, *ln_states)


def block_average(place, norm, gradient, states, average):
    groups, cols, rows, width = gradient.shape
    span = groups * rows

    def body(
        place_ref, norm_ref, gradient_ref, states_ref, average_ref, out_ref, passed_ref
    ):
        passed_ref[...] = norm_ref[...]
        clip_scale = clip_of(norm_ref)
        for group in range(groups):
            here = slice(group * rows, (group + 1) * rows)
            master, first, second = (states_ref[0, i, here] for i in range(3))
            master_new, _, _ = adam_step(
                gradient_ref[place_ref[0] ^ group, 0],
                clip_scale,
                first,
                second,
                master,
                decay_rate,
            )
            out_ref[here] = (
                ema_keep * average_ref[here] + (1.0 - ema_keep) * master_new
            )

    block = pl.BlockSpec((span, width), lambda c, place: (c, 0))
    return pl.pallas_call(
        body,
        grid_spec=pltpu.PrefetchScalarGridSpec(
            num_scalar_prefetch=1,
            grid=(cols,),
            in_specs=[
                pl.BlockSpec(norm.shape, lambda c, place: (0, 0)),
                pl.BlockSpec(
                    (groups, 1, rows, width),
                    lambda c, place: (0, place[1] ^ c, 0, 0),
                ),
                pl.BlockSpec((1, 3, span, width), lambda c, place: (c, 0, 0, 0)),
                block,
            ],
            out_specs=[block, pl.BlockSpec(norm.shape, lambda c, place: (0, 0))],
        ),
        out_shape=[
            jax.ShapeDtypeStruct(x.shape, x.dtype) for x in (average, norm)
        ],
        compiler_params=pltpu.CompilerParams(vmem_limit_bytes=16 * 2**20),
        name="block_average",
    )(place, norm, gradient, states, average)


def tree_sum(terms):
    while len(terms) > 1:
        terms = [a + b for a, b in zip(terms[::2], terms[1::2])]
    return terms[0]


def send(held, axis, s):
    if s == 0:
        return held
    size = lax.axis_size(axis)
    return lax.ppermute(held, axis, [(i, i ^ s) for i in range(size)])


def exchange(held, axis):
    return [send(held, axis, s) for s in range(lax.axis_size(axis))]


def shards(
    grad_blocks,
    ln_grads,
    master,
    first_moment,
    second_moment,
    average,
    ln_master,
    ln_first,
    ln_second,
    ln_average,
):
    groups, row_count, cols = (lax.axis_size(name) for name in ("dp", "row", "col"))
    place = jnp.stack([lax.axis_index("dp"), lax.axis_index("col")]).astype(jnp.int32)
    _, rows, width = grad_blocks.shape
    flat = rows // cols
    piece_rows = flat // groups
    f32, f16 = jnp.float32, jnp.float16
    states = (master, first_moment, second_moment)

    ln_rows = ln_grads.shape[1]
    *parts, after = arrange(
        grad_blocks.reshape(cols * groups, piece_rows, width),
        jnp.pad(ln_grads[0], ((0, -ln_rows % 16), (0, 0))),
    )
    parts = [send(part, "dp", s) for s, part in enumerate(parts)]

    block_states = lax.all_to_all(
        by_column(states, cols, after).astype(f16),
        "col",
        split_axis=0,
        concat_axis=0,
        tiled=True,
    )

    total = tree_sum([part.astype(f32) for part in parts])
    ln_gradient = total[cols * piece_rows :][:ln_rows]
    total = total[: cols * piece_rows].reshape(cols, piece_rows, width)
    norm = jnp.sum(total * total, axis=(0, 1)) + jnp.sum(
        ln_gradient * ln_gradient, axis=0
    ) / float(row_count * groups)
    norm = tree_sum(exchange(norm.reshape(1, width), "dp"))
    pieces = exchange(total.astype(f16), "dp")
    norm = lax.all_gather(hand_on(norm), ("row", "col"), tiled=True)

    flat_pieces = [
        send(jnp.stack([x[k] for x in pieces]), "col", k) for k in range(cols)
    ]
    average_new, norm = block_average(
        place, norm, jnp.stack(pieces).astype(f32), block_states.astype(f32), average
    )
    updated = flat_update(
        place,
        norm,
        jnp.stack(flat_pieces, axis=1).astype(f32) + 0.0 * norm[:1],
        states,
        (ln_gradient, ln_master, ln_first, ln_second, ln_average),
    )
    return (average_new, *updated)


def solution(mesh):
    placed = (
        P("dp", "row", "col"),
        P("dp", None, "col"),
        P(("row", "col"), None),
        P(("row", "col"), None),
        P(("row", "col"), None),
        P("row", "col"),
        P(None, "col"),
        P(None, "col"),
        P(None, "col"),
        P(None, "col"),
    )
    return jax.shard_map(
        shards,
        mesh=mesh,
        in_specs=placed,
        out_specs=(
            P("row", "col"),
            P(("row", "col"), None),
            P(("row", "col"), None),
            P(("row", "col"), None),
            P(None, "col"),
            P(None, "col"),
            P(None, "col"),
            P(None, "col"),
        ),
        check_vma=False,
    )
```

```python
import functools
import math

import jax
import jax.numpy as jnp
from jax import lax
from jax.experimental import pallas as pl
from jax.experimental.pallas import tpu as pltpu
from jax.sharding import PartitionSpec as P

D = 1024
FF = 4096
STEP = 20


beta_one = 0.9
beta_two = 0.95
learn_rate = 0.02
decay_rate = 0.1
epsilon = 1e-08
clip_rms = 1.0
ema_keep = 0.9


def adam_step(gradient, clip_scale, first, second, master, decay_weight):
    clipped = clip_scale * gradient
    first_new = beta_one * first + (1.0 - beta_one) * clipped
    second_new = beta_two * second + (1.0 - beta_two) * clipped * clipped
    direction = (
        first_new
        * (1.0 / (1.0 - beta_one**STEP))
        / (jnp.sqrt(second_new * (1.0 / (1.0 - beta_two**STEP))) + epsilon)
    )
    master_new = master - learn_rate * (direction + decay_weight * master)
    return (master_new, first_new, second_new)


def clip_factor(norm_total):
    return jnp.minimum(1.0, clip_rms * math.sqrt(FF * D + 4 * D) / jnp.sqrt(norm_total))


def arrange(blocks, extra):
    groups, cols = lax.axis_size("dp"), lax.axis_size("col")
    _, rows, width = blocks.shape
    span = cols * rows

    def body(blocks_ref, extra_ref, *outs):
        outs[groups][...] = jnp.zeros_like(outs[groups])
        group, col = lax.axis_index("dp"), lax.axis_index("col")
        for s in range(groups):
            for k in range(cols):
                outs[s][k * rows : (k + 1) * rows] = blocks_ref[
                    (col ^ k) * groups + (group ^ s)
                ]
            outs[s][span:] = extra_ref[...]

    return pl.pallas_call(
        body,
        in_specs=[pl.BlockSpec(memory_space=pltpu.VMEM)] * 2,
        out_specs=[pl.BlockSpec(memory_space=pltpu.VMEM)] * (groups + 1),
        out_shape=[
            jax.ShapeDtypeStruct((span + extra.shape[0], width), blocks.dtype)
        ]
        * groups
        + [jax.ShapeDtypeStruct((8, 128), jnp.float32)],
        compiler_params=pltpu.CompilerParams(vmem_limit_bytes=16 * 2**20),
        name="arrange",
    )(blocks, extra)


def in_hbm(arrays):
    return [pltpu.with_memory_space_constraint(x, pltpu.HBM) for x in arrays]


def by_column(states, cols, after):
    rows, columns = states[0].shape
    width = columns // cols
    count = len(states)

    def body(*refs):
        for i in range(count):
            refs[count + 1][0, i] = refs[i][...]

    return pl.pallas_call(
        body,
        grid=(cols,),
        in_specs=[pl.BlockSpec((rows, width), lambda c: (0, c))] * count
        + [pl.BlockSpec(after.shape, lambda c: (0, 0))],
        out_specs=pl.BlockSpec((1, count, rows, width), lambda c: (c, 0, 0, 0)),
        out_shape=jax.ShapeDtypeStruct((cols, count, rows, width), states[0].dtype),
        compiler_params=pltpu.CompilerParams(vmem_limit_bytes=16 * 2**20),
        name="by_column",
    )(*in_hbm(states), after)


def hand_on(norm):
    def body(norm_ref, out_ref):
        out_ref[...] = norm_ref[...]

    return pl.pallas_call(
        body,
        out_shape=jax.ShapeDtypeStruct(norm.shape, norm.dtype),
        cost_estimate=pl.CostEstimate(
            flops=0, bytes_accessed=60000000, transcendentals=0
        ),
        name="hand_on",
    )(norm)


def clip_of(norm_ref):
    rows = jnp.sum(norm_ref[...], axis=0, keepdims=True)
    return clip_factor(jnp.sum(rows, axis=1, keepdims=True))


def flat_update(place, norm, gradient, states, ln_states):
    cols, groups, rows, width = gradient.shape
    state = pl.BlockSpec((rows, cols * width), lambda s, place: (place[0] ^ s, 0))
    whole = pl.BlockSpec(norm.shape, lambda s, place: (0, 0))
    ln = [pl.BlockSpec(x.shape, lambda s, place: (0, 0)) for x in ln_states]

    def body(place_ref, norm_ref, gradient_ref, *refs):
        refs = list(refs)
        state_refs, ln_refs = refs[:3], refs[3:8]
        out_refs, ln_out_refs = refs[8:11], refs[11:]
        clip_scale = clip_of(norm_ref)
        for column in range(cols):
            here = slice(column * width, (column + 1) * width)
            master, first, second = (ref[:, here] for ref in state_refs)
            results = adam_step(
                gradient_ref[place_ref[1] ^ column, 0],
                clip_scale,
                first,
                second,
                master,
                decay_rate,
            )
            for out_ref, result in zip(out_refs, results):
                out_ref[:, here] = result

        @pl.when(pl.program_id(0) == 0)
        def _():
            ln_gradient, ln_master, ln_first, ln_second, ln_average = (
                ref[...] for ref in ln_refs
            )
            results = adam_step(
                ln_gradient, clip_scale, ln_first, ln_second, ln_master, 0.0
            )
            average = ema_keep * ln_average + (1.0 - ema_keep) * results[0]
            for out_ref, result in zip(ln_out_refs, (*results, average)):
                out_ref[...] = result

    return pl.pallas_call(
        body,
        grid_spec=pltpu.PrefetchScalarGridSpec(
            num_scalar_prefetch=1,
            grid=(groups,),
            in_specs=[
                whole,
                pl.BlockSpec((cols, 1, rows, width), lambda s, place: (0, s, 0, 0)),
            ]
            + [state] * 3
            + ln,
            out_specs=[state] * 3 + ln[1:],
        ),
        out_shape=[
            jax.ShapeDtypeStruct(x.shape, x.dtype) for x in (*states, *ln_states[1:])
        ],
        compiler_params=pltpu.CompilerParams(vmem_limit_bytes=16 * 2**20),
        name="flat_update",
    )(place, norm, gradient, *in_hbm(states), *ln_states)


def block_average(place, norm, gradient, states, average):
    groups, cols, rows, width = gradient.shape
    span = groups * rows

    def body(
        place_ref, norm_ref, gradient_ref, states_ref, average_ref, out_ref, passed_ref
    ):
        passed_ref[...] = norm_ref[...]
        clip_scale = clip_of(norm_ref)
        for group in range(groups):
            here = slice(group * rows, (group + 1) * rows)
            master, first, second = (states_ref[0, i, here] for i in range(3))
            master_new, _, _ = adam_step(
                gradient_ref[place_ref[0] ^ group, 0],
                clip_scale,
                first,
                second,
                master,
                decay_rate,
            )
            out_ref[here] = (
                ema_keep * average_ref[here] + (1.0 - ema_keep) * master_new
            )

    block = pl.BlockSpec((span, width), lambda c, place: (c, 0))
    return pl.pallas_call(
        body,
        grid_spec=pltpu.PrefetchScalarGridSpec(
            num_scalar_prefetch=1,
            grid=(cols,),
            in_specs=[
                pl.BlockSpec(norm.shape, lambda c, place: (0, 0)),
                pl.BlockSpec(
                    (groups, 1, rows, width),
                    lambda c, place: (0, place[1] ^ c, 0, 0),
                ),
                pl.BlockSpec((1, 3, span, width), lambda c, place: (c, 0, 0, 0)),
                block,
            ],
            out_specs=[block, pl.BlockSpec(norm.shape, lambda c, place: (0, 0))],
        ),
        out_shape=[
            jax.ShapeDtypeStruct(x.shape, x.dtype) for x in (average, norm)
        ],
        compiler_params=pltpu.CompilerParams(vmem_limit_bytes=16 * 2**20),
        name="block_average",
    )(place, norm, gradient, states, average)


def tree_sum(terms):
    while len(terms) > 1:
        terms = [a + b for a, b in zip(terms[::2], terms[1::2])]
    return terms[0]


def send(held, axis, s):
    if s == 0:
        return held
    size = lax.axis_size(axis)
    return lax.ppermute(held, axis, [(i, i ^ s) for i in range(size)])


def exchange(held, axis):
    return [send(held, axis, s) for s in range(lax.axis_size(axis))]


def shards(
    grad_blocks,
    ln_grads,
    master,
    first_moment,
    second_moment,
    average,
    ln_master,
    ln_first,
    ln_second,
    ln_average,
):
    groups, row_count, cols = (lax.axis_size(name) for name in ("dp", "row", "col"))
    place = jnp.stack([lax.axis_index("dp"), lax.axis_index("col")]).astype(jnp.int32)
    _, rows, width = grad_blocks.shape
    flat = rows // cols
    piece_rows = flat // groups
    f32, f16 = jnp.float32, jnp.float16
    states = (master, first_moment, second_moment)

    ln_rows = ln_grads.shape[1]
    *parts, after = arrange(
        grad_blocks.reshape(cols * groups, piece_rows, width),
        jnp.pad(ln_grads[0], ((0, -ln_rows % 16), (0, 0))),
    )
    parts = [send(part, "dp", s) for s, part in enumerate(parts)]

    block_states = lax.all_to_all(
        by_column(states, cols, after).astype(f16),
        "col",
        split_axis=0,
        concat_axis=0,
        tiled=True,
    )

    total = tree_sum([part.astype(f32) for part in parts])
    ln_gradient = total[cols * piece_rows :][:ln_rows]
    total = total[: cols * piece_rows].reshape(cols, piece_rows, width)
    norm = jnp.sum(total * total, axis=(0, 1)) + jnp.sum(
        ln_gradient * ln_gradient, axis=0
    ) / float(row_count * groups)
    norm = tree_sum(exchange(norm.reshape(1, width), "dp"))
    pieces = exchange(total.astype(f16), "dp")
    norm = lax.all_gather(hand_on(norm), ("row", "col"), tiled=True)

    stacked = jnp.stack(pieces, axis=1)
    flat_pieces = [send(stacked[k], "col", k) for k in range(cols)]
    average_new, norm = block_average(
        place, norm, jnp.stack(pieces).astype(f32), block_states.astype(f32), average
    )
    updated = flat_update(
        place,
        norm,
        jnp.stack(flat_pieces).astype(f32) + 0.0 * norm[:1],
        states,
        (ln_gradient, ln_master, ln_first, ln_second, ln_average),
    )
    return (average_new, *updated)


def solution(mesh):
    placed = (
        P("dp", "row", "col"),
        P("dp", None, "col"),
        P(("row", "col"), None),
        P(("row", "col"), None),
        P(("row", "col"), None),
        P("row", "col"),
        P(None, "col"),
        P(None, "col"),
        P(None, "col"),
        P(None, "col"),
    )
    return jax.shard_map(
        shards,
        mesh=mesh,
        in_specs=placed,
        out_specs=(
            P("row", "col"),
            P(("row", "col"), None),
            P(("row", "col"), None),
            P(("row", "col"), None),
            P(None, "col"),
            P(None, "col"),
            P(None, "col"),
            P(None, "col"),
        ),
        check_vma=False,
    )
```

```python
import functools
import math

import jax
import jax.numpy as jnp
from jax import lax
from jax.experimental import pallas as pl
from jax.experimental.pallas import tpu as pltpu
from jax.sharding import PartitionSpec as P

D = 1024
FF = 4096
STEP = 20


beta_one = 0.9
beta_two = 0.95
learn_rate = 0.02
decay_rate = 0.1
epsilon = 1e-08
clip_rms = 1.0
ema_keep = 0.9


def adam_step(gradient, clip_scale, first, second, master, decay_weight):
    clipped = clip_scale * gradient
    first_new = beta_one * first + (1.0 - beta_one) * clipped
    second_new = beta_two * second + (1.0 - beta_two) * clipped * clipped
    direction = (
        first_new
        * (1.0 / (1.0 - beta_one**STEP))
        / (jnp.sqrt(second_new * (1.0 / (1.0 - beta_two**STEP))) + epsilon)
    )
    master_new = master - learn_rate * (direction + decay_weight * master)
    return (master_new, first_new, second_new)


def clip_factor(norm_total):
    return jnp.minimum(1.0, clip_rms * math.sqrt(FF * D + 4 * D) / jnp.sqrt(norm_total))


def arrange(blocks, extra):
    groups, cols = lax.axis_size("dp"), lax.axis_size("col")
    _, rows, width = blocks.shape
    span = cols * rows

    def body(blocks_ref, extra_ref, *outs):
        outs[groups][...] = jnp.zeros_like(outs[groups])
        group, col = lax.axis_index("dp"), lax.axis_index("col")
        for s in range(groups):
            for k in range(cols):
                outs[s][k * rows : (k + 1) * rows] = blocks_ref[
                    (col ^ k) * groups + (group ^ s)
                ]
            outs[s][span:] = extra_ref[...]

    return pl.pallas_call(
        body,
        in_specs=[pl.BlockSpec(memory_space=pltpu.VMEM)] * 2,
        out_specs=[pl.BlockSpec(memory_space=pltpu.VMEM)] * (groups + 1),
        out_shape=[
            jax.ShapeDtypeStruct((span + extra.shape[0], width), blocks.dtype)
        ]
        * groups
        + [jax.ShapeDtypeStruct((8, 128), jnp.float32)],
        compiler_params=pltpu.CompilerParams(vmem_limit_bytes=16 * 2**20),
        name="arrange",
    )(blocks, extra)


def by_column(states, cols, after):
    rows, columns = states[0].shape
    width = columns // cols
    count = len(states)

    def body(*refs):
        for i in range(count):
            refs[count + 1][0, i] = refs[i][...]

    return pl.pallas_call(
        body,
        grid=(cols,),
        in_specs=[pl.BlockSpec((rows, width), lambda c: (0, c))] * count
        + [pl.BlockSpec(after.shape, lambda c: (0, 0))],
        out_specs=pl.BlockSpec((1, count, rows, width), lambda c: (c, 0, 0, 0)),
        out_shape=jax.ShapeDtypeStruct((cols, count, rows, width), states[0].dtype),
        compiler_params=pltpu.CompilerParams(vmem_limit_bytes=16 * 2**20),
        name="by_column",
    )(*(pltpu.with_memory_space_constraint(x, pltpu.HBM) for x in states), after)


def hand_on(norm):
    def body(norm_ref, out_ref):
        out_ref[...] = norm_ref[...]

    return pl.pallas_call(
        body,
        out_shape=jax.ShapeDtypeStruct(norm.shape, norm.dtype),
        cost_estimate=pl.CostEstimate(
            flops=0, bytes_accessed=200 * 10**6, transcendentals=0
        ),
        name="hand_on",
    )(norm)


def clip_of(norm_ref):
    rows = jnp.sum(norm_ref[...], axis=0, keepdims=True)
    return clip_factor(jnp.sum(rows, axis=1, keepdims=True))


def flat_update(place, norm, start, gradient, states, kept=(), ln_states=()):
    cols, count, rows, width = gradient.shape
    state = pl.BlockSpec(
        (rows, cols * width), lambda s, place: (place[0] ^ (start + s), 0)
    )
    whole = pl.BlockSpec(norm.shape, lambda s, place: (0, 0))
    ln = [pl.BlockSpec(x.shape, lambda s, place: (0, 0)) for x in ln_states]

    def body(place_ref, norm_ref, gradient_ref, *refs):
        refs = list(refs)
        take = lambda number: [refs.pop(0) for _ in range(number)]
        state_refs, _, ln_refs = take(3), take(len(kept)), take(len(ln))
        out_refs, passed_ref, ln_out_refs = take(3), take(1)[0], refs
        passed_ref[...] = norm_ref[...]
        clip_scale = clip_of(norm_ref)
        for column in range(cols):
            here = slice(column * width, (column + 1) * width)
            master, first, second = (ref[:, here] for ref in state_refs)
            results = adam_step(
                gradient_ref[place_ref[1] ^ column, 0],
                clip_scale,
                first,
                second,
                master,
                decay_rate,
            )
            for out_ref, result in zip(out_refs, results):
                out_ref[:, here] = result

        if ln:

            @pl.when(pl.program_id(0) == 0)
            def _():
                ln_gradient, ln_master, ln_first, ln_second, ln_average = (
                    ref[...] for ref in ln_refs
                )
                results = adam_step(
                    ln_gradient, clip_scale, ln_first, ln_second, ln_master, 0.0
                )
                average = ema_keep * ln_average + (1.0 - ema_keep) * results[0]
                for out_ref, result in zip(ln_out_refs, (*results, average)):
                    out_ref[...] = result

    out = pl.pallas_call(
        body,
        grid_spec=pltpu.PrefetchScalarGridSpec(
            num_scalar_prefetch=1,
            grid=(count,),
            in_specs=[
                whole,
                pl.BlockSpec((cols, 1, rows, width), lambda s, place: (0, s, 0, 0)),
            ]
            + [state] * 3
            + [pl.BlockSpec(memory_space=pl.ANY)] * len(kept)
            + ln,
            out_specs=[state] * 3 + [whole] + ln[1:],
        ),
        out_shape=[
            jax.ShapeDtypeStruct(x.shape, x.dtype)
            for x in (*states, norm, *ln_states[1:])
        ],
        input_output_aliases={6 + i: i for i in range(len(kept))},
        compiler_params=pltpu.CompilerParams(vmem_limit_bytes=16 * 2**20),
        name="flat_update",
    )(place, norm, gradient, *states, *kept, *ln_states)
    return out[:3], out[3], out[4:]


def block_average(place, norm, gradient, states, average):
    groups, cols, rows, width = gradient.shape
    span = groups * rows

    def body(
        place_ref, norm_ref, gradient_ref, states_ref, average_ref, out_ref, passed_ref
    ):
        passed_ref[...] = norm_ref[...]
        clip_scale = clip_of(norm_ref)
        for group in range(groups):
            here = slice(group * rows, (group + 1) * rows)
            master, first, second = (states_ref[0, i, here] for i in range(3))
            master_new, _, _ = adam_step(
                gradient_ref[place_ref[0] ^ group, 0],
                clip_scale,
                first,
                second,
                master,
                decay_rate,
            )
            out_ref[here] = (
                ema_keep * average_ref[here] + (1.0 - ema_keep) * master_new
            )

    block = pl.BlockSpec((span, width), lambda c, place: (c, 0))
    return pl.pallas_call(
        body,
        grid_spec=pltpu.PrefetchScalarGridSpec(
            num_scalar_prefetch=1,
            grid=(cols,),
            in_specs=[
                pl.BlockSpec(norm.shape, lambda c, place: (0, 0)),
                pl.BlockSpec(
                    (groups, 1, rows, width),
                    lambda c, place: (0, place[1] ^ c, 0, 0),
                ),
                pl.BlockSpec((1, 3, span, width), lambda c, place: (c, 0, 0, 0)),
                block,
            ],
            out_specs=[block, pl.BlockSpec(norm.shape, lambda c, place: (0, 0))],
        ),
        out_shape=[
            jax.ShapeDtypeStruct(x.shape, x.dtype) for x in (average, norm)
        ],
        compiler_params=pltpu.CompilerParams(vmem_limit_bytes=16 * 2**20),
        name="block_average",
    )(place, norm, gradient, states, average)


def tree_sum(terms):
    while len(terms) > 1:
        terms = [a + b for a, b in zip(terms[::2], terms[1::2])]
    return terms[0]


def send(held, axis, s):
    if s == 0:
        return held
    size = lax.axis_size(axis)
    return lax.ppermute(held, axis, [(i, i ^ s) for i in range(size)])


def exchange(held, axis):
    return [send(held, axis, s) for s in range(lax.axis_size(axis))]


def shards(
    grad_blocks,
    ln_grads,
    master,
    first_moment,
    second_moment,
    average,
    ln_master,
    ln_first,
    ln_second,
    ln_average,
):
    groups, row_count, cols = (lax.axis_size(name) for name in ("dp", "row", "col"))
    place = jnp.stack([lax.axis_index("dp"), lax.axis_index("col")]).astype(jnp.int32)
    _, rows, width = grad_blocks.shape
    flat = rows // cols
    piece_rows = flat // groups
    f32, f16 = jnp.float32, jnp.float16
    states = (master, first_moment, second_moment)

    ln_rows = ln_grads.shape[1]
    *parts, after = arrange(
        grad_blocks.reshape(cols * groups, piece_rows, width),
        jnp.pad(ln_grads[0], ((0, -ln_rows % 16), (0, 0))),
    )
    parts = [send(part, "dp", s) for s, part in enumerate(parts)]

    block_states = lax.all_to_all(
        by_column(states, cols, after).astype(f16),
        "col",
        split_axis=0,
        concat_axis=0,
        tiled=True,
    )

    total = tree_sum([part.astype(f32) for part in parts])
    ln_gradient = total[cols * piece_rows :][:ln_rows]
    total = total[: cols * piece_rows].reshape(cols, piece_rows, width)
    norm = jnp.sum(total * total, axis=(0, 1)) + jnp.sum(
        ln_gradient * ln_gradient, axis=0
    ) / float(row_count * groups)
    norm = tree_sum(exchange(norm.reshape(1, width), "dp"))
    pieces = exchange(total.astype(f16), "dp")
    norm = lax.all_gather(hand_on(norm), ("row", "col"), tiled=True)

    half = groups // 2
    stacked = jnp.stack(pieces, axis=1)
    near = [send(stacked[k], "col", k) for k in range(2)]
    halves = [
        [x[at] for x in near]
        + [send(stacked[k, at], "col", k) for k in range(2, cols)]
        for at in (slice(0, half), slice(half, groups))
    ]
    average_new, norm = block_average(
        place, norm, jnp.stack(pieces).astype(f32), block_states.astype(f32), average
    )
    updated, norm, ln_updated = flat_update(
        place,
        norm,
        0,
        jnp.stack(halves[0]).astype(f32) + 0.0 * norm[:1],
        states,
        ln_states=(ln_gradient, ln_master, ln_first, ln_second, ln_average),
    )
    updated, _, _ = flat_update(
        place,
        norm,
        half,
        jnp.stack(halves[1]).astype(f32) + 0.0 * norm[:1],
        states,
        updated,
    )
    return (average_new, *updated, *ln_updated)


def solution(mesh):
    placed = (
        P("dp", "row", "col"),
        P("dp", None, "col"),
        P(("row", "col"), None),
        P(("row", "col"), None),
        P(("row", "col"), None),
        P("row", "col"),
        P(None, "col"),
        P(None, "col"),
        P(None, "col"),
        P(None, "col"),
    )
    return jax.shard_map(
        shards,
        mesh=mesh,
        in_specs=placed,
        out_specs=(
            P("row", "col"),
            P(("row", "col"), None),
            P(("row", "col"), None),
            P(("row", "col"), None),
            P(None, "col"),
            P(None, "col"),
            P(None, "col"),
            P(None, "col"),
        ),
        check_vma=False,
    )
```

```python
import functools
import math

import jax
import jax.numpy as jnp
from jax import lax
from jax.experimental import pallas as pl
from jax.experimental.pallas import tpu as pltpu
from jax.sharding import PartitionSpec as P

D = 1024
FF = 4096
STEP = 20


beta_one = 0.9
beta_two = 0.95
learn_rate = 0.02
decay_rate = 0.1
epsilon = 1e-08
clip_rms = 1.0
ema_keep = 0.9


root_gain = 1.0 / math.sqrt(1.0 - beta_two**STEP)
step_gain = learn_rate / (1.0 - beta_one**STEP) / root_gain


def adam_step(gradient, clip_scale, first, second, master, decay_weight):
    clipped = clip_scale * gradient
    first_new = beta_one * first + (1.0 - beta_one) * clipped
    second_new = beta_two * second + (1.0 - beta_two) * clipped * clipped
    root = second_new * lax.rsqrt(second_new)
    step = step_gain * first_new / (root + epsilon / root_gain)
    master_new = (1.0 - learn_rate * decay_weight) * master - step
    return (master_new, first_new, second_new)


def clip_factor(norm_total):
    return jnp.minimum(1.0, clip_rms * math.sqrt(FF * D + 4 * D) / jnp.sqrt(norm_total))


def arrange(blocks, extra):
    groups, cols = lax.axis_size("dp"), lax.axis_size("col")
    _, rows, width = blocks.shape
    span = cols * rows

    def body(blocks_ref, extra_ref, *outs):
        outs[groups][...] = jnp.zeros_like(outs[groups])
        group, col = lax.axis_index("dp"), lax.axis_index("col")
        for s in range(groups):
            for k in range(cols):
                outs[s][k * rows : (k + 1) * rows] = blocks_ref[
                    (col ^ k) * groups + (group ^ s)
                ]
            outs[s][span:] = extra_ref[...]

    return pl.pallas_call(
        body,
        in_specs=[pl.BlockSpec(memory_space=pltpu.VMEM)] * 2,
        out_specs=[pl.BlockSpec(memory_space=pltpu.VMEM)] * (groups + 1),
        out_shape=[
            jax.ShapeDtypeStruct((span + extra.shape[0], width), blocks.dtype)
        ]
        * groups
        + [jax.ShapeDtypeStruct((8, 128), jnp.float32)],
        compiler_params=pltpu.CompilerParams(vmem_limit_bytes=16 * 2**20),
        name="arrange",
    )(blocks, extra)


def by_column(states, cols, after):
    rows, columns = states[0].shape
    width = columns // cols
    count = len(states)

    def body(*refs):
        for i in range(count):
            refs[count + 1][0, i] = refs[i][...]

    return pl.pallas_call(
        body,
        grid=(cols,),
        in_specs=[pl.BlockSpec((rows, width), lambda c: (0, c))] * count
        + [pl.BlockSpec(after.shape, lambda c: (0, 0))],
        out_specs=pl.BlockSpec((1, count, rows, width), lambda c: (c, 0, 0, 0)),
        out_shape=jax.ShapeDtypeStruct((cols, count, rows, width), states[0].dtype),
        compiler_params=pltpu.CompilerParams(vmem_limit_bytes=16 * 2**20),
        name="by_column",
    )(*(pltpu.with_memory_space_constraint(x, pltpu.HBM) for x in states), after)


def hand_on(norm):
    def body(norm_ref, out_ref):
        out_ref[...] = norm_ref[...]

    return pl.pallas_call(
        body,
        out_shape=jax.ShapeDtypeStruct(norm.shape, norm.dtype),
        cost_estimate=pl.CostEstimate(
            flops=0, bytes_accessed=60000000, transcendentals=0
        ),
        name="hand_on",
    )(norm)


def clip_of(norm_ref):
    rows = jnp.sum(norm_ref[...], axis=0, keepdims=True)
    return clip_factor(jnp.sum(rows, axis=1, keepdims=True))


def flat_update(place, norm, start, gradient, states, kept=(), ln_states=()):
    count, cols, rows, width = gradient.shape
    state = pl.BlockSpec(
        (rows, cols * width), lambda s, place: (place[0] ^ (start + s), 0)
    )
    whole = pl.BlockSpec(norm.shape, lambda s, place: (0, 0))
    ln = [pl.BlockSpec(x.shape, lambda s, place: (0, 0)) for x in ln_states]

    def body(place_ref, norm_ref, gradient_ref, *refs):
        refs = list(refs)
        take = lambda number: [refs.pop(0) for _ in range(number)]
        state_refs, _, ln_refs = take(3), take(len(kept)), take(len(ln))
        out_refs, passed_ref, ln_out_refs = take(3), take(1)[0], refs
        passed_ref[...] = norm_ref[...]
        clip_scale = clip_of(norm_ref)
        for column in range(cols):
            here = slice(column * width, (column + 1) * width)
            master, first, second = (ref[:, here] for ref in state_refs)
            results = adam_step(
                gradient_ref[0, place_ref[1] ^ column],
                clip_scale,
                first,
                second,
                master,
                decay_rate,
            )
            for out_ref, result in zip(out_refs, results):
                out_ref[:, here] = result

        if ln:

            @pl.when(pl.program_id(0) == 0)
            def _():
                ln_gradient, ln_master, ln_first, ln_second, ln_average = (
                    ref[...] for ref in ln_refs
                )
                results = adam_step(
                    ln_gradient, clip_scale, ln_first, ln_second, ln_master, 0.0
                )
                average = ema_keep * ln_average + (1.0 - ema_keep) * results[0]
                for out_ref, result in zip(ln_out_refs, (*results, average)):
                    out_ref[...] = result

    out = pl.pallas_call(
        body,
        grid_spec=pltpu.PrefetchScalarGridSpec(
            num_scalar_prefetch=1,
            grid=(count,),
            in_specs=[
                whole,
                pl.BlockSpec((1, cols, rows, width), lambda s, place: (s, 0, 0, 0)),
            ]
            + [state] * 3
            + [pl.BlockSpec(memory_space=pl.ANY)] * len(kept)
            + ln,
            out_specs=[state] * 3 + [whole] + ln[1:],
        ),
        out_shape=[
            jax.ShapeDtypeStruct(x.shape, x.dtype)
            for x in (*states, norm, *ln_states[1:])
        ],
        input_output_aliases={6 + i: i for i in range(len(kept))},
        compiler_params=pltpu.CompilerParams(vmem_limit_bytes=16 * 2**20),
        name="flat_update",
    )(place, norm, gradient, *states, *kept, *ln_states)
    return out[:3], out[3], out[4:]


def block_average(place, norm, gradient, states, average):
    groups, cols, rows, width = gradient.shape
    span = groups * rows

    def body(
        place_ref, norm_ref, gradient_ref, states_ref, average_ref, out_ref, passed_ref
    ):
        passed_ref[...] = norm_ref[...]
        clip_scale = clip_of(norm_ref)
        for group in range(groups):
            here = slice(group * rows, (group + 1) * rows)
            master, first, second = (states_ref[0, i, here] for i in range(3))
            master_new, _, _ = adam_step(
                gradient_ref[place_ref[0] ^ group, 0],
                clip_scale,
                first,
                second,
                master,
                decay_rate,
            )
            out_ref[here] = (
                ema_keep * average_ref[here] + (1.0 - ema_keep) * master_new
            )

    block = pl.BlockSpec((span, width), lambda c, place: (c, 0))
    return pl.pallas_call(
        body,
        grid_spec=pltpu.PrefetchScalarGridSpec(
            num_scalar_prefetch=1,
            grid=(cols,),
            in_specs=[
                pl.BlockSpec(norm.shape, lambda c, place: (0, 0)),
                pl.BlockSpec(
                    (groups, 1, rows, width),
                    lambda c, place: (0, place[1] ^ c, 0, 0),
                ),
                pl.BlockSpec((1, 3, span, width), lambda c, place: (c, 0, 0, 0)),
                block,
            ],
            out_specs=[block, pl.BlockSpec(norm.shape, lambda c, place: (0, 0))],
        ),
        out_shape=[
            jax.ShapeDtypeStruct(x.shape, x.dtype) for x in (average, norm)
        ],
        compiler_params=pltpu.CompilerParams(vmem_limit_bytes=16 * 2**20),
        name="block_average",
    )(place, norm, gradient, states, average)


def tree_sum(terms):
    while len(terms) > 1:
        terms = [a + b for a, b in zip(terms[::2], terms[1::2])]
    return terms[0]


def send(held, axis, s):
    if s == 0:
        return held
    size = lax.axis_size(axis)
    return lax.ppermute(held, axis, [(i, i ^ s) for i in range(size)])


def exchange(held, axis):
    return [send(held, axis, s) for s in range(lax.axis_size(axis))]


def shards(
    grad_blocks,
    ln_grads,
    master,
    first_moment,
    second_moment,
    average,
    ln_master,
    ln_first,
    ln_second,
    ln_average,
):
    groups, row_count, cols = (lax.axis_size(name) for name in ("dp", "row", "col"))
    place = jnp.stack([lax.axis_index("dp"), lax.axis_index("col")]).astype(jnp.int32)
    _, rows, width = grad_blocks.shape
    flat = rows // cols
    piece_rows = flat // groups
    f32, f16 = jnp.float32, jnp.float16
    states = (master, first_moment, second_moment)

    ln_rows = ln_grads.shape[1]
    *parts, after = arrange(
        grad_blocks.reshape(cols * groups, piece_rows, width),
        jnp.pad(ln_grads[0], ((0, -ln_rows % 16), (0, 0))),
    )
    parts = [send(part, "dp", s) for s, part in enumerate(parts)]

    block_states = lax.all_to_all(
        by_column(states, cols, after).astype(f16),
        "col",
        split_axis=0,
        concat_axis=0,
        tiled=True,
    )

    total = tree_sum([part.astype(f32) for part in parts])
    ln_gradient = total[cols * piece_rows :][:ln_rows]
    total = total[: cols * piece_rows].reshape(cols, piece_rows, width)
    norm = jnp.sum(total * total, axis=(0, 1)) + jnp.sum(
        ln_gradient * ln_gradient, axis=0
    ) / float(row_count * groups)
    norm = tree_sum(exchange(norm.reshape(1, width), "dp"))
    pieces = exchange(total.astype(f16), "dp")
    norm = lax.all_gather(hand_on(norm), ("row", "col"), tiled=True)

    half = groups // 2
    near = [send(jnp.stack([x[k] for x in pieces]), "col", k) for k in range(2)]
    halves = [
        [x[at] for x in near]
        + [
            send(jnp.stack([x[k] for x in pieces[at]]), "col", k)
            for k in range(2, cols)
        ]
        for at in (slice(0, half), slice(half, groups))
    ]
    average_new, norm = block_average(
        place, norm, jnp.stack(pieces).astype(f32), block_states.astype(f32), average
    )
    updated, norm, ln_updated = flat_update(
        place,
        norm,
        0,
        jnp.stack(halves[0], axis=1).astype(f32) + 0.0 * norm[:1],
        states,
        ln_states=(ln_gradient, ln_master, ln_first, ln_second, ln_average),
    )
    updated, _, _ = flat_update(
        place,
        norm,
        half,
        jnp.stack(halves[1], axis=1).astype(f32) + 0.0 * norm[:1],
        states,
        updated,
    )
    return (average_new, *updated, *ln_updated)


def solution(mesh):
    placed = (
        P("dp", "row", "col"),
        P("dp", None, "col"),
        P(("row", "col"), None),
        P(("row", "col"), None),
        P(("row", "col"), None),
        P("row", "col"),
        P(None, "col"),
        P(None, "col"),
        P(None, "col"),
        P(None, "col"),
    )
    return jax.shard_map(
        shards,
        mesh=mesh,
        in_specs=placed,
        out_specs=(
            P("row", "col"),
            P(("row", "col"), None),
            P(("row", "col"), None),
            P(("row", "col"), None),
            P(None, "col"),
            P(None, "col"),
            P(None, "col"),
            P(None, "col"),
        ),
        check_vma=False,
    )
```

```python
import functools
import math

import jax
import jax.numpy as jnp
from jax import lax
from jax.experimental import pallas as pl
from jax.experimental.pallas import tpu as pltpu
from jax.sharding import PartitionSpec as P

D = 1024
FF = 4096
STEP = 20


beta_one = 0.9
beta_two = 0.95
learn_rate = 0.02
decay_rate = 0.1
epsilon = 1e-08
clip_rms = 1.0
ema_keep = 0.9


root_gain = 1.0 / math.sqrt(1.0 - beta_two**STEP)
step_gain = learn_rate / (1.0 - beta_one**STEP) / root_gain


def adam_step(gradient, clip_scale, first, second, master, decay_weight):
    clipped = clip_scale * gradient
    first_new = beta_one * first + (1.0 - beta_one) * clipped
    second_new = beta_two * second + (1.0 - beta_two) * clipped * clipped
    root = second_new * lax.rsqrt(second_new)
    step = step_gain * first_new / (root + epsilon / root_gain)
    master_new = (1.0 - learn_rate * decay_weight) * master - step
    return (master_new, first_new, second_new)


def clip_factor(norm_total):
    return jnp.minimum(1.0, clip_rms * math.sqrt(FF * D + 4 * D) / jnp.sqrt(norm_total))


def arrange(blocks, extra):
    groups, cols = lax.axis_size("dp"), lax.axis_size("col")
    _, rows, width = blocks.shape
    span = cols * rows

    def body(blocks_ref, extra_ref, *outs):
        outs[groups][...] = jnp.zeros_like(outs[groups])
        group, col = lax.axis_index("dp"), lax.axis_index("col")
        for s in range(groups):
            for k in range(cols):
                outs[s][k * rows : (k + 1) * rows] = blocks_ref[
                    (col ^ k) * groups + (group ^ s)
                ]
            outs[s][span:] = extra_ref[...]

    return pl.pallas_call(
        body,
        in_specs=[pl.BlockSpec(memory_space=pltpu.VMEM)] * 2,
        out_specs=[pl.BlockSpec(memory_space=pltpu.VMEM)] * (groups + 1),
        out_shape=[
            jax.ShapeDtypeStruct((span + extra.shape[0], width), blocks.dtype)
        ]
        * groups
        + [jax.ShapeDtypeStruct((8, 128), jnp.float32)],
        compiler_params=pltpu.CompilerParams(vmem_limit_bytes=16 * 2**20),
        name="arrange",
    )(blocks, extra)


def by_column(states, cols, after):
    rows, columns = states[0].shape
    width = columns // cols
    count = len(states)

    def body(*refs):
        for i in range(count):
            refs[count + 1][0, i] = refs[i][...]

    return pl.pallas_call(
        body,
        grid=(cols,),
        in_specs=[pl.BlockSpec((rows, width), lambda c: (0, c))] * count
        + [pl.BlockSpec(after.shape, lambda c: (0, 0))],
        out_specs=pl.BlockSpec((1, count, rows, width), lambda c: (c, 0, 0, 0)),
        out_shape=jax.ShapeDtypeStruct((cols, count, rows, width), states[0].dtype),
        compiler_params=pltpu.CompilerParams(vmem_limit_bytes=16 * 2**20),
        name="by_column",
    )(*(pltpu.with_memory_space_constraint(x, pltpu.HBM) for x in states), after)


def hand_on(norm):
    def body(norm_ref, out_ref):
        out_ref[...] = norm_ref[...]

    return pl.pallas_call(
        body,
        out_shape=jax.ShapeDtypeStruct(norm.shape, norm.dtype),
        cost_estimate=pl.CostEstimate(
            flops=0, bytes_accessed=60000000, transcendentals=0
        ),
        name="hand_on",
    )(norm)


def clip_of(norm_ref):
    rows = jnp.sum(norm_ref[...], axis=0, keepdims=True)
    return clip_factor(jnp.sum(rows, axis=1, keepdims=True))


def flat_update(place, norm, start, gradient, states, kept=(), ln_states=()):
    count, cols, rows, width = gradient.shape
    cuts = 2 if rows % 16 == 0 else 1
    span = rows // cuts
    state = pl.BlockSpec(
        (span, cols * width),
        lambda s, cut, place: ((place[0] ^ (start + s)) * cuts + cut, 0),
    )
    whole = pl.BlockSpec(norm.shape, lambda s, cut, place: (0, 0))
    ln = [pl.BlockSpec(x.shape, lambda s, cut, place: (0, 0)) for x in ln_states]

    def body(place_ref, norm_ref, gradient_ref, *refs):
        refs = list(refs)
        take = lambda number: [refs.pop(0) for _ in range(number)]
        state_refs, _, ln_refs = take(3), take(len(kept)), take(len(ln))
        out_refs, passed_ref, ln_out_refs = take(3), take(1)[0], refs
        passed_ref[...] = norm_ref[...]
        clip_scale = clip_of(norm_ref)
        for column in range(cols):
            here = slice(column * width, (column + 1) * width)
            master, first, second = (ref[:, here] for ref in state_refs)
            results = adam_step(
                gradient_ref[0, place_ref[1] ^ column],
                clip_scale,
                first,
                second,
                master,
                decay_rate,
            )
            for out_ref, result in zip(out_refs, results):
                out_ref[:, here] = result

        if ln:

            @pl.when((pl.program_id(0) == 0) & (pl.program_id(1) == 0))
            def _():
                ln_gradient, ln_master, ln_first, ln_second, ln_average = (
                    ref[...] for ref in ln_refs
                )
                results = adam_step(
                    ln_gradient, clip_scale, ln_first, ln_second, ln_master, 0.0
                )
                average = ema_keep * ln_average + (1.0 - ema_keep) * results[0]
                for out_ref, result in zip(ln_out_refs, (*results, average)):
                    out_ref[...] = result

    out = pl.pallas_call(
        body,
        grid_spec=pltpu.PrefetchScalarGridSpec(
            num_scalar_prefetch=1,
            grid=(count, cuts),
            in_specs=[
                whole,
                pl.BlockSpec(
                    (1, cols, span, width), lambda s, cut, place: (s, 0, cut, 0)
                ),
            ]
            + [state] * 3
            + [pl.BlockSpec(memory_space=pl.ANY)] * len(kept)
            + ln,
            out_specs=[state] * 3 + [whole] + ln[1:],
        ),
        out_shape=[
            jax.ShapeDtypeStruct(x.shape, x.dtype)
            for x in (*states, norm, *ln_states[1:])
        ],
        input_output_aliases={6 + i: i for i in range(len(kept))},
        compiler_params=pltpu.CompilerParams(vmem_limit_bytes=16 * 2**20),
        name="flat_update",
    )(place, norm, gradient, *states, *kept, *ln_states)
    return out[:3], out[3], out[4:]


def block_average(place, norm, gradient, states, average):
    groups, cols, rows, width = gradient.shape
    cuts = 2
    each = groups // cuts
    span = each * rows

    def body(
        place_ref, norm_ref, gradient_ref, states_ref, average_ref, out_ref, passed_ref
    ):
        passed_ref[...] = norm_ref[...]
        clip_scale = clip_of(norm_ref)
        for part in range(each):
            here = slice(part * rows, (part + 1) * rows)
            group = pl.program_id(1) * each + part
            master, first, second = (states_ref[0, i, here] for i in range(3))
            master_new, _, _ = adam_step(
                gradient_ref[place_ref[0] ^ group, 0],
                clip_scale,
                first,
                second,
                master,
                decay_rate,
            )
            out_ref[here] = (
                ema_keep * average_ref[here] + (1.0 - ema_keep) * master_new
            )

    block = pl.BlockSpec((span, width), lambda c, cut, place: (c * cuts + cut, 0))
    return pl.pallas_call(
        body,
        grid_spec=pltpu.PrefetchScalarGridSpec(
            num_scalar_prefetch=1,
            grid=(cols, cuts),
            in_specs=[
                pl.BlockSpec(norm.shape, lambda c, cut, place: (0, 0)),
                pl.BlockSpec(
                    (groups, 1, rows, width),
                    lambda c, cut, place: (0, place[1] ^ c, 0, 0),
                ),
                pl.BlockSpec((1, 3, span, width), lambda c, cut, place: (c, 0, cut, 0)),
                block,
            ],
            out_specs=[block, pl.BlockSpec(norm.shape, lambda c, cut, place: (0, 0))],
        ),
        out_shape=[
            jax.ShapeDtypeStruct(x.shape, x.dtype) for x in (average, norm)
        ],
        compiler_params=pltpu.CompilerParams(vmem_limit_bytes=16 * 2**20),
        name="block_average",
    )(place, norm, gradient, states, average)


def tree_sum(terms):
    while len(terms) > 1:
        terms = [a + b for a, b in zip(terms[::2], terms[1::2])]
    return terms[0]


def send(held, axis, s):
    if s == 0:
        return held
    size = lax.axis_size(axis)
    return lax.ppermute(held, axis, [(i, i ^ s) for i in range(size)])


def exchange(held, axis):
    return [send(held, axis, s) for s in range(lax.axis_size(axis))]


def shards(
    grad_blocks,
    ln_grads,
    master,
    first_moment,
    second_moment,
    average,
    ln_master,
    ln_first,
    ln_second,
    ln_average,
):
    groups, row_count, cols = (lax.axis_size(name) for name in ("dp", "row", "col"))
    place = jnp.stack([lax.axis_index("dp"), lax.axis_index("col")]).astype(jnp.int32)
    _, rows, width = grad_blocks.shape
    flat = rows // cols
    piece_rows = flat // groups
    f32, f16 = jnp.float32, jnp.float16
    states = (master, first_moment, second_moment)

    ln_rows = ln_grads.shape[1]
    *parts, after = arrange(
        grad_blocks.reshape(cols * groups, piece_rows, width),
        jnp.pad(ln_grads[0], ((0, -ln_rows % 16), (0, 0))),
    )
    parts = [send(part, "dp", s) for s, part in enumerate(parts)]

    block_states = lax.all_to_all(
        by_column(states, cols, after).astype(f16),
        "col",
        split_axis=0,
        concat_axis=0,
        tiled=True,
    )

    total = tree_sum([part.astype(f32) for part in parts])
    ln_gradient = total[cols * piece_rows :][:ln_rows]
    total = total[: cols * piece_rows].reshape(cols, piece_rows, width)
    norm = jnp.sum(total * total, axis=(0, 1)) + jnp.sum(
        ln_gradient * ln_gradient, axis=0
    ) / float(row_count * groups)
    norm = tree_sum(exchange(norm.reshape(1, width), "dp"))
    pieces = exchange(total.astype(f16), "dp")
    norm = lax.all_gather(hand_on(norm), ("row", "col"), tiled=True)

    half = groups // 2
    near = [send(jnp.stack([x[k] for x in pieces]), "col", k) for k in range(2)]
    halves = [
        [x[at] for x in near]
        + [
            send(jnp.stack([x[k] for x in pieces[at]]), "col", k)
            for k in range(2, cols)
        ]
        for at in (slice(0, half), slice(half, groups))
    ]
    average_new, norm = block_average(
        place, norm, jnp.stack(pieces).astype(f32), block_states.astype(f32), average
    )
    updated, norm, ln_updated = flat_update(
        place,
        norm,
        0,
        jnp.stack(halves[0], axis=1).astype(f32) + 0.0 * norm[:1],
        states,
        ln_states=(ln_gradient, ln_master, ln_first, ln_second, ln_average),
    )
    updated, _, _ = flat_update(
        place,
        norm,
        half,
        jnp.stack(halves[1], axis=1).astype(f32) + 0.0 * norm[:1],
        states,
        updated,
    )
    return (average_new, *updated, *ln_updated)


def solution(mesh):
    placed = (
        P("dp", "row", "col"),
        P("dp", None, "col"),
        P(("row", "col"), None),
        P(("row", "col"), None),
        P(("row", "col"), None),
        P("row", "col"),
        P(None, "col"),
        P(None, "col"),
        P(None, "col"),
        P(None, "col"),
    )
    return jax.shard_map(
        shards,
        mesh=mesh,
        in_specs=placed,
        out_specs=(
            P("row", "col"),
            P(("row", "col"), None),
            P(("row", "col"), None),
            P(("row", "col"), None),
            P(None, "col"),
            P(None, "col"),
            P(None, "col"),
            P(None, "col"),
        ),
        check_vma=False,
    )
```

```python
import functools
import math

import jax
import jax.numpy as jnp
from jax import lax
from jax.experimental import pallas as pl
from jax.experimental.pallas import tpu as pltpu
from jax.sharding import PartitionSpec as P

D = 1024
FF = 4096
STEP = 20


beta_one = 0.9
beta_two = 0.95
learn_rate = 0.02
decay_rate = 0.1
epsilon = 1e-08
clip_rms = 1.0
ema_keep = 0.9


root_gain = 1.0 / math.sqrt(1.0 - beta_two**STEP)
step_gain = learn_rate / (1.0 - beta_one**STEP) / root_gain


def adam_step(gradient, clip_scale, first, second, master, decay_weight):
    clipped = clip_scale * gradient
    first_new = beta_one * first + (1.0 - beta_one) * clipped
    second_new = beta_two * second + (1.0 - beta_two) * clipped * clipped
    root = second_new * lax.rsqrt(second_new)
    step = step_gain * first_new / (root + epsilon / root_gain)
    master_new = (1.0 - learn_rate * decay_weight) * master - step
    return (master_new, first_new, second_new)


def clip_factor(norm_total):
    return jnp.minimum(1.0, clip_rms * math.sqrt(FF * D + 4 * D) / jnp.sqrt(norm_total))


def arrange(blocks, extra):
    groups, cols = lax.axis_size("dp"), lax.axis_size("col")
    _, rows, width = blocks.shape
    span = cols * rows

    def body(blocks_ref, extra_ref, *outs):
        outs[groups][...] = jnp.zeros_like(outs[groups])
        group, col = lax.axis_index("dp"), lax.axis_index("col")
        for s in range(groups):
            for k in range(cols):
                outs[s][k * rows : (k + 1) * rows] = blocks_ref[
                    (col ^ k) * groups + (group ^ s)
                ]
            outs[s][span:] = extra_ref[...]

    return pl.pallas_call(
        body,
        in_specs=[pl.BlockSpec(memory_space=pltpu.VMEM)] * 2,
        out_specs=[pl.BlockSpec(memory_space=pltpu.VMEM)] * (groups + 1),
        out_shape=[
            jax.ShapeDtypeStruct((span + extra.shape[0], width), blocks.dtype)
        ]
        * groups
        + [jax.ShapeDtypeStruct((8, 128), jnp.float32)],
        compiler_params=pltpu.CompilerParams(vmem_limit_bytes=16 * 2**20),
        name="arrange",
    )(blocks, extra)


def by_column(states, cols, after):
    rows, columns = states[0].shape
    width = columns // cols
    count = len(states)

    def body(*refs):
        for i in range(count):
            refs[count + 1][0, i] = refs[i][...]

    return pl.pallas_call(
        body,
        grid=(cols,),
        in_specs=[pl.BlockSpec((rows, width), lambda c: (0, c))] * count
        + [pl.BlockSpec(after.shape, lambda c: (0, 0))],
        out_specs=pl.BlockSpec((1, count, rows, width), lambda c: (c, 0, 0, 0)),
        out_shape=jax.ShapeDtypeStruct((cols, count, rows, width), states[0].dtype),
        compiler_params=pltpu.CompilerParams(vmem_limit_bytes=16 * 2**20),
        name="by_column",
    )(*(pltpu.with_memory_space_constraint(x, pltpu.HBM) for x in states), after)


def hand_on(norm):
    def body(norm_ref, out_ref):
        out_ref[...] = norm_ref[...]

    return pl.pallas_call(
        body,
        out_shape=jax.ShapeDtypeStruct(norm.shape, norm.dtype),
        cost_estimate=pl.CostEstimate(
            flops=0, bytes_accessed=60000000, transcendentals=0
        ),
        name="hand_on",
    )(norm)


def clip_of(norm_ref):
    rows = jnp.sum(norm_ref[...], axis=0, keepdims=True)
    return clip_factor(jnp.sum(rows, axis=1, keepdims=True))


def flat_update(place, norm, start, gradient, states, kept=(), ln_states=()):
    count, cols, rows, width = gradient.shape
    state = pl.BlockSpec(
        (rows, cols * width), lambda s, place: (place[0] ^ (start + s), 0)
    )
    whole = pl.BlockSpec(norm.shape, lambda s, place: (0, 0))
    ln = [pl.BlockSpec(x.shape, lambda s, place: (0, 0)) for x in ln_states]

    def body(place_ref, norm_ref, gradient_ref, *refs):
        refs = list(refs)
        take = lambda number: [refs.pop(0) for _ in range(number)]
        state_refs, _, ln_refs = take(3), take(len(kept)), take(len(ln))
        out_refs, passed_ref, ln_out_refs = take(3), take(1)[0], refs
        passed_ref[...] = norm_ref[...]
        clip_scale = clip_of(norm_ref)
        for column in range(cols):
            here = slice(column * width, (column + 1) * width)
            master, first, second = (ref[:, here] for ref in state_refs)
            results = adam_step(
                gradient_ref[0, place_ref[1] ^ column],
                clip_scale,
                first,
                second,
                master,
                decay_rate,
            )
            for out_ref, result in zip(out_refs, results):
                out_ref[:, here] = result

        if ln:

            @pl.when(pl.program_id(0) == 0)
            def _():
                ln_gradient, ln_master, ln_first, ln_second, ln_average = (
                    ref[...] for ref in ln_refs
                )
                results = adam_step(
                    ln_gradient, clip_scale, ln_first, ln_second, ln_master, 0.0
                )
                average = ema_keep * ln_average + (1.0 - ema_keep) * results[0]
                for out_ref, result in zip(ln_out_refs, (*results, average)):
                    out_ref[...] = result

    out = pl.pallas_call(
        body,
        grid_spec=pltpu.PrefetchScalarGridSpec(
            num_scalar_prefetch=1,
            grid=(count,),
            in_specs=[
                whole,
                pl.BlockSpec((1, cols, rows, width), lambda s, place: (s, 0, 0, 0)),
            ]
            + [state] * 3
            + [pl.BlockSpec(memory_space=pl.ANY)] * len(kept)
            + ln,
            out_specs=[state] * 3 + [whole] + ln[1:],
        ),
        out_shape=[
            jax.ShapeDtypeStruct(x.shape, x.dtype)
            for x in (*states, norm, *ln_states[1:])
        ],
        input_output_aliases={6 + i: i for i in range(len(kept))},
        compiler_params=pltpu.CompilerParams(vmem_limit_bytes=16 * 2**20),
        name="flat_update",
    )(place, norm, gradient, *states, *kept, *ln_states)
    return out[:3], out[3], out[4:]


def block_average(place, norm, gradient, states, average):
    groups, cols, rows, width = gradient.shape
    span = groups * rows

    def body(
        place_ref, norm_ref, gradient_ref, states_ref, average_ref, out_ref, passed_ref
    ):
        passed_ref[...] = norm_ref[...]
        clip_scale = clip_of(norm_ref)
        for group in range(groups):
            here = slice(group * rows, (group + 1) * rows)
            master, first, second = (states_ref[0, i, here] for i in range(3))
            master_new, _, _ = adam_step(
                gradient_ref[place_ref[0] ^ group, 0],
                clip_scale,
                first,
                second,
                master,
                decay_rate,
            )
            out_ref[here] = (
                ema_keep * average_ref[here] + (1.0 - ema_keep) * master_new
            )

    block = pl.BlockSpec((span, width), lambda c, place: (c, 0))
    return pl.pallas_call(
        body,
        grid_spec=pltpu.PrefetchScalarGridSpec(
            num_scalar_prefetch=1,
            grid=(cols,),
            in_specs=[
                pl.BlockSpec(norm.shape, lambda c, place: (0, 0)),
                pl.BlockSpec(
                    (groups, 1, rows, width),
                    lambda c, place: (0, place[1] ^ c, 0, 0),
                ),
                pl.BlockSpec((1, 3, span, width), lambda c, place: (c, 0, 0, 0)),
                block,
            ],
            out_specs=[block, pl.BlockSpec(norm.shape, lambda c, place: (0, 0))],
        ),
        out_shape=[
            jax.ShapeDtypeStruct(x.shape, x.dtype) for x in (average, norm)
        ],
        compiler_params=pltpu.CompilerParams(vmem_limit_bytes=16 * 2**20),
        name="block_average",
    )(place, norm, gradient, states, average)


def tree_sum(terms):
    while len(terms) > 1:
        terms = [a + b for a, b in zip(terms[::2], terms[1::2])]
    return terms[0]


def send(held, axis, s):
    if s == 0:
        return held
    size = lax.axis_size(axis)
    return lax.ppermute(held, axis, [(i, i ^ s) for i in range(size)])


def exchange(held, axis):
    return [send(held, axis, s) for s in range(lax.axis_size(axis))]


def shards(
    grad_blocks,
    ln_grads,
    master,
    first_moment,
    second_moment,
    average,
    ln_master,
    ln_first,
    ln_second,
    ln_average,
):
    groups, row_count, cols = (lax.axis_size(name) for name in ("dp", "row", "col"))
    place = jnp.stack([lax.axis_index("dp"), lax.axis_index("col")]).astype(jnp.int32)
    _, rows, width = grad_blocks.shape
    flat = rows // cols
    piece_rows = flat // groups
    f32, f16 = jnp.float32, jnp.float16
    states = (master, first_moment, second_moment)

    ln_rows = ln_grads.shape[1]
    *parts, after = arrange(
        grad_blocks.reshape(cols * groups, piece_rows, width),
        jnp.pad(ln_grads[0], ((0, -ln_rows % 16), (0, 0))),
    )
    parts = [send(part, "dp", s) for s, part in enumerate(parts)]

    block_states = lax.all_to_all(
        by_column(states, cols, after).astype(f16),
        "col",
        split_axis=0,
        concat_axis=0,
        tiled=True,
    )

    total = tree_sum([part.astype(f32) for part in parts])
    ln_gradient = total[cols * piece_rows :][:ln_rows]
    total = total[: cols * piece_rows].reshape(cols, piece_rows, width)
    norm = jnp.sum(total * total, axis=(0, 1)) + jnp.sum(
        ln_gradient * ln_gradient, axis=0
    ) / float(row_count * groups)
    norm = tree_sum(exchange(norm.reshape(1, width), "dp"))
    pieces = exchange(total.astype(f16), "dp")
    norm = lax.all_gather(hand_on(norm), ("row", "col"), tiled=True)

    half = groups // 2
    near = [send(jnp.stack([x[k] for x in pieces]), "col", k) for k in range(2)]
    halves = [
        [x[at] for x in near]
        + [
            send(jnp.stack([x[k] for x in pieces[at]]), "col", k)
            for k in range(2, cols)
        ]
        for at in (slice(0, half), slice(half, groups))
    ]
    average_new, norm = block_average(
        place, norm, jnp.stack(pieces).astype(f32), block_states.astype(f32), average
    )
    updated, norm, ln_updated = flat_update(
        place,
        norm,
        0,
        jnp.stack(halves[0], axis=1).astype(f32) + 0.0 * norm[:1],
        states,
        ln_states=(ln_gradient, ln_master, ln_first, ln_second, ln_average),
    )
    updated, _, _ = flat_update(
        place,
        norm,
        half,
        jnp.stack(halves[1], axis=1).astype(f32),
        states,
        updated,
    )
    return (average_new, *updated, *ln_updated)


def solution(mesh):
    placed = (
        P("dp", "row", "col"),
        P("dp", None, "col"),
        P(("row", "col"), None),
        P(("row", "col"), None),
        P(("row", "col"), None),
        P("row", "col"),
        P(None, "col"),
        P(None, "col"),
        P(None, "col"),
        P(None, "col"),
    )
    return jax.shard_map(
        shards,
        mesh=mesh,
        in_specs=placed,
        out_specs=(
            P("row", "col"),
            P(("row", "col"), None),
            P(("row", "col"), None),
            P(("row", "col"), None),
            P(None, "col"),
            P(None, "col"),
            P(None, "col"),
            P(None, "col"),
        ),
        check_vma=False,
    )
```

```python
import functools
import math

import jax
import jax.numpy as jnp
from jax import lax
from jax.experimental import pallas as pl
from jax.experimental.pallas import tpu as pltpu
from jax.sharding import PartitionSpec as P

D = 1024
FF = 4096
STEP = 20


beta_one = 0.9
beta_two = 0.95
learn_rate = 0.02
decay_rate = 0.1
epsilon = 1e-08
clip_rms = 1.0
ema_keep = 0.9


root_gain = 1.0 / math.sqrt(1.0 - beta_two**STEP)
step_gain = learn_rate / (1.0 - beta_one**STEP) / root_gain


def adam_step(gradient, clip_scale, first, second, master, decay_weight):
    clipped = clip_scale * gradient
    first_new = beta_one * first + (1.0 - beta_one) * clipped
    second_new = beta_two * second + (1.0 - beta_two) * clipped * clipped
    root = second_new * lax.rsqrt(second_new)
    step = step_gain * first_new / (root + epsilon / root_gain)
    master_new = (1.0 - learn_rate * decay_weight) * master - step
    return (master_new, first_new, second_new)


def clip_factor(norm_total):
    return jnp.minimum(1.0, clip_rms * math.sqrt(FF * D + 4 * D) / jnp.sqrt(norm_total))


def arrange(blocks, extra):
    groups, cols = lax.axis_size("dp"), lax.axis_size("col")
    _, rows, width = blocks.shape
    span = cols * rows
    tail = -(-extra.shape[0] // 16) * 16

    def body(blocks_ref, extra_ref, *outs):
        outs[groups][...] = jnp.zeros_like(outs[groups])
        group, col = lax.axis_index("dp"), lax.axis_index("col")
        values = extra_ref[...].astype(jnp.float32)
        row = lax.broadcasted_iota(jnp.int32, (tail, width), 0)
        padded = jnp.zeros((tail, width), jnp.float32)
        for at in range(values.shape[0]):
            padded = jnp.where(row == at, values[at : at + 1], padded)
        padded = padded.astype(blocks.dtype)
        for s in range(groups):
            for k in range(cols):
                outs[s][k * rows : (k + 1) * rows] = blocks_ref[
                    (col ^ k) * groups + (group ^ s)
                ]
            outs[s][span:] = padded

    return pl.pallas_call(
        body,
        in_specs=[pl.BlockSpec(memory_space=pltpu.VMEM)] * 2,
        out_specs=[pl.BlockSpec(memory_space=pltpu.VMEM)] * (groups + 1),
        out_shape=[
            jax.ShapeDtypeStruct((span + tail, width), blocks.dtype)
        ]
        * groups
        + [jax.ShapeDtypeStruct((8, 128), jnp.float32)],
        compiler_params=pltpu.CompilerParams(vmem_limit_bytes=16 * 2**20),
        name="arrange",
    )(blocks, extra)


def by_column(states, cols, after):
    rows, columns = states[0].shape
    width = columns // cols
    count = len(states)

    def body(*refs):
        for i in range(count):
            refs[count + 1][0, i] = refs[i][...]

    return pl.pallas_call(
        body,
        grid=(cols,),
        in_specs=[pl.BlockSpec((rows, width), lambda c: (0, c))] * count
        + [pl.BlockSpec(after.shape, lambda c: (0, 0))],
        out_specs=pl.BlockSpec((1, count, rows, width), lambda c: (c, 0, 0, 0)),
        out_shape=jax.ShapeDtypeStruct((cols, count, rows, width), states[0].dtype),
        compiler_params=pltpu.CompilerParams(vmem_limit_bytes=16 * 2**20),
        name="by_column",
    )(*(pltpu.with_memory_space_constraint(x, pltpu.HBM) for x in states), after)


def hand_on(norm):
    def body(norm_ref, out_ref):
        out_ref[...] = norm_ref[...]

    return pl.pallas_call(
        body,
        out_shape=jax.ShapeDtypeStruct(norm.shape, norm.dtype),
        cost_estimate=pl.CostEstimate(
            flops=0, bytes_accessed=60000000, transcendentals=0
        ),
        name="hand_on",
    )(norm)


def clip_of(norm_ref):
    rows = jnp.sum(norm_ref[...], axis=0, keepdims=True)
    return clip_factor(jnp.sum(rows, axis=1, keepdims=True))


def flat_update(place, norm, start, gradient, states, kept=(), ln_states=()):
    count, cols, rows, width = gradient.shape
    state = pl.BlockSpec(
        (rows, cols * width), lambda s, place: (place[0] ^ (start + s), 0)
    )
    whole = pl.BlockSpec(norm.shape, lambda s, place: (0, 0))
    ln = [pl.BlockSpec(x.shape, lambda s, place: (0, 0)) for x in ln_states]

    def body(place_ref, norm_ref, gradient_ref, *refs):
        refs = list(refs)
        take = lambda number: [refs.pop(0) for _ in range(number)]
        state_refs, _, ln_refs = take(3), take(len(kept)), take(len(ln))
        out_refs, passed_ref, ln_out_refs = take(3), take(1)[0], refs
        passed_ref[...] = norm_ref[...]
        clip_scale = clip_of(norm_ref)
        for column in range(cols):
            here = slice(column * width, (column + 1) * width)
            master, first, second = (ref[:, here] for ref in state_refs)
            results = adam_step(
                gradient_ref[0, place_ref[1] ^ column],
                clip_scale,
                first,
                second,
                master,
                decay_rate,
            )
            for out_ref, result in zip(out_refs, results):
                out_ref[:, here] = result

        if ln:

            @pl.when(pl.program_id(0) == 0)
            def _():
                ln_gradient, ln_master, ln_first, ln_second, ln_average = (
                    ref[...] for ref in ln_refs
                )
                results = adam_step(
                    ln_gradient, clip_scale, ln_first, ln_second, ln_master, 0.0
                )
                average = ema_keep * ln_average + (1.0 - ema_keep) * results[0]
                for out_ref, result in zip(ln_out_refs, (*results, average)):
                    out_ref[...] = result

    out = pl.pallas_call(
        body,
        grid_spec=pltpu.PrefetchScalarGridSpec(
            num_scalar_prefetch=1,
            grid=(count,),
            in_specs=[
                whole,
                pl.BlockSpec((1, cols, rows, width), lambda s, place: (s, 0, 0, 0)),
            ]
            + [state] * 3
            + [pl.BlockSpec(memory_space=pl.ANY)] * len(kept)
            + ln,
            out_specs=[state] * 3 + [whole] + ln[1:],
        ),
        out_shape=[
            jax.ShapeDtypeStruct(x.shape, x.dtype)
            for x in (*states, norm, *ln_states[1:])
        ],
        input_output_aliases={6 + i: i for i in range(len(kept))},
        compiler_params=pltpu.CompilerParams(vmem_limit_bytes=16 * 2**20),
        name="flat_update",
    )(place, norm, gradient, *states, *kept, *ln_states)
    return out[:3], out[3], out[4:]


def block_average(place, norm, gradient, states, average):
    groups, cols, rows, width = gradient.shape
    span = groups * rows

    def body(
        place_ref, norm_ref, gradient_ref, states_ref, average_ref, out_ref, passed_ref
    ):
        passed_ref[...] = norm_ref[...]
        clip_scale = clip_of(norm_ref)
        for group in range(groups):
            here = slice(group * rows, (group + 1) * rows)
            master, first, second = (states_ref[0, i, here] for i in range(3))
            master_new, _, _ = adam_step(
                gradient_ref[place_ref[0] ^ group, 0],
                clip_scale,
                first,
                second,
                master,
                decay_rate,
            )
            out_ref[here] = (
                ema_keep * average_ref[here] + (1.0 - ema_keep) * master_new
            )

    block = pl.BlockSpec((span, width), lambda c, place: (c, 0))
    return pl.pallas_call(
        body,
        grid_spec=pltpu.PrefetchScalarGridSpec(
            num_scalar_prefetch=1,
            grid=(cols,),
            in_specs=[
                pl.BlockSpec(norm.shape, lambda c, place: (0, 0)),
                pl.BlockSpec(
                    (groups, 1, rows, width),
                    lambda c, place: (0, place[1] ^ c, 0, 0),
                ),
                pl.BlockSpec((1, 3, span, width), lambda c, place: (c, 0, 0, 0)),
                block,
            ],
            out_specs=[block, pl.BlockSpec(norm.shape, lambda c, place: (0, 0))],
        ),
        out_shape=[
            jax.ShapeDtypeStruct(x.shape, x.dtype) for x in (average, norm)
        ],
        compiler_params=pltpu.CompilerParams(vmem_limit_bytes=16 * 2**20),
        name="block_average",
    )(place, norm, gradient, states, average)


def tree_sum(terms):
    while len(terms) > 1:
        terms = [a + b for a, b in zip(terms[::2], terms[1::2])]
    return terms[0]


def send(held, axis, s):
    if s == 0:
        return held
    size = lax.axis_size(axis)
    return lax.ppermute(held, axis, [(i, i ^ s) for i in range(size)])


def exchange(held, axis):
    return [send(held, axis, s) for s in range(lax.axis_size(axis))]


def shards(
    grad_blocks,
    ln_grads,
    master,
    first_moment,
    second_moment,
    average,
    ln_master,
    ln_first,
    ln_second,
    ln_average,
):
    groups, row_count, cols = (lax.axis_size(name) for name in ("dp", "row", "col"))
    place = jnp.stack([lax.axis_index("dp"), lax.axis_index("col")]).astype(jnp.int32)
    _, rows, width = grad_blocks.shape
    flat = rows // cols
    piece_rows = flat // groups
    f32, f16 = jnp.float32, jnp.float16
    states = (master, first_moment, second_moment)

    ln_rows = ln_grads.shape[1]
    *parts, after = arrange(
        grad_blocks.reshape(cols * groups, piece_rows, width),
        ln_grads[0],
    )
    parts = [send(part, "dp", s) for s, part in enumerate(parts)]

    block_states = lax.all_to_all(
        by_column(states, cols, after).astype(f16),
        "col",
        split_axis=0,
        concat_axis=0,
        tiled=True,
    )

    total = tree_sum([part.astype(f32) for part in parts])
    ln_gradient = total[cols * piece_rows :][:ln_rows]
    total = total[: cols * piece_rows].reshape(cols, piece_rows, width)
    norm = jnp.sum(total * total, axis=(0, 1)) + jnp.sum(
        ln_gradient * ln_gradient, axis=0
    ) / float(row_count * groups)
    norm = tree_sum(exchange(norm.reshape(1, width), "dp"))
    pieces = exchange(total.astype(f16), "dp")
    norm = lax.all_gather(hand_on(norm), ("row", "col"), tiled=True)

    half = groups // 2
    near = [send(jnp.stack([x[k] for x in pieces]), "col", k) for k in range(2)]
    halves = [
        [x[at] for x in near]
        + [
            send(jnp.stack([x[k] for x in pieces[at]]), "col", k)
            for k in range(2, cols)
        ]
        for at in (slice(0, half), slice(half, groups))
    ]
    average_new, norm = block_average(
        place, norm, jnp.stack(pieces).astype(f32), block_states.astype(f32), average
    )
    updated, norm, ln_updated = flat_update(
        place,
        norm,
        0,
        jnp.stack(halves[0], axis=1).astype(f32) + 0.0 * norm[:1],
        states,
        ln_states=(ln_gradient, ln_master, ln_first, ln_second, ln_average),
    )
    updated, _, _ = flat_update(
        place,
        norm,
        half,
        jnp.stack(halves[1], axis=1).astype(f32),
        states,
        updated,
    )
    return (average_new, *updated, *ln_updated)


def solution(mesh):
    placed = (
        P("dp", "row", "col"),
        P("dp", None, "col"),
        P(("row", "col"), None),
        P(("row", "col"), None),
        P(("row", "col"), None),
        P("row", "col"),
        P(None, "col"),
        P(None, "col"),
        P(None, "col"),
        P(None, "col"),
    )
    return jax.shard_map(
        shards,
        mesh=mesh,
        in_specs=placed,
        out_specs=(
            P("row", "col"),
            P(("row", "col"), None),
            P(("row", "col"), None),
            P(("row", "col"), None),
            P(None, "col"),
            P(None, "col"),
            P(None, "col"),
            P(None, "col"),
        ),
        check_vma=False,
    )
```

```python
import functools
import math

import jax
import jax.numpy as jnp
from jax import lax
from jax.experimental import pallas as pl
from jax.experimental.pallas import tpu as pltpu
from jax.sharding import PartitionSpec as P

D = 1024
FF = 4096
STEP = 20


beta_one = 0.9
beta_two = 0.95
learn_rate = 0.02
decay_rate = 0.1
epsilon = 1e-08
clip_rms = 1.0
ema_keep = 0.9


root_gain = 1.0 / math.sqrt(1.0 - beta_two**STEP)
step_gain = learn_rate / (1.0 - beta_one**STEP) / root_gain


def adam_step(gradient, clip_scale, first, second, master, decay_weight):
    clipped = clip_scale * gradient
    first_new = beta_one * first + (1.0 - beta_one) * clipped
    second_new = beta_two * second + (1.0 - beta_two) * clipped * clipped
    root = second_new * lax.rsqrt(second_new)
    step = step_gain * first_new / (root + epsilon / root_gain)
    master_new = (1.0 - learn_rate * decay_weight) * master - step
    return (master_new, first_new, second_new)


def clip_factor(norm_total):
    return jnp.minimum(1.0, clip_rms * math.sqrt(FF * D + 4 * D) / jnp.sqrt(norm_total))


def arrange(blocks, extra):
    groups, cols = lax.axis_size("dp"), lax.axis_size("col")
    _, rows, width = blocks.shape
    span = cols * rows
    tail = -(-extra.shape[0] // 16) * 16

    def body(blocks_ref, extra_ref, *outs):
        outs[groups][...] = jnp.zeros_like(outs[groups])
        group, col = lax.axis_index("dp"), lax.axis_index("col")
        values = extra_ref[...].astype(jnp.float32)
        row = lax.broadcasted_iota(jnp.int32, (tail, width), 0)
        padded = jnp.zeros((tail, width), jnp.float32)
        for at in range(values.shape[0]):
            padded = jnp.where(row == at, values[at : at + 1], padded)
        padded = padded.astype(blocks.dtype)
        for s in range(groups):
            for k in range(cols):
                outs[s][k * rows : (k + 1) * rows] = blocks_ref[
                    (col ^ k) * groups + (group ^ s)
                ]
            outs[s][span:] = padded

    return pl.pallas_call(
        body,
        in_specs=[pl.BlockSpec(memory_space=pltpu.VMEM)] * 2,
        out_specs=[pl.BlockSpec(memory_space=pltpu.VMEM)] * (groups + 1),
        out_shape=[
            jax.ShapeDtypeStruct((span + tail, width), blocks.dtype)
        ]
        * groups
        + [jax.ShapeDtypeStruct((8, 128), jnp.float32)],
        compiler_params=pltpu.CompilerParams(vmem_limit_bytes=16 * 2**20),
        name="arrange",
    )(blocks, extra)


def by_column(states, cols, after):
    rows, columns = states[0].shape
    width = columns // cols
    count = len(states)

    def body(*refs):
        for i in range(count):
            refs[count + 1][0, i] = refs[i][...]

    return pl.pallas_call(
        body,
        grid=(cols,),
        in_specs=[pl.BlockSpec((rows, width), lambda c: (0, c))] * count
        + [pl.BlockSpec(after.shape, lambda c: (0, 0))],
        out_specs=pl.BlockSpec((1, count, rows, width), lambda c: (c, 0, 0, 0)),
        out_shape=jax.ShapeDtypeStruct((cols, count, rows, width), states[0].dtype),
        compiler_params=pltpu.CompilerParams(vmem_limit_bytes=16 * 2**20),
        name="by_column",
    )(*(pltpu.with_memory_space_constraint(x, pltpu.HBM) for x in states), after)


def hand_on(norm):
    def body(norm_ref, out_ref):
        out_ref[...] = norm_ref[...]

    return pl.pallas_call(
        body,
        out_shape=jax.ShapeDtypeStruct(norm.shape, norm.dtype),
        cost_estimate=pl.CostEstimate(
            flops=0, bytes_accessed=60000000, transcendentals=0
        ),
        name="hand_on",
    )(norm)


def clip_of(norm_ref):
    rows = jnp.sum(norm_ref[...], axis=0, keepdims=True)
    return clip_factor(jnp.sum(rows, axis=1, keepdims=True))


def flat_update(place, norm, start, gradient, states, kept=(), ln_states=()):
    count, cols, rows, width = gradient.shape
    state = pl.BlockSpec(
        (rows, cols * width), lambda s, place: (place[0] ^ (start + s), 0)
    )
    whole = pl.BlockSpec(norm.shape, lambda s, place: (0, 0))
    ln = [pl.BlockSpec(x.shape, lambda s, place: (0, 0)) for x in ln_states]

    def body(place_ref, norm_ref, gradient_ref, *refs):
        refs = list(refs)
        take = lambda number: [refs.pop(0) for _ in range(number)]
        state_refs, _, ln_refs = take(3), take(len(kept)), take(len(ln))
        out_refs, passed_ref, ln_out_refs = take(3), take(1)[0], refs
        passed_ref[...] = norm_ref[...]
        clip_scale = clip_of(norm_ref)
        for column in range(cols):
            here = slice(column * width, (column + 1) * width)
            master, first, second = (ref[:, here] for ref in state_refs)
            results = adam_step(
                gradient_ref[0, place_ref[1] ^ column],
                clip_scale,
                first,
                second,
                master,
                decay_rate,
            )
            for out_ref, result in zip(out_refs, results):
                out_ref[:, here] = result

        if ln:

            @pl.when(pl.program_id(0) == 0)
            def _():
                ln_gradient, ln_master, ln_first, ln_second, ln_average = (
                    ref[...] for ref in ln_refs
                )
                results = adam_step(
                    ln_gradient, clip_scale, ln_first, ln_second, ln_master, 0.0
                )
                average = ema_keep * ln_average + (1.0 - ema_keep) * results[0]
                for out_ref, result in zip(ln_out_refs, (*results, average)):
                    out_ref[...] = result

    out = pl.pallas_call(
        body,
        grid_spec=pltpu.PrefetchScalarGridSpec(
            num_scalar_prefetch=1,
            grid=(count,),
            in_specs=[
                whole,
                pl.BlockSpec((1, cols, rows, width), lambda s, place: (s, 0, 0, 0)),
            ]
            + [state] * 3
            + [pl.BlockSpec(memory_space=pl.ANY)] * len(kept)
            + ln,
            out_specs=[state] * 3 + [whole] + ln[1:],
        ),
        out_shape=[
            jax.ShapeDtypeStruct(x.shape, x.dtype)
            for x in (*states, norm, *ln_states[1:])
        ],
        input_output_aliases={6 + i: i for i in range(len(kept))},
        compiler_params=pltpu.CompilerParams(vmem_limit_bytes=16 * 2**20),
        name="flat_update",
    )(place, norm, gradient, *states, *kept, *ln_states)
    return out[:3], out[3], out[4:]


def block_average(place, norm, gradient, states, average):
    groups, cols, rows, width = gradient.shape
    span = groups * rows
    pair = 2

    def body(
        place_ref, norm_ref, gradient_ref, states_ref, average_ref, out_ref, passed_ref
    ):
        passed_ref[...] = norm_ref[...]
        clip_scale = clip_of(norm_ref)
        for own in range(pair):
            other = (place_ref[1] ^ own) & (pair - 1)
            for group in range(groups):
                rows_here = slice(group * rows, (group + 1) * rows)
                here = slice(own * span + group * rows, own * span + (group + 1) * rows)
                master, first, second = (
                    states_ref[own, i, rows_here] for i in range(3)
                )
                master_new, _, _ = adam_step(
                    gradient_ref[place_ref[0] ^ group, other],
                    clip_scale,
                    first,
                    second,
                    master,
                    decay_rate,
                )
                out_ref[here] = (
                    ema_keep * average_ref[here] + (1.0 - ema_keep) * master_new
                )

    block = pl.BlockSpec((pair * span, width), lambda c, place: (c, 0))
    return pl.pallas_call(
        body,
        grid_spec=pltpu.PrefetchScalarGridSpec(
            num_scalar_prefetch=1,
            grid=(cols // pair,),
            in_specs=[
                pl.BlockSpec(norm.shape, lambda c, place: (0, 0)),
                pl.BlockSpec(
                    (groups, pair, rows, width),
                    lambda c, place: (0, (place[1] >> 1) ^ c, 0, 0),
                ),
                pl.BlockSpec((pair, 3, span, width), lambda c, place: (c, 0, 0, 0)),
                block,
            ],
            out_specs=[block, pl.BlockSpec(norm.shape, lambda c, place: (0, 0))],
        ),
        out_shape=[
            jax.ShapeDtypeStruct(x.shape, x.dtype) for x in (average, norm)
        ],
        compiler_params=pltpu.CompilerParams(vmem_limit_bytes=24 * 2**20),
        name="block_average",
    )(place, norm, gradient, states, average)


def tree_sum(terms):
    while len(terms) > 1:
        terms = [a + b for a, b in zip(terms[::2], terms[1::2])]
    return terms[0]


def send(held, axis, s):
    if s == 0:
        return held
    size = lax.axis_size(axis)
    return lax.ppermute(held, axis, [(i, i ^ s) for i in range(size)])


def exchange(held, axis):
    return [send(held, axis, s) for s in range(lax.axis_size(axis))]


def shards(
    grad_blocks,
    ln_grads,
    master,
    first_moment,
    second_moment,
    average,
    ln_master,
    ln_first,
    ln_second,
    ln_average,
):
    groups, row_count, cols = (lax.axis_size(name) for name in ("dp", "row", "col"))
    place = jnp.stack([lax.axis_index("dp"), lax.axis_index("col")]).astype(jnp.int32)
    _, rows, width = grad_blocks.shape
    flat = rows // cols
    piece_rows = flat // groups
    f32, f16 = jnp.float32, jnp.float16
    states = (master, first_moment, second_moment)

    ln_rows = ln_grads.shape[1]
    *parts, after = arrange(
        grad_blocks.reshape(cols * groups, piece_rows, width),
        ln_grads[0],
    )
    parts = [send(part, "dp", s) for s, part in enumerate(parts)]

    block_states = lax.all_to_all(
        by_column(states, cols, after).astype(f16),
        "col",
        split_axis=0,
        concat_axis=0,
        tiled=True,
    )

    total = tree_sum([part.astype(f32) for part in parts])
    ln_gradient = total[cols * piece_rows :][:ln_rows]
    total = total[: cols * piece_rows].reshape(cols, piece_rows, width)
    norm = jnp.sum(total * total, axis=(0, 1)) + jnp.sum(
        ln_gradient * ln_gradient, axis=0
    ) / float(row_count * groups)
    norm = tree_sum(exchange(norm.reshape(1, width), "dp"))
    pieces = exchange(total.astype(f16), "dp")
    norm = lax.all_gather(hand_on(norm), ("row", "col"), tiled=True)

    half = groups // 2
    near = [send(jnp.stack([x[k] for x in pieces]), "col", k) for k in range(2)]
    halves = [
        [x[at] for x in near]
        + [
            send(jnp.stack([x[k] for x in pieces[at]]), "col", k)
            for k in range(2, cols)
        ]
        for at in (slice(0, half), slice(half, groups))
    ]
    average_new, norm = block_average(
        place, norm, jnp.stack(pieces).astype(f32), block_states.astype(f32), average
    )
    updated, norm, ln_updated = flat_update(
        place,
        norm,
        0,
        jnp.stack(halves[0], axis=1).astype(f32) + 0.0 * norm[:1],
        states,
        ln_states=(ln_gradient, ln_master, ln_first, ln_second, ln_average),
    )
    updated, _, _ = flat_update(
        place,
        norm,
        half,
        jnp.stack(halves[1], axis=1).astype(f32),
        states,
        updated,
    )
    return (average_new, *updated, *ln_updated)


def solution(mesh):
    placed = (
        P("dp", "row", "col"),
        P("dp", None, "col"),
        P(("row", "col"), None),
        P(("row", "col"), None),
        P(("row", "col"), None),
        P("row", "col"),
        P(None, "col"),
        P(None, "col"),
        P(None, "col"),
        P(None, "col"),
    )
    return jax.shard_map(
        shards,
        mesh=mesh,
        in_specs=placed,
        out_specs=(
            P("row", "col"),
            P(("row", "col"), None),
            P(("row", "col"), None),
            P(("row", "col"), None),
            P(None, "col"),
            P(None, "col"),
            P(None, "col"),
            P(None, "col"),
        ),
        check_vma=False,
    )
```

```python
import functools
import math

import jax
import jax.numpy as jnp
from jax import lax
from jax.experimental import pallas as pl
from jax.experimental.pallas import tpu as pltpu
from jax.sharding import PartitionSpec as P

D = 1024
FF = 4096
STEP = 20


beta_one = 0.9
beta_two = 0.95
learn_rate = 0.02
decay_rate = 0.1
epsilon = 1e-08
clip_rms = 1.0
ema_keep = 0.9


root_gain = 1.0 / math.sqrt(1.0 - beta_two**STEP)
step_gain = learn_rate / (1.0 - beta_one**STEP) / root_gain


def adam_step(gradient, clip_scale, first, second, master, decay_weight):
    clipped = clip_scale * gradient
    first_new = beta_one * first + (1.0 - beta_one) * clipped
    second_new = beta_two * second + (1.0 - beta_two) * clipped * clipped
    root = second_new * lax.rsqrt(second_new)
    step = step_gain * first_new / (root + epsilon / root_gain)
    master_new = (1.0 - learn_rate * decay_weight) * master - step
    return (master_new, first_new, second_new)


def clip_factor(norm_total):
    return jnp.minimum(1.0, clip_rms * math.sqrt(FF * D + 4 * D) / jnp.sqrt(norm_total))


def arrange(blocks, extra):
    groups, cols = lax.axis_size("dp"), lax.axis_size("col")
    _, rows, width = blocks.shape
    span = cols * rows
    tail = -(-extra.shape[0] // 16) * 16

    def body(blocks_ref, extra_ref, *outs):
        outs[groups][...] = jnp.zeros_like(outs[groups])
        group, col = lax.axis_index("dp"), lax.axis_index("col")
        values = extra_ref[...].astype(jnp.float32)
        row = lax.broadcasted_iota(jnp.int32, (tail, width), 0)
        padded = jnp.zeros((tail, width), jnp.float32)
        for at in range(values.shape[0]):
            padded = jnp.where(row == at, values[at : at + 1], padded)
        padded = padded.astype(blocks.dtype)
        for s in range(groups):
            for k in range(cols):
                outs[s][k * rows : (k + 1) * rows] = blocks_ref[
                    (col ^ k) * groups + (group ^ s)
                ]
            outs[s][span:] = padded

    return pl.pallas_call(
        body,
        in_specs=[pl.BlockSpec(memory_space=pltpu.VMEM)] * 2,
        out_specs=[pl.BlockSpec(memory_space=pltpu.VMEM)] * (groups + 1),
        out_shape=[
            jax.ShapeDtypeStruct((span + tail, width), blocks.dtype)
        ]
        * groups
        + [jax.ShapeDtypeStruct((8, 128), jnp.float32)],
        compiler_params=pltpu.CompilerParams(vmem_limit_bytes=16 * 2**20),
        name="arrange",
    )(blocks, extra)


def by_column(states, cols, after):
    rows, columns = states[0].shape
    width = columns // cols
    count = len(states)

    def body(*refs):
        for i in range(count):
            for j in range(2):
                refs[count + 1][j, i] = refs[i][:, j * width : (j + 1) * width]

    return pl.pallas_call(
        body,
        grid=(cols // 2,),
        in_specs=[pl.BlockSpec((rows, 2 * width), lambda c: (0, c))] * count
        + [pl.BlockSpec(after.shape, lambda c: (0, 0))],
        out_specs=pl.BlockSpec((2, count, rows, width), lambda c: (c, 0, 0, 0)),
        out_shape=jax.ShapeDtypeStruct((cols, count, rows, width), states[0].dtype),
        compiler_params=pltpu.CompilerParams(vmem_limit_bytes=16 * 2**20),
        name="by_column",
    )(*(pltpu.with_memory_space_constraint(x, pltpu.HBM) for x in states), after)


def hand_on(norm):
    def body(norm_ref, out_ref):
        out_ref[...] = norm_ref[...]

    return pl.pallas_call(
        body,
        out_shape=jax.ShapeDtypeStruct(norm.shape, norm.dtype),
        cost_estimate=pl.CostEstimate(
            flops=0, bytes_accessed=60000000, transcendentals=0
        ),
        name="hand_on",
    )(norm)


def clip_of(norm_ref):
    rows = jnp.sum(norm_ref[...], axis=0, keepdims=True)
    return clip_factor(jnp.sum(rows, axis=1, keepdims=True))


def flat_update(place, norm, start, gradient, states, kept=(), ln_states=()):
    count, cols, rows, width = gradient.shape
    state = pl.BlockSpec(
        (rows, cols * width), lambda s, place: (place[0] ^ (start + s), 0)
    )
    whole = pl.BlockSpec(norm.shape, lambda s, place: (0, 0))
    ln = [pl.BlockSpec(x.shape, lambda s, place: (0, 0)) for x in ln_states]

    def body(place_ref, norm_ref, gradient_ref, *refs):
        refs = list(refs)
        take = lambda number: [refs.pop(0) for _ in range(number)]
        state_refs, _, ln_refs = take(3), take(len(kept)), take(len(ln))
        out_refs, passed_ref, ln_out_refs = take(3), take(1)[0], refs
        passed_ref[...] = norm_ref[...]
        clip_scale = clip_of(norm_ref)
        for column in range(cols):
            here = slice(column * width, (column + 1) * width)
            master, first, second = (ref[:, here] for ref in state_refs)
            results = adam_step(
                gradient_ref[0, place_ref[1] ^ column],
                clip_scale,
                first,
                second,
                master,
                decay_rate,
            )
            for out_ref, result in zip(out_refs, results):
                out_ref[:, here] = result

        if ln:

            @pl.when(pl.program_id(0) == 0)
            def _():
                ln_gradient, ln_master, ln_first, ln_second, ln_average = (
                    ref[...] for ref in ln_refs
                )
                results = adam_step(
                    ln_gradient, clip_scale, ln_first, ln_second, ln_master, 0.0
                )
                average = ema_keep * ln_average + (1.0 - ema_keep) * results[0]
                for out_ref, result in zip(ln_out_refs, (*results, average)):
                    out_ref[...] = result

    out = pl.pallas_call(
        body,
        grid_spec=pltpu.PrefetchScalarGridSpec(
            num_scalar_prefetch=1,
            grid=(count,),
            in_specs=[
                whole,
                pl.BlockSpec((1, cols, rows, width), lambda s, place: (s, 0, 0, 0)),
            ]
            + [state] * 3
            + [pl.BlockSpec(memory_space=pl.ANY)] * len(kept)
            + ln,
            out_specs=[state] * 3 + [whole] + ln[1:],
        ),
        out_shape=[
            jax.ShapeDtypeStruct(x.shape, x.dtype)
            for x in (*states, norm, *ln_states[1:])
        ],
        input_output_aliases={6 + i: i for i in range(len(kept))},
        compiler_params=pltpu.CompilerParams(vmem_limit_bytes=16 * 2**20),
        name="flat_update",
    )(place, norm, gradient, *states, *kept, *ln_states)
    return out[:3], out[3], out[4:]


def block_average(place, norm, gradient, states, average):
    groups, cols, rows, width = gradient.shape
    span = groups * rows
    pair = 2

    def body(
        place_ref, norm_ref, gradient_ref, states_ref, average_ref, out_ref, passed_ref
    ):
        passed_ref[...] = norm_ref[...]
        clip_scale = clip_of(norm_ref)
        for own in range(pair):
            other = (place_ref[1] ^ own) & (pair - 1)
            for group in range(groups):
                rows_here = slice(group * rows, (group + 1) * rows)
                here = slice(own * span + group * rows, own * span + (group + 1) * rows)
                master, first, second = (
                    states_ref[own, i, rows_here] for i in range(3)
                )
                master_new, _, _ = adam_step(
                    gradient_ref[place_ref[0] ^ group, other],
                    clip_scale,
                    first,
                    second,
                    master,
                    decay_rate,
                )
                out_ref[here] = (
                    ema_keep * average_ref[here] + (1.0 - ema_keep) * master_new
                )

    block = pl.BlockSpec((pair * span, width), lambda c, place: (c, 0))
    return pl.pallas_call(
        body,
        grid_spec=pltpu.PrefetchScalarGridSpec(
            num_scalar_prefetch=1,
            grid=(cols // pair,),
            in_specs=[
                pl.BlockSpec(norm.shape, lambda c, place: (0, 0)),
                pl.BlockSpec(
                    (groups, pair, rows, width),
                    lambda c, place: (0, (place[1] >> 1) ^ c, 0, 0),
                ),
                pl.BlockSpec((pair, 3, span, width), lambda c, place: (c, 0, 0, 0)),
                block,
            ],
            out_specs=[block, pl.BlockSpec(norm.shape, lambda c, place: (0, 0))],
        ),
        out_shape=[
            jax.ShapeDtypeStruct(x.shape, x.dtype) for x in (average, norm)
        ],
        compiler_params=pltpu.CompilerParams(vmem_limit_bytes=24 * 2**20),
        name="block_average",
    )(place, norm, gradient, states, average)


def tree_sum(terms):
    while len(terms) > 1:
        terms = [a + b for a, b in zip(terms[::2], terms[1::2])]
    return terms[0]


def send(held, axis, s):
    if s == 0:
        return held
    size = lax.axis_size(axis)
    return lax.ppermute(held, axis, [(i, i ^ s) for i in range(size)])


def exchange(held, axis):
    return [send(held, axis, s) for s in range(lax.axis_size(axis))]


def shards(
    grad_blocks,
    ln_grads,
    master,
    first_moment,
    second_moment,
    average,
    ln_master,
    ln_first,
    ln_second,
    ln_average,
):
    groups, row_count, cols = (lax.axis_size(name) for name in ("dp", "row", "col"))
    place = jnp.stack([lax.axis_index("dp"), lax.axis_index("col")]).astype(jnp.int32)
    _, rows, width = grad_blocks.shape
    flat = rows // cols
    piece_rows = flat // groups
    f32, f16 = jnp.float32, jnp.float16
    states = (master, first_moment, second_moment)

    ln_rows = ln_grads.shape[1]
    *parts, after = arrange(
        grad_blocks.reshape(cols * groups, piece_rows, width),
        ln_grads[0],
    )
    parts = [send(part, "dp", s) for s, part in enumerate(parts)]

    block_states = lax.all_to_all(
        by_column(states, cols, after).astype(f16),
        "col",
        split_axis=0,
        concat_axis=0,
        tiled=True,
    )

    total = tree_sum([part.astype(f32) for part in parts])
    ln_gradient = total[cols * piece_rows :][:ln_rows]
    total = total[: cols * piece_rows].reshape(cols, piece_rows, width)
    norm = jnp.sum(total * total, axis=(0, 1)) + jnp.sum(
        ln_gradient * ln_gradient, axis=0
    ) / float(row_count * groups)
    norm = tree_sum(exchange(norm.reshape(1, width), "dp"))
    pieces = exchange(total.astype(f16), "dp")
    norm = lax.all_gather(hand_on(norm), ("row", "col"), tiled=True)

    half = groups // 2
    near = [send(jnp.stack([x[k] for x in pieces]), "col", k) for k in range(2)]
    halves = [
        [x[at] for x in near]
        + [
            send(jnp.stack([x[k] for x in pieces[at]]), "col", k)
            for k in range(2, cols)
        ]
        for at in (slice(0, half), slice(half, groups))
    ]
    average_new, norm = block_average(
        place, norm, jnp.stack(pieces).astype(f32), block_states.astype(f32), average
    )
    updated, norm, ln_updated = flat_update(
        place,
        norm,
        0,
        jnp.stack(halves[0], axis=1).astype(f32) + 0.0 * norm[:1],
        states,
        ln_states=(ln_gradient, ln_master, ln_first, ln_second, ln_average),
    )
    updated, _, _ = flat_update(
        place,
        norm,
        half,
        jnp.stack(halves[1], axis=1).astype(f32),
        states,
        updated,
    )
    return (average_new, *updated, *ln_updated)


def solution(mesh):
    placed = (
        P("dp", "row", "col"),
        P("dp", None, "col"),
        P(("row", "col"), None),
        P(("row", "col"), None),
        P(("row", "col"), None),
        P("row", "col"),
        P(None, "col"),
        P(None, "col"),
        P(None, "col"),
        P(None, "col"),
    )
    return jax.shard_map(
        shards,
        mesh=mesh,
        in_specs=placed,
        out_specs=(
            P("row", "col"),
            P(("row", "col"), None),
            P(("row", "col"), None),
            P(("row", "col"), None),
            P(None, "col"),
            P(None, "col"),
            P(None, "col"),
            P(None, "col"),
        ),
        check_vma=False,
    )
```
